32 devices in a mesh: pipe: 2 (over x), ctx: 8 (over z, y), tp: 2 (over core).
Axes of the slice: x: 2, y: 2, z: 4, core: 2. Of those that a mesh axis runs over, the one named last changes fastest.
Arguments:
- qkv_proj: bfloat16 [2, 3, 1024, 8192], P('pipe', None, 'ctx', 'tp'), may hold values from -6 to 6
- cotangent: bfloat16 [2, 1024, 8192], P('pipe', 'ctx', 'tp'), may hold values from -6 to 6
- block_dest: int32 [2, 64], replicated, may hold values from 0 to 63, as said below
- doc_start: int32 [2, 1024], P('pipe', 'ctx'), may hold values 0 or 1
- mr_filter: bfloat16 [2, 512, 128], P('pipe', 'tp'), may hold values from -0.5 to 0.5
Outputs:
- input_grads: bfloat16 [2, 3, 1024, 8192], P('pipe', None, ('ctx', 'tp'))
The draws below stay inside these ranges and needn't reach their ends.
Inputs may be any that keep to these rules, and one draw needn't show every extreme that they name: For each section p, block_dest[p] is a permutation of 0 .. 63. Entry d * 8 + b belongs to block b of ctx index d, and its value lies in b * 8 .. b * 8 + 7: every ctx index sends its block b to the part of the sequence held by ctx index b.
All inputs are finite; a program needn't handle non-finite values. No bound on the sum of `doc_start` on one device may be relied on, other than what follows from the above.
Results may differ from the reference program's by a relative error of at most 0.0049.
Values may be sent and summed in bfloat16 or wider, within the bound.
No kernel may reach another device: no remote copies, remote signals or barrier semaphores. Data moves between devices by JAX's collectives and lax.ppermute only.
A program may use at most 128 MiB of HBM per device.

```python
import jax
import jax.numpy as jnp
from jax import lax

D = 8192
GROUPS = 512
MR_TAPS = 128
ROWS_DEV = 128
SECTIONS = 2
SEQ = 1024
BLOCKS_DEV = 8
NBLK = 64


def permute_slots(sub_key):
    return jax.random.permutation(sub_key, BLOCKS_DEV).astype(jnp.int32)


def draw_block_dest(key, part):
    key_list = jax.random.split(key, SECTIONS * BLOCKS_DEV)
    slot_sets = jax.vmap(permute_slots)(key_list).reshape(SECTIONS, BLOCKS_DEV, BLOCKS_DEV)
    targets = jnp.arange(BLOCKS_DEV, dtype=jnp.int32)
    result = targets[None, None, :] * BLOCKS_DEV + jnp.transpose(slot_sets, (0, 2, 1))
    return result.reshape(SECTIONS, NBLK).astype(jnp.int32)


def plant(values, key, least, high):
    extent = values.shape
    place = [jax.random.randint(jax.random.fold_in(key, axis), (), 0, extent[axis]) for axis in range(len(extent))]
    values = values.at[tuple(place)].set(least)
    longest = extent.index(max(extent))
    place[longest] = (place[longest] + 1) % extent[longest]
    return values.at[tuple(place)].set(high)


def steps_of(key, shape, cuts, least, high):
    level = 1.0
    for dim, shards_of in cuts:
        heights = jax.random.uniform(jax.random.fold_in(jax.random.fold_in(key, 6), dim), (shards_of,), jnp.float32, least / len(cuts), high / len(cuts))
        level = level * jnp.repeat(jnp.exp(heights), shape[dim] // shards_of).reshape((-1,) + (1,) * (len(shape) - 1 - dim))
    return level


def scatter_about(rng, dims, width, bound, shards=(), kind=jnp.bfloat16):
    array = jax.random.normal(rng, dims, jnp.float32) * width
    if len(shards) > 0:
        array = steps_of(rng, dims, shards, -0.22, 0.18) * array
    return jnp.clip(array, min=-bound, max=bound).astype(kind)


def setup_inputs(seed: int = 0) -> dict:
    seeds = jax.random.split(jax.random.key(seed), 6)
    qkv_proj = scatter_about(seeds[0], (SECTIONS, 3, SEQ, D), 1.0, 6.0, ((0, 2), (2, 8), (3, 2)))
    cotangent = scatter_about(seeds[1], (SECTIONS, SEQ, D), 1.0, 6.0, ((0, 2), (1, 8), (2, 2)))
    block_dest = draw_block_dest(jax.random.fold_in(seeds[5], 71), 0)
    doc_start = plant((jax.random.randint(seeds[3], (SECTIONS, SEQ), 0, 200) < 1).astype(jnp.int32), jax.random.fold_in(seeds[3], 1), 0, 1)
    mr_filter = scatter_about(seeds[4], (SECTIONS, GROUPS, MR_TAPS), MR_TAPS ** -0.5, 0.5, ((0, 2), (1, 2)))
    return dict(qkv_proj=qkv_proj, cotangent=cotangent, block_dest=block_dest, doc_start=doc_start, mr_filter=mr_filter)


def medium_conv(source, segment, filt_wide, forward):
    rim_rows = MR_TAPS - 1
    span_rows = ROWS_DEV + rim_rows
    group_size = D // GROUPS
    if forward:
        padded = jnp.concatenate([jnp.zeros((rim_rows, D), source.dtype), source], axis=0)
        seg_pad = jnp.concatenate([jnp.full((rim_rows,), -1, jnp.int32), segment])
        lag_table = jnp.arange(ROWS_DEV, dtype=jnp.int32)[:, None] + rim_rows - jnp.arange(span_rows, dtype=jnp.int32)[None, :]
    else:
        padded = jnp.concatenate([source, jnp.zeros((rim_rows, D), source.dtype)], axis=0)
        seg_pad = jnp.concatenate([segment, jnp.full((rim_rows,), -1, jnp.int32)])
        lag_table = jnp.arange(span_rows, dtype=jnp.int32)[None, :] - jnp.arange(ROWS_DEV, dtype=jnp.int32)[:, None]

    def one_block(first_row):
        window = lax.dynamic_slice_in_dim(padded, first_row, span_rows, 0).astype(jnp.float32)
        window = window.reshape(span_rows, GROUPS, group_size)
        seg_window = lax.dynamic_slice_in_dim(seg_pad, first_row, span_rows, 0)
        seg_target = lax.dynamic_slice_in_dim(segment, first_row, ROWS_DEV, 0)
        valid = (lag_table >= 0) & (lag_table < MR_TAPS) & (seg_window[None, :] == seg_target[:, None])
        picked = jnp.take(filt_wide, jnp.clip(lag_table, 0, MR_TAPS - 1), axis=1)
        toeplitz = jnp.where(valid[None], picked, jnp.float32(0.0))
        return jnp.einsum("gts,sgc->tgc", toeplitz, window, precision=lax.Precision.HIGHEST)

    block_starts = jnp.arange(SEQ // ROWS_DEV, dtype=jnp.int32) * ROWS_DEV
    return lax.map(one_block, block_starts).reshape(SEQ, D)


def one_section(qkv, grad_arrival, dest, marks_arrival, filt):
    count = dest.shape[0]
    block_rows = SEQ // count
    inverse = jnp.zeros((count,), jnp.int32).at[dest].set(jnp.arange(count, dtype=jnp.int32))

    def sequence_order(matrix):
        return jnp.take(matrix.reshape(count, block_rows, -1), inverse, axis=0).reshape(SEQ, -1)

    def arrival_order(matrix):
        return jnp.take(matrix.reshape(count, block_rows, -1), dest, axis=0).reshape(SEQ, -1)

    query = sequence_order(qkv[0])
    key_rows = sequence_order(qkv[1])
    value = sequence_order(qkv[2])
    grad_in = sequence_order(grad_arrival)
    marks = sequence_order(marks_arrival[:, None])[:, 0]
    segment = jnp.cumsum(marks, dtype=jnp.int32)
    mixed = (key_rows.astype(jnp.float32) * value.astype(jnp.float32)).astype(jnp.bfloat16)
    filt_wide = filt.astype(jnp.float32)
    medium = medium_conv(mixed, segment, filt_wide, True)
    gate_grad = (grad_in.astype(jnp.float32) * query.astype(jnp.float32)).astype(jnp.bfloat16)
    mixed_grad = medium_conv(gate_grad, segment, filt_wide, False)
    d_query = (grad_in.astype(jnp.float32) * medium).astype(jnp.bfloat16)
    d_key = (mixed_grad * value.astype(jnp.float32)).astype(jnp.bfloat16)
    d_value = (mixed_grad * key_rows.astype(jnp.float32)).astype(jnp.bfloat16)
    return jnp.stack([arrival_order(d_query), arrival_order(d_key), arrival_order(d_value)])


def reference(qkv_proj, cotangent, block_dest, doc_start, mr_filter):
    results = []
    for section in range(SECTIONS):
        results.append(one_section(qkv_proj[section], cotangent[section], block_dest[section], doc_start[section], mr_filter[section]))
    return jnp.stack([results[(section + 1) % SECTIONS] for section in range(SECTIONS)])
```

```python
import functools

import jax
import jax.numpy as jnp
from jax import lax
from jax.experimental import pallas as pl
from jax.experimental.pallas import tpu as pltpu
from jax.sharding import PartitionSpec as P

LANES = 128
VMEM_BYTES = 48 * 1024 * 1024
F32 = jnp.float32
BF16 = jnp.bfloat16


def params():
    return pltpu.CompilerParams(vmem_limit_bytes=VMEM_BYTES)


def whole_block(*shape):
    return pl.BlockSpec(shape, lambda _: (0,) * len(shape))


def smem():
    return pl.BlockSpec(memory_space=pltpu.SMEM)


def multiply_kernel(marked, proj_ref, grad_ref, *rest):
    marks_ref, out_ref = rest if marked else (None, rest[0])
    peers = out_ref.shape[0]
    rows = grad_ref.shape[1]
    for peer in range(peers):
        lanes = slice(peer * LANES, (peer + 1) * LANES)
        query = proj_ref[0, 0, :, lanes].astype(F32)
        key_rows = proj_ref[0, 1, :, lanes].astype(F32)
        value = proj_ref[0, 2, :, lanes].astype(F32)
        grad_in = grad_ref[0, :, lanes].astype(F32)
        out_ref[peer, :rows, :] = (key_rows * value).astype(BF16)
        out_ref[peer, rows : 2 * rows, :] = (grad_in * query).astype(BF16)
        if marked:
            out_ref[peer, 2 * rows :, :] = marks_ref[...]


def multiply(chunk, peers, qkv_proj, cotangent, marks):
    rows = cotangent.shape[1]
    width = peers * LANES
    marked = marks is not None
    extra = marks.shape[0] if marked else 0
    in_specs = [
        pl.BlockSpec((1, 3, rows, width), lambda _: (0, 0, 0, chunk)),
        pl.BlockSpec((1, rows, width), lambda _: (0, 0, chunk)),
    ]
    args = [qkv_proj, cotangent]
    if marked:
        in_specs.append(whole_block(*marks.shape))
        args.append(marks)
    out = (peers, 2 * rows + extra, LANES)
    return pl.pallas_call(
        functools.partial(multiply_kernel, marked),
        out_shape=jax.ShapeDtypeStruct(out, BF16),
        in_specs=in_specs,
        out_specs=whole_block(*out),
        compiler_params=params(),
        cost_estimate=pl.CostEstimate(
            flops=2 * rows * width, bytes_accessed=12 * rows * width, transcendentals=0
        ),
        grid=(1,),
        name="multiply",
    )(*args)


def slot_of(meta_ref, peers, source, block):
    return meta_ref[source * peers + block] - block * peers


def masks_kernel(meta_ref, marks_ref, out_ref, seq, across):
    peers = marks_ref.shape[0]
    tile = LANES
    block_rows = tile // peers
    row_ids = lax.broadcasted_iota(jnp.int32, (tile, tile), 0)
    lane_ids = lax.broadcasted_iota(jnp.int32, (tile, tile), 1)
    eye = (row_ids == lane_ids).astype(BF16)
    lower = (row_ids >= lane_ids).astype(BF16)
    for source in range(peers):
        spread = lax.dot_general(
            eye, marks_ref[source], (((1,), (1,)), ((), ())), preferred_element_type=F32
        )
        column = jnp.broadcast_to(spread[:, :1], (tile, tile))
        for block in range(peers):
            first = block * tile + slot_of(meta_ref, peers, source, block) * block_rows
            seq[pl.ds(pl.multiple_of(first, block_rows), block_rows), :] = column[
                block * block_rows : (block + 1) * block_rows
            ]
    carry = jnp.zeros((1, tile), F32)
    for b in range(peers):
        rows = slice(b * tile, (b + 1) * tile)
        count = (
            jnp.dot(lower, seq[rows, :].astype(BF16), preferred_element_type=F32) + carry
        )
        carry = count[tile - 1 :, :]
        seq[rows, :] = count
        across[rows, :] = count.T
    for b in range(peers):
        here = seq[b * tile : (b + 1) * tile, :]

        def same(other):
            return (here == across[other * tile : (other + 1) * tile, :]).astype(F32).astype(BF16)

        out_ref[b, 0, :, :tile] = same(max(b - 1, 0))
        out_ref[b, 0, :, tile:] = same(b)
        out_ref[b, 1, :, :tile] = same(b)
        out_ref[b, 1, :, tile:] = same(min(b + 1, peers - 1))


def document_masks(meta, received, mark_rows):
    peers, all_rows, tile = received.shape
    last = all_rows // mark_rows - 1
    out = (peers, 2, tile, 2 * tile)
    return pl.pallas_call(
        masks_kernel,
        out_shape=jax.ShapeDtypeStruct(out, BF16),
        in_specs=[smem(), pl.BlockSpec((peers, mark_rows, tile), lambda _: (0, last, 0))],
        out_specs=whole_block(*out),
        scratch_shapes=[
            pltpu.VMEM((peers * tile, tile), F32),
            pltpu.VMEM((peers * tile, tile), F32),
        ],
        compiler_params=params(),
        cost_estimate=pl.CostEstimate(
            flops=8 * peers * tile * tile, bytes_accessed=8 * peers * tile * tile, transcendentals=0
        ),
        grid=(1,),
        name="masks",
    )(meta, received)


def conv_kernel(group_size, meta_ref, recv_ref, mask_ref, base_ref, out_ref, rows32, rows16, toep):
    peers = recv_ref.shape[0]
    tile = LANES
    groups = base_ref.shape[1]
    block_rows = tile // peers
    rows16[0, :tile, :] = jnp.zeros((tile, tile), BF16)
    rows16[1, peers * tile :, :] = jnp.zeros((tile, tile), BF16)

    def to_sequence(source, carry):
        for half in range(2):
            arrived = recv_ref[source, half * tile : (half + 1) * tile, :].astype(F32)
            for block in range(peers):
                first = block * tile + slot_of(meta_ref, peers, source, block) * block_rows
                rows32[half, pl.ds(pl.multiple_of(first, block_rows), block_rows), :] = arrived[
                    block * block_rows : (block + 1) * block_rows
                ]
        return carry

    lax.fori_loop(0, peers, to_sequence, 0)
    rows16[0, tile:, :] = rows32[0].astype(BF16)
    rows16[1, : peers * tile, :] = rows32[1].astype(BF16)

    for half in range(2):
        for group in range(groups):
            base = jnp.broadcast_to(base_ref[half, group : group + 1, :], (tile, 2 * tile))
            toep[half, group] = pltpu.roll(base, 0, 1, stride=1, stride_axis=0).astype(BF16)

    lane_group = lax.broadcasted_iota(jnp.int32, (tile, tile), 1) // group_size

    def one_tile(b, carry):
        first = pl.multiple_of(b * tile, tile)
        for half in range(2):
            window = rows16[half, pl.ds(first, 2 * tile), :]
            mask = mask_ref[b, half]
            total = jnp.zeros((tile, tile), F32)
            for group in range(groups):
                part = jnp.dot(toep[half, group] * mask, window, preferred_element_type=F32)
                total = jnp.where(lane_group == group, part, total)
            rows32[half, pl.ds(first, tile), :] = total
        return carry

    lax.fori_loop(0, peers, one_tile, 0)

    def to_arrival(source, carry):
        for half in range(2):
            pieces = []
            for block in range(peers):
                first = block * tile + slot_of(meta_ref, peers, source, block) * block_rows
                pieces.append(
                    rows32[half, pl.ds(pl.multiple_of(first, block_rows), block_rows), :]
                )
            out_ref[source, half * tile : (half + 1) * tile, :] = jnp.concatenate(
                pieces, axis=0
            ).astype(BF16)
        return carry

    lax.fori_loop(0, peers, to_arrival, 0)


def convolve(group_size, meta, received, masks, bases):
    peers, all_rows, tile = received.shape
    groups = bases.shape[1]
    out = (peers, 2 * tile, tile)
    return pl.pallas_call(
        functools.partial(conv_kernel, group_size),
        out_shape=jax.ShapeDtypeStruct(out, BF16),
        in_specs=[
            smem(),
            whole_block(*received.shape),
            whole_block(*masks.shape),
            whole_block(*bases.shape),
        ],
        out_specs=whole_block(*out),
        scratch_shapes=[
            pltpu.VMEM((2, peers * tile, tile), F32),
            pltpu.VMEM((2, (peers + 1) * tile, tile), BF16),
            pltpu.VMEM((2, groups, tile, 2 * tile), BF16),
        ],
        compiler_params=params(),
        cost_estimate=pl.CostEstimate(
            flops=8 * groups * peers * tile**3, bytes_accessed=16 * peers * tile**2, transcendentals=0
        ),
        grid=(1,),
        name="convolve",
    )(meta, received, masks, bases)


def gradients_kernel(tp_at, meta_ref, back_ref, key_ref, value_ref, grad_ref, keep_ref, cross_ref):
    peers = back_ref.shape[0]
    rows = grad_ref.shape[1]
    part = keep_ref.shape[1]
    mine = meta_ref[tp_at]
    for out_ref, index in ((keep_ref, mine), (cross_ref, 1 - mine)):
        first = pl.multiple_of(index * part, part)
        at = pl.ds(first, part)
        later = pl.ds(pl.multiple_of(first + rows, part), part)
        for peer in range(peers):
            lanes = slice(peer * LANES, (peer + 1) * LANES)
            medium = back_ref[peer, at, :].astype(F32)
            mixed_grad = back_ref[peer, later, :].astype(F32)
            grad_in = grad_ref[0, at, lanes].astype(F32)
            key_rows = key_ref[0, 0, at, lanes].astype(F32)
            value = value_ref[0, 0, at, lanes].astype(F32)
            out_ref[0, :, lanes] = (grad_in * medium).astype(BF16)
            out_ref[1, :, lanes] = (mixed_grad * value).astype(BF16)
            out_ref[2, :, lanes] = (mixed_grad * key_rows).astype(BF16)


def gradients(chunk, tp_at, tp_count, meta, back, qkv_proj, cotangent):
    peers, two_rows, _ = back.shape
    rows = two_rows // 2
    width = peers * LANES
    out = (3, rows // tp_count, width)
    return pl.pallas_call(
        functools.partial(gradients_kernel, tp_at),
        out_shape=[jax.ShapeDtypeStruct(out, BF16)] * 2,
        in_specs=[
            smem(),
            whole_block(*back.shape),
            pl.BlockSpec((1, 1, rows, width), lambda _: (0, 1, 0, chunk)),
            pl.BlockSpec((1, 1, rows, width), lambda _: (0, 2, 0, chunk)),
            pl.BlockSpec((1, rows, width), lambda _: (0, 0, chunk)),
        ],
        out_specs=[whole_block(*out)] * 2,
        compiler_params=params(),
        cost_estimate=pl.CostEstimate(
            flops=3 * rows * width, bytes_accessed=16 * rows * width, transcendentals=0
        ),
        grid=(1,),
        name="gradients",
    )(meta, back, qkv_proj, qkv_proj, cotangent)


def assemble_kernel(tp_at, chunks, half_width, meta_ref, *refs):
    pieces = refs[: 2 * chunks]
    out_ref = refs[2 * chunks]
    sems = refs[2 * chunks + 1]
    mine = meta_ref[tp_at]
    copies = []
    for chunk in range(chunks):
        width = pieces[2 * chunk].shape[2]
        for side, index in ((0, mine), (1, 1 - mine)):
            first = pl.multiple_of(index * half_width + chunk * width, LANES)
            copies.append(
                pltpu.make_async_copy(
                    pieces[2 * chunk + side],
                    out_ref.at[0, :, :, pl.ds(first, width)],
                    sems.at[2 * chunk + side],
                )
            )
    for copy in copies:
        copy.start()
    for copy in copies:
        copy.wait()


def assemble(tp_at, channels, tp_count, meta, pieces):
    three, part, _ = pieces[0].shape
    return pl.pallas_call(
        functools.partial(assemble_kernel, tp_at, len(pieces) // 2, channels),
        out_shape=jax.ShapeDtypeStruct((1, three, part, tp_count * channels), BF16),
        in_specs=[smem()] + [pl.BlockSpec(memory_space=pl.ANY)] * len(pieces),
        out_specs=pl.BlockSpec(memory_space=pl.ANY),
        scratch_shapes=[pltpu.SemaphoreType.DMA((len(pieces),))],
        compiler_params=params(),
        name="assemble",
    )(meta, *pieces)


def shards(qkv_proj, cotangent, block_dest, doc_start, mr_filter):
    peers = lax.axis_size("ctx")
    pipes = lax.axis_size("pipe")
    tp_count = lax.axis_size("tp")
    channels = cotangent.shape[2]
    group_count, taps = mr_filter.shape[1:]
    group_size = channels // group_count
    chunks = channels // (peers * LANES)
    chunk_groups = LANES // group_size

    dest = lax.dynamic_index_in_dim(block_dest, lax.axis_index("pipe"), 0, keepdims=False)
    tp_at = dest.shape[0]
    meta = jnp.concatenate([dest, lax.axis_index("tp").astype(jnp.int32)[None]])
    marks = jnp.broadcast_to(doc_start.astype(BF16), (16, doc_start.shape[1]))

    filt = lax.dynamic_index_in_dim(
        mr_filter[0].astype(F32).reshape(chunks, peers, chunk_groups, taps),
        lax.axis_index("ctx"),
        1,
        keepdims=False,
    )
    causal = jnp.pad(filt[:, :, ::-1], ((0, 0), (0, 0), (1, taps - 1)))
    anti = jnp.pad(filt, ((0, 0), (0, 0), (0, taps)))
    bases = jnp.stack([causal, anti], axis=1)

    sent = []
    for chunk in range(chunks):
        sent.append(
            multiply(chunk, peers, qkv_proj, cotangent, marks if chunk == 0 else None)
        )
    received = [lax.all_to_all(s, "ctx", split_axis=0, concat_axis=0, tiled=True) for s in sent]
    masks = document_masks(meta, received[0], marks.shape[0])
    backs = []
    for chunk in range(chunks):
        convolved = convolve(group_size, meta, received[chunk], masks, bases[chunk])
        backs.append(lax.all_to_all(convolved, "ctx", split_axis=0, concat_axis=0, tiled=True))

    straight, crossed = [], []
    for pipe in range(pipes):
        for tp in range(tp_count):
            target = (pipe - 1) % pipes
            straight.append((pipe * tp_count + tp, target * tp_count + tp))
            crossed.append((pipe * tp_count + tp, target * tp_count + (1 - tp)))
    pieces = []
    for chunk in range(chunks):
        keep, cross = gradients(chunk, tp_at, tp_count, meta, backs[chunk], qkv_proj, cotangent)
        pieces.append(lax.ppermute(keep, ("pipe", "tp"), straight))
        pieces.append(lax.ppermute(cross, ("pipe", "tp"), crossed))
    return assemble(tp_at, channels, tp_count, meta, pieces)


def solution(mesh):
    placed = (
        P("pipe", None, "ctx", "tp"),
        P("pipe", "ctx", "tp"),
        P(),
        P("pipe", "ctx"),
        P("pipe", "tp", None),
    )
    return jax.shard_map(
        shards,
        mesh=mesh,
        in_specs=placed,
        out_specs=P("pipe", None, ("ctx", "tp"), None),
        check_vma=False,
    )
```

```python
import functools
import math

import jax
import jax.numpy as jnp
from jax import lax
from jax.experimental import pallas as pl
from jax.experimental.pallas import tpu as pltpu
from jax.sharding import PartitionSpec as P

LANES = 128
CHUNKS = 2
VMEM_BYTES = 60 * 1024 * 1024
F32 = jnp.float32
BF16 = jnp.bfloat16


def params():
    return pltpu.CompilerParams(vmem_limit_bytes=VMEM_BYTES)


def whole_block(*shape):
    return pl.BlockSpec(shape, lambda _: (0,) * len(shape))


def smem():
    return pl.BlockSpec(memory_space=pltpu.SMEM)


def multiply_kernel(marked, me_at, meta_ref, proj_ref, grad_ref, *rest):
    marks_ref, outs = (rest[0], rest[1:]) if marked else (None, rest)
    rows = grad_ref.shape[1]
    width = outs[0].shape[1]
    me = meta_ref[me_at]
    for k in reversed(range(len(outs))):
        out_ref = outs[k]
        lanes = pl.ds(pl.multiple_of((me ^ k) * width, LANES), width)
        query = proj_ref[0, 0, :, lanes].astype(F32)
        key_rows = proj_ref[0, 1, :, lanes].astype(F32)
        value = proj_ref[0, 2, :, lanes].astype(F32)
        grad_in = grad_ref[0, :, lanes].astype(F32)
        out_ref[:rows, :] = (key_rows * value).astype(BF16)
        out_ref[rows : 2 * rows, :] = (grad_in * query).astype(BF16)
        if marked:
            out_ref[2 * rows :, :LANES] = marks_ref[...]
            if width > LANES:
                out_ref[2 * rows :, LANES:] = jnp.zeros(
                    (marks_ref.shape[0], width - LANES), BF16
                )


def multiply(index, width, peers, me_at, meta, qkv_proj, cotangent, marks):
    rows = cotangent.shape[1]
    span = peers * width
    marked = marks is not None
    extra = marks.shape[0] if marked else 0
    in_specs = [
        smem(),
        pl.BlockSpec((1, 3, rows, span), lambda _: (0, 0, 0, index)),
        pl.BlockSpec((1, rows, span), lambda _: (0, 0, index)),
    ]
    args = [meta, qkv_proj, cotangent]
    if marked:
        in_specs.append(whole_block(*marks.shape))
        args.append(marks)
    out = (2 * rows + extra, width)
    return pl.pallas_call(
        functools.partial(multiply_kernel, marked, me_at),
        out_shape=[jax.ShapeDtypeStruct(out, BF16)] * peers,
        in_specs=in_specs,
        out_specs=[whole_block(*out)] * peers,
        compiler_params=params(),
        cost_estimate=pl.CostEstimate(
            flops=2 * rows * span, bytes_accessed=12 * rows * span, transcendentals=0
        ),
        grid=(1,),
        name="multiply",
    )(*args)


def first_row(meta_ref, peers, source, block):
    block_rows = LANES // peers
    row = meta_ref[source * peers + block] * block_rows
    return pl.multiple_of(row, block_rows)


def masks_kernel(me_at, meta_ref, *refs):
    marks_refs, (out_ref, seq, across) = refs[:-3], refs[-3:]
    peers = len(marks_refs)
    tile = LANES
    block_rows = tile // peers
    me = meta_ref[me_at]
    row_ids = lax.broadcasted_iota(jnp.int32, (tile, tile), 0)
    lane_ids = lax.broadcasted_iota(jnp.int32, (tile, tile), 1)
    eye = (row_ids == lane_ids).astype(BF16)
    lower = (row_ids >= lane_ids).astype(BF16)
    for k in range(peers):
        spread = lax.dot_general(
            eye, marks_refs[k][...], (((1,), (1,)), ((), ())), preferred_element_type=F32
        )
        column = jnp.broadcast_to(spread[:, :1], (tile, tile))
        for block in range(peers):
            first = first_row(meta_ref, peers, me ^ k, block)
            seq[pl.ds(first, block_rows), :] = column[
                block * block_rows : (block + 1) * block_rows
            ]
    carry = jnp.zeros((1, tile), F32)
    for b in range(peers):
        rows = slice(b * tile, (b + 1) * tile)
        count = (
            jnp.dot(lower, seq[rows, :].astype(BF16), preferred_element_type=F32) + carry
        )
        carry = count[tile - 1 :, :]
        seq[rows, :] = count
        across[rows, :] = count.T
    for b in range(peers):
        here = seq[b * tile : (b + 1) * tile, :]

        def same(other):
            return (here == across[other * tile : (other + 1) * tile, :]).astype(F32).astype(BF16)

        out_ref[b, 0, :, :tile] = same(max(b - 1, 0))
        out_ref[b, 0, :, tile:] = same(b)
        out_ref[b, 1, :, :tile] = same(b)
        out_ref[b, 1, :, tile:] = same(min(b + 1, peers - 1))


def document_masks(me_at, meta, received, mark_rows):
    peers = len(received)
    tile = LANES
    last = received[0].shape[0] // mark_rows - 1
    out = (peers, 2, tile, 2 * tile)
    return pl.pallas_call(
        functools.partial(masks_kernel, me_at),
        out_shape=jax.ShapeDtypeStruct(out, BF16),
        in_specs=[smem()] + [pl.BlockSpec((mark_rows, tile), lambda _: (last, 0))] * peers,
        out_specs=whole_block(*out),
        scratch_shapes=[
            pltpu.VMEM((peers * tile, tile), F32),
            pltpu.VMEM((peers * tile, tile), F32),
        ],
        compiler_params=params(),
        cost_estimate=pl.CostEstimate(
            flops=8 * peers * tile * tile, bytes_accessed=8 * peers * tile * tile, transcendentals=0
        ),
        grid=(1,),
        name="masks",
    )(meta, *received)


def conv_kernel(group_size, me_at, meta_ref, mask_ref, base_ref, *refs):
    rows32, rows16, toep = refs[-3:]
    peers = (len(refs) - 3) // 2
    recv, outs = refs[:peers], refs[peers : 2 * peers]
    tile = LANES
    width = outs[0].shape[1]
    groups = base_ref.shape[1]
    block_rows = tile // peers
    me = meta_ref[me_at]
    rows16[0, :tile, :] = jnp.zeros((tile, width), BF16)
    rows16[1, peers * tile :, :] = jnp.zeros((tile, width), BF16)

    for half in range(2):
        for group in range(groups):
            base = jnp.broadcast_to(base_ref[half, group : group + 1, :], (tile, 2 * tile))
            toep[half, group] = pltpu.roll(base, 0, 1, stride=1, stride_axis=0).astype(BF16)

    for k in range(peers):
        firsts = [first_row(meta_ref, peers, me ^ k, block) for block in range(peers)]
        for half in range(2):
            arrived = recv[k][half * tile : (half + 1) * tile, :].astype(F32)
            for block in range(peers):
                rows32[half, pl.ds(firsts[block], block_rows), :] = arrived[
                    block * block_rows : (block + 1) * block_rows
                ]
    rows16[0, tile:, :] = rows32[0].astype(BF16)
    rows16[1, : peers * tile, :] = rows32[1].astype(BF16)

    tile_groups = tile // group_size
    lane_group = lax.broadcasted_iota(jnp.int32, (tile, tile), 1) // group_size

    def one_tile(b, carry):
        first = pl.multiple_of(b * tile, tile)
        for half in range(2):
            mask = mask_ref[b, half]
            for sub in range(width // tile):
                lanes = slice(sub * tile, (sub + 1) * tile)
                window = rows16[half, pl.ds(first, 2 * tile), lanes]
                total = jnp.zeros((tile, tile), F32)
                for group in range(tile_groups):
                    part = jnp.dot(
                        toep[half, sub * tile_groups + group] * mask,
                        window,
                        preferred_element_type=F32,
                    )
                    total = jnp.where(lane_group == group, part, total)
                rows32[half, pl.ds(first, tile), lanes] = total
        return carry

    lax.fori_loop(0, peers, one_tile, 0)

    for k in range(peers):
        firsts = [first_row(meta_ref, peers, me ^ k, block) for block in range(peers)]
        for half in range(2):
            pieces = [rows32[half, pl.ds(first, block_rows), :] for first in firsts]
            outs[k][half * tile : (half + 1) * tile, :] = jnp.concatenate(pieces, axis=0).astype(
                BF16
            )


def convolve(group_size, me_at, meta, received, masks, bases):
    peers = len(received)
    tile = LANES
    width = received[0].shape[1]
    groups = bases.shape[1]
    out = (2 * tile, width)
    return pl.pallas_call(
        functools.partial(conv_kernel, group_size, me_at),
        out_shape=[jax.ShapeDtypeStruct(out, BF16)] * peers,
        in_specs=[smem(), whole_block(*masks.shape), whole_block(*bases.shape)]
        + [whole_block(*received[0].shape)] * peers,
        out_specs=[whole_block(*out)] * peers,
        scratch_shapes=[
            pltpu.VMEM((2, peers * tile, width), F32),
            pltpu.VMEM((2, (peers + 1) * tile, width), BF16),
            pltpu.VMEM((2, groups, tile, 2 * tile), BF16),
        ],
        compiler_params=params(),
        cost_estimate=pl.CostEstimate(
            flops=8 * groups * peers * tile**3,
            bytes_accessed=8 * peers * tile * width + 4 * peers * tile**2,
            transcendentals=0,
        ),
        grid=(1,),
        name="convolve",
    )(meta, masks, bases, *received)


def gradients_kernel(me_at, tp_at, meta_ref, key_ref, value_ref, grad_ref, *refs):
    backs, (keep_ref, cross_ref) = refs[:-2], refs[-2:]
    rows = grad_ref.shape[1]
    width = backs[0].shape[1]
    part = keep_ref.shape[1]
    me = meta_ref[me_at]
    mine = meta_ref[tp_at]
    for out_ref, index in ((keep_ref, mine), (cross_ref, 1 - mine)):
        first = pl.multiple_of(index * part, part)
        at = pl.ds(first, part)
        later = pl.ds(pl.multiple_of(first + rows, part), part)
        for k, back_ref in enumerate(backs):
            lanes = pl.ds(pl.multiple_of((me ^ k) * width, LANES), width)
            medium = back_ref[at, :].astype(F32)
            mixed_grad = back_ref[later, :].astype(F32)
            grad_in = grad_ref[0, at, lanes].astype(F32)
            key_rows = key_ref[0, 0, at, lanes].astype(F32)
            value = value_ref[0, 0, at, lanes].astype(F32)
            out_ref[0, :, lanes] = (grad_in * medium).astype(BF16)
            out_ref[1, :, lanes] = (mixed_grad * value).astype(BF16)
            out_ref[2, :, lanes] = (mixed_grad * key_rows).astype(BF16)


def gradients(index, me_at, tp_at, tp_count, meta, backs, qkv_proj, cotangent):
    peers = len(backs)
    rows = cotangent.shape[1]
    span = peers * backs[0].shape[1]
    out = (3, rows // tp_count, span)
    return pl.pallas_call(
        functools.partial(gradients_kernel, me_at, tp_at),
        out_shape=[jax.ShapeDtypeStruct(out, BF16)] * 2,
        in_specs=[
            smem(),
            pl.BlockSpec((1, 1, rows, span), lambda _: (0, 1, 0, index)),
            pl.BlockSpec((1, 1, rows, span), lambda _: (0, 2, 0, index)),
            pl.BlockSpec((1, rows, span), lambda _: (0, 0, index)),
        ]
        + [whole_block(*backs[0].shape)] * peers,
        out_specs=[whole_block(*out)] * 2,
        compiler_params=params(),
        cost_estimate=pl.CostEstimate(
            flops=3 * rows * span, bytes_accessed=16 * rows * span, transcendentals=0
        ),
        grid=(1,),
        name="gradients",
    )(meta, qkv_proj, qkv_proj, cotangent, *backs)


def assemble_kernel(tp_at, half_width, meta_ref, *refs):
    pieces, out_ref = refs[:-1], refs[-1]
    mine = meta_ref[tp_at]
    done = 0
    for keep, cross in zip(pieces[::2], pieces[1::2]):
        width = keep.shape[2]
        for piece, index in ((keep, mine), (cross, 1 - mine)):
            first = pl.multiple_of(index * half_width + done, LANES)
            out_ref[0, 0, :, pl.ds(first, width)] = piece[0]
        done += width


def assemble(tp_at, channels, tp_count, meta, pieces):
    three, part, _ = pieces[0].shape
    out = (1, three, part, tp_count * channels)
    return pl.pallas_call(
        functools.partial(assemble_kernel, tp_at, channels),
        out_shape=jax.ShapeDtypeStruct(out, BF16),
        grid=(three,),
        in_specs=[smem()] + [pl.BlockSpec((1,) + p.shape[1:], lambda i: (i, 0, 0)) for p in pieces],
        out_specs=pl.BlockSpec((1, 1) + out[2:], lambda i: (0, i, 0, 0)),
        compiler_params=params(),
        cost_estimate=pl.CostEstimate(
            flops=0, bytes_accessed=4 * three * part * tp_count * channels, transcendentals=0
        ),
        name="assemble",
    )(meta, *pieces)


def exchanged(arrays):
    peers = len(arrays)
    return [
        lax.ppermute(array, "ctx", [(i, i ^ k) for i in range(peers)]) if k else array
        for k, array in reversed(list(enumerate(arrays)))
    ][::-1]


def shards(qkv_proj, cotangent, block_dest, doc_start, mr_filter):
    peers = lax.axis_size("ctx")
    pipes = lax.axis_size("pipe")
    tp_count = lax.axis_size("tp")
    channels = cotangent.shape[2]
    group_count, taps = mr_filter.shape[1:]
    group_size = channels // group_count
    units = channels // (peers * LANES)
    chunks = math.gcd(units, CHUNKS)
    width = channels // (peers * chunks)
    chunk_groups = width // group_size

    dest = lax.dynamic_index_in_dim(block_dest, lax.axis_index("pipe"), 0, keepdims=False)
    me_at = dest.shape[0]
    tp_at = me_at + 1
    here = [lax.axis_index("ctx"), lax.axis_index("tp")]
    meta = jnp.concatenate([dest, jnp.stack(here).astype(jnp.int32)])
    marks = jnp.broadcast_to(doc_start.astype(BF16), (16, doc_start.shape[1]))

    filt = lax.dynamic_index_in_dim(
        mr_filter[0].astype(F32).reshape(chunks, peers, chunk_groups, taps),
        lax.axis_index("ctx"),
        1,
        keepdims=False,
    )
    causal = jnp.pad(filt[:, :, ::-1], ((0, 0), (0, 0), (1, taps - 1)))
    anti = jnp.pad(filt, ((0, 0), (0, 0), (0, taps)))
    bases = jnp.stack([causal, anti], axis=1)

    received = []
    for chunk in range(chunks):
        products = multiply(
            chunk, width, peers, me_at, meta, qkv_proj, cotangent, marks if chunk == 0 else None
        )
        received.append(exchanged(products))
    masks = document_masks(me_at, meta, received[0], marks.shape[0])
    backs = []
    for chunk in range(chunks):
        convolved = convolve(group_size, me_at, meta, received[chunk], masks, bases[chunk])
        backs.append(exchanged(convolved))

    straight, crossed = [], []
    for pipe in range(pipes):
        for tp in range(tp_count):
            target = (pipe - 1) % pipes
            straight.append((pipe * tp_count + tp, target * tp_count + tp))
            crossed.append((pipe * tp_count + tp, target * tp_count + (1 - tp)))
    pieces = []
    for chunk in range(chunks):
        keep, cross = gradients(
            chunk, me_at, tp_at, tp_count, meta, backs[chunk], qkv_proj, cotangent
        )
        pieces.append(lax.ppermute(keep, ("pipe", "tp"), straight))
        pieces.append(lax.ppermute(cross, ("pipe", "tp"), crossed))
    return assemble(tp_at, channels, tp_count, meta, pieces)


def solution(mesh):
    placed = (
        P("pipe", None, "ctx", "tp"),
        P("pipe", "ctx", "tp"),
        P(),
        P("pipe", "ctx"),
        P("pipe", "tp", None),
    )
    return jax.shard_map(
        shards,
        mesh=mesh,
        in_specs=placed,
        out_specs=P("pipe", None, ("ctx", "tp"), None),
        check_vma=False,
    )
```

```python
import functools
import math

import jax
import jax.numpy as jnp
from jax import lax
from jax.experimental import pallas as pl
from jax.experimental.pallas import tpu as pltpu
from jax.sharding import PartitionSpec as P

LANES = 128
CHUNKS = 2
VMEM_BYTES = 60 * 1024 * 1024
F32 = jnp.float32
BF16 = jnp.bfloat16


def params():
    return pltpu.CompilerParams(vmem_limit_bytes=VMEM_BYTES)


def whole_block(*shape):
    return pl.BlockSpec(shape, lambda _: (0,) * len(shape))


def smem():
    return pl.BlockSpec(memory_space=pltpu.SMEM)


def multiply_kernel(marked, me_at, meta_ref, proj_ref, grad_ref, *rest):
    marks_ref, outs = (rest[0], rest[1:]) if marked else (None, rest)
    rows = grad_ref.shape[1]
    width = outs[0].shape[1]
    me = meta_ref[me_at]
    for k in reversed(range(len(outs))):
        out_ref = outs[k]
        lanes = pl.ds(pl.multiple_of((me ^ k) * width, LANES), width)
        query = proj_ref[0, 0, :, lanes].astype(F32)
        key_rows = proj_ref[0, 1, :, lanes].astype(F32)
        value = proj_ref[0, 2, :, lanes].astype(F32)
        grad_in = grad_ref[0, :, lanes].astype(F32)
        out_ref[:rows, :] = (key_rows * value).astype(BF16)
        out_ref[rows : 2 * rows, :] = (grad_in * query).astype(BF16)
        if marked:
            out_ref[2 * rows :, :LANES] = marks_ref[...]
            if width > LANES:
                out_ref[2 * rows :, LANES:] = jnp.zeros(
                    (marks_ref.shape[0], width - LANES), BF16
                )


def multiply(index, width, peers, me_at, meta, qkv_proj, cotangent, marks):
    rows = cotangent.shape[1]
    span = peers * width
    marked = marks is not None
    extra = marks.shape[0] if marked else 0
    in_specs = [
        smem(),
        pl.BlockSpec((1, 3, rows, span), lambda _: (0, 0, 0, index)),
        pl.BlockSpec((1, rows, span), lambda _: (0, 0, index)),
    ]
    args = [meta, qkv_proj, cotangent]
    if marked:
        in_specs.append(whole_block(*marks.shape))
        args.append(marks)
    out = (2 * rows + extra, width)
    return pl.pallas_call(
        functools.partial(multiply_kernel, marked, me_at),
        out_shape=[jax.ShapeDtypeStruct(out, BF16)] * peers,
        in_specs=in_specs,
        out_specs=[whole_block(*out)] * peers,
        compiler_params=params(),
        cost_estimate=pl.CostEstimate(
            flops=2 * rows * span, bytes_accessed=12 * rows * span, transcendentals=0
        ),
        grid=(1,),
        name="multiply",
    )(*args)


def first_row(meta_ref, peers, source, block):
    block_rows = LANES // peers
    row = meta_ref[source * peers + block] * block_rows
    return pl.multiple_of(row, block_rows)


def masks_kernel(me_at, meta_ref, *refs):
    marks_refs, (out_ref, seq, across) = refs[:-3], refs[-3:]
    peers = len(marks_refs)
    tile = LANES
    block_rows = tile // peers
    me = meta_ref[me_at]
    row_ids = lax.broadcasted_iota(jnp.int32, (tile, tile), 0)
    lane_ids = lax.broadcasted_iota(jnp.int32, (tile, tile), 1)
    eye = (row_ids == lane_ids).astype(BF16)
    lower = (row_ids >= lane_ids).astype(BF16)
    for k in range(peers):
        spread = lax.dot_general(
            eye, marks_refs[k][...], (((1,), (1,)), ((), ())), preferred_element_type=F32
        )
        column = jnp.broadcast_to(spread[:, :1], (tile, tile))
        for block in range(peers):
            first = first_row(meta_ref, peers, me ^ k, block)
            seq[pl.ds(first, block_rows), :] = column[
                block * block_rows : (block + 1) * block_rows
            ]
    carry = jnp.zeros((1, tile), F32)
    for b in range(peers):
        rows = slice(b * tile, (b + 1) * tile)
        count = (
            jnp.dot(lower, seq[rows, :].astype(BF16), preferred_element_type=F32) + carry
        )
        carry = count[tile - 1 :, :]
        seq[rows, :] = count
        across[rows, :] = count.T
    for b in range(peers):
        here = seq[b * tile : (b + 1) * tile, :]

        def same(other):
            return (here == across[other * tile : (other + 1) * tile, :]).astype(F32).astype(BF16)

        out_ref[b, 0, :, :tile] = same(max(b - 1, 0))
        out_ref[b, 0, :, tile:] = same(b)
        out_ref[b, 1, :, :tile] = same(b)
        out_ref[b, 1, :, tile:] = same(min(b + 1, peers - 1))


def document_masks(me_at, meta, received, mark_rows):
    peers = len(received)
    tile = LANES
    last = received[0].shape[0] // mark_rows - 1
    out = (peers, 2, tile, 2 * tile)
    return pl.pallas_call(
        functools.partial(masks_kernel, me_at),
        out_shape=jax.ShapeDtypeStruct(out, BF16),
        in_specs=[smem()] + [pl.BlockSpec((mark_rows, tile), lambda _: (last, 0))] * peers,
        out_specs=whole_block(*out),
        scratch_shapes=[
            pltpu.VMEM((peers * tile, tile), F32),
            pltpu.VMEM((peers * tile, tile), F32),
        ],
        compiler_params=params(),
        cost_estimate=pl.CostEstimate(
            flops=8 * peers * tile * tile, bytes_accessed=8 * peers * tile * tile, transcendentals=0
        ),
        grid=(1,),
        name="masks",
    )(meta, *received)


def conv_kernel(group_size, me_at, meta_ref, mask_ref, base_ref, *refs):
    rows32, rows16, toep = refs[-3:]
    peers = (len(refs) - 3) // 2
    recv, outs = refs[:peers], refs[peers : 2 * peers]
    tile = LANES
    width = outs[0].shape[1]
    groups = base_ref.shape[1]
    block_rows = tile // peers
    me = meta_ref[me_at]
    rows16[0, :tile, :] = jnp.zeros((tile, width), BF16)
    rows16[1, peers * tile :, :] = jnp.zeros((tile, width), BF16)

    for half in range(2):
        for group in range(groups):
            base = jnp.broadcast_to(base_ref[half, group : group + 1, :], (tile, 2 * tile))
            toep[half, group] = pltpu.roll(base, 0, 1, stride=1, stride_axis=0).astype(BF16)

    for k in range(peers):
        firsts = [first_row(meta_ref, peers, me ^ k, block) for block in range(peers)]
        for half in range(2):
            arrived = recv[k][half * tile : (half + 1) * tile, :].astype(F32)
            for block in range(peers):
                rows32[half, pl.ds(firsts[block], block_rows), :] = arrived[
                    block * block_rows : (block + 1) * block_rows
                ]
    rows16[0, tile:, :] = rows32[0].astype(BF16)
    rows16[1, : peers * tile, :] = rows32[1].astype(BF16)

    tile_groups = tile // group_size
    lane_group = lax.broadcasted_iota(jnp.int32, (tile, tile), 1) // group_size

    def one_tile(b, carry):
        first = pl.multiple_of(b * tile, tile)
        for half in range(2):
            mask = mask_ref[b, half]
            for sub in range(width // tile):
                lanes = slice(sub * tile, (sub + 1) * tile)
                window = rows16[half, pl.ds(first, 2 * tile), lanes]
                total = jnp.zeros((tile, tile), F32)
                for group in range(tile_groups):
                    part = jnp.dot(
                        toep[half, sub * tile_groups + group] * mask,
                        window,
                        preferred_element_type=F32,
                    )
                    total = jnp.where(lane_group == group, part, total)
                rows32[half, pl.ds(first, tile), lanes] = total
        return carry

    lax.fori_loop(0, peers, one_tile, 0)

    for k in range(peers):
        firsts = [first_row(meta_ref, peers, me ^ k, block) for block in range(peers)]
        for half in range(2):
            pieces = [rows32[half, pl.ds(first, block_rows), :] for first in firsts]
            outs[k][half * tile : (half + 1) * tile, :] = jnp.concatenate(pieces, axis=0).astype(
                BF16
            )


def convolve(group_size, me_at, meta, received, masks, bases):
    peers = len(received)
    tile = LANES
    width = received[0].shape[1]
    groups = bases.shape[1]
    out = (2 * tile, width)
    return pl.pallas_call(
        functools.partial(conv_kernel, group_size, me_at),
        out_shape=[jax.ShapeDtypeStruct(out, BF16)] * peers,
        in_specs=[smem(), whole_block(*masks.shape), whole_block(*bases.shape)]
        + [whole_block(*received[0].shape)] * peers,
        out_specs=[whole_block(*out)] * peers,
        scratch_shapes=[
            pltpu.VMEM((2, peers * tile, width), F32),
            pltpu.VMEM((2, (peers + 1) * tile, width), BF16),
            pltpu.VMEM((2, groups, tile, 2 * tile), BF16),
        ],
        compiler_params=params(),
        cost_estimate=pl.CostEstimate(
            flops=8 * groups * peers * tile**3,
            bytes_accessed=8 * peers * tile * width + 4 * peers * tile**2,
            transcendentals=0,
        ),
        grid=(1,),
        name="convolve",
    )(meta, masks, bases, *received)


def gradients_kernel(me_at, tp_at, meta_ref, key_ref, value_ref, grad_ref, *refs):
    backs, (keep_ref, cross_ref) = refs[:-2], refs[-2:]
    rows = grad_ref.shape[1]
    width = backs[0].shape[1]
    part = keep_ref.shape[1]
    me = meta_ref[me_at]
    mine = meta_ref[tp_at]
    for out_ref, index in ((keep_ref, mine), (cross_ref, 1 - mine)):
        first = pl.multiple_of(index * part, part)
        at = pl.ds(first, part)
        later = pl.ds(pl.multiple_of(first + rows, part), part)
        for k, back_ref in enumerate(backs):
            lanes = pl.ds(pl.multiple_of((me ^ k) * width, LANES), width)
            medium = back_ref[at, :].astype(F32)
            mixed_grad = back_ref[later, :].astype(F32)
            grad_in = grad_ref[0, at, lanes].astype(F32)
            key_rows = key_ref[0, 0, at, lanes].astype(F32)
            value = value_ref[0, 0, at, lanes].astype(F32)
            out_ref[0, :, lanes] = (grad_in * medium).astype(BF16)
            out_ref[1, :, lanes] = (mixed_grad * value).astype(BF16)
            out_ref[2, :, lanes] = (mixed_grad * key_rows).astype(BF16)


def gradients(index, me_at, tp_at, tp_count, meta, backs, key_value, grad_in):
    peers = len(backs)
    rows = grad_in.shape[1]
    span = peers * backs[0].shape[1]
    out = (3, rows // tp_count, span)
    return pl.pallas_call(
        functools.partial(gradients_kernel, me_at, tp_at),
        out_shape=[jax.ShapeDtypeStruct(out, BF16)] * 2,
        in_specs=[
            smem(),
            pl.BlockSpec((1, 1, rows, span), lambda _: (0, 0, 0, index)),
            pl.BlockSpec((1, 1, rows, span), lambda _: (0, 1, 0, index)),
            pl.BlockSpec((1, rows, span), lambda _: (0, 0, index)),
        ]
        + [whole_block(*backs[0].shape)] * peers,
        out_specs=[whole_block(*out)] * 2,
        compiler_params=params(),
        cost_estimate=pl.CostEstimate(
            flops=3 * rows * span, bytes_accessed=16 * rows * span, transcendentals=0
        ),
        grid=(1,),
        name="gradients",
    )(meta, key_value, key_value, grad_in, *backs)


def assemble_kernel(tp_at, half_width, meta_ref, *refs):
    pieces, out_ref = refs[:-1], refs[-1]
    mine = meta_ref[tp_at]
    done = 0
    for keep, cross in zip(pieces[::2], pieces[1::2]):
        width = keep.shape[2]
        for piece, index in ((keep, mine), (cross, 1 - mine)):
            first = pl.multiple_of(index * half_width + done, LANES)
            out_ref[0, 0, :, pl.ds(first, width)] = piece[0]
        done += width


def assemble(tp_at, channels, tp_count, meta, pieces):
    three, part, _ = pieces[0].shape
    out = (1, three, part, tp_count * channels)
    return pl.pallas_call(
        functools.partial(assemble_kernel, tp_at, channels),
        out_shape=jax.ShapeDtypeStruct(out, BF16),
        grid=(three,),
        in_specs=[smem()] + [pl.BlockSpec((1,) + p.shape[1:], lambda i: (i, 0, 0)) for p in pieces],
        out_specs=pl.BlockSpec((1, 1) + out[2:], lambda i: (0, i, 0, 0)),
        compiler_params=params(),
        cost_estimate=pl.CostEstimate(
            flops=0, bytes_accessed=4 * three * part * tp_count * channels, transcendentals=0
        ),
        name="assemble",
    )(meta, *pieces)


def exchanged(arrays):
    peers = len(arrays)
    return [
        lax.ppermute(array, "ctx", [(i, i ^ k) for i in range(peers)]) if k else array
        for k, array in enumerate(arrays)
    ]


def back_to_previous(arrays):
    peers = len(arrays)
    pipes = lax.axis_size("pipe")
    return [
        lax.ppermute(
            array,
            ("pipe", "ctx"),
            [
                (pipe * peers + i, (pipe - 1) % pipes * peers + (i ^ k))
                for pipe in range(pipes)
                for i in range(peers)
            ],
        )
        for k, array in enumerate(arrays)
    ]


def shards(qkv_proj, cotangent, block_dest, doc_start, mr_filter):
    peers = lax.axis_size("ctx")
    pipes = lax.axis_size("pipe")
    tp_count = lax.axis_size("tp")
    channels = cotangent.shape[2]
    group_count, taps = mr_filter.shape[1:]
    group_size = channels // group_count
    units = channels // (peers * LANES)
    chunks = math.gcd(units, CHUNKS)
    width = channels // (peers * chunks)
    chunk_groups = width // group_size

    dest = lax.dynamic_index_in_dim(block_dest, lax.axis_index("pipe"), 0, keepdims=False)
    me_at = dest.shape[0]
    tp_at = me_at + 1
    here = [lax.axis_index("ctx"), lax.axis_index("tp")]
    meta = jnp.concatenate([dest, jnp.stack(here).astype(jnp.int32)])
    marks = jnp.broadcast_to(doc_start.astype(BF16), (16, doc_start.shape[1]))

    filt = lax.dynamic_index_in_dim(
        mr_filter[0].astype(F32).reshape(chunks, peers, chunk_groups, taps),
        lax.axis_index("ctx"),
        1,
        keepdims=False,
    )
    causal = jnp.pad(filt[:, :, ::-1], ((0, 0), (0, 0), (1, taps - 1)))
    anti = jnp.pad(filt, ((0, 0), (0, 0), (0, taps)))
    bases = jnp.stack([causal, anti], axis=1)

    to_previous = [(pipe, (pipe - 1) % pipes) for pipe in range(pipes)]
    key_value = lax.ppermute(qkv_proj[:, 1:], "pipe", to_previous)
    grad_in = lax.ppermute(cotangent, "pipe", to_previous)

    received = []
    for chunk in range(chunks):
        products = multiply(
            chunk, width, peers, me_at, meta, qkv_proj, cotangent, marks if chunk == 0 else None
        )
        received.append(exchanged(products))
    masks = document_masks(me_at, meta, received[0], marks.shape[0])
    backs = []
    for chunk in range(chunks):
        convolved = convolve(group_size, me_at, meta, received[chunk], masks, bases[chunk])
        backs.append(back_to_previous(convolved))

    pieces = []
    for chunk in range(chunks):
        keep, cross = gradients(
            chunk, me_at, tp_at, tp_count, meta, backs[chunk], key_value, grad_in
        )
        pieces.append(keep)
        pieces.append(lax.ppermute(cross, "tp", [(0, 1), (1, 0)]))
    return assemble(tp_at, channels, tp_count, meta, pieces)


def solution(mesh):
    placed = (
        P("pipe", None, "ctx", "tp"),
        P("pipe", "ctx", "tp"),
        P(),
        P("pipe", "ctx"),
        P("pipe", "tp", None),
    )
    return jax.shard_map(
        shards,
        mesh=mesh,
        in_specs=placed,
        out_specs=P("pipe", None, ("ctx", "tp"), None),
        check_vma=False,
    )
```

```python
import functools
import math

import jax
import jax.numpy as jnp
from jax import lax
from jax.experimental import pallas as pl
from jax.experimental.pallas import tpu as pltpu
from jax.sharding import PartitionSpec as P

LANES = 128
CHUNKS = 2
VMEM_BYTES = 60 * 1024 * 1024
F32 = jnp.float32
BF16 = jnp.bfloat16


def params():
    return pltpu.CompilerParams(vmem_limit_bytes=VMEM_BYTES)


def whole_block(*shape):
    return pl.BlockSpec(shape, lambda _: (0,) * len(shape))


def smem():
    return pl.BlockSpec(memory_space=pltpu.SMEM)


def sending_order(peers):
    half = peers // 2
    return [k for i in range(half) for k in (half + i, i)]


def multiply_kernel(marked, me_at, meta_ref, proj_ref, grad_ref, *rest):
    marks_ref, outs = (rest[0], rest[1:-1]) if marked else (None, rest[:-1])
    side_ref = rest[-1]
    rows = grad_ref.shape[1]
    width = outs[0].shape[1]
    me = meta_ref[me_at]
    side_ref[0] = proj_ref[0, 1]
    side_ref[1] = proj_ref[0, 2]
    side_ref[2] = grad_ref[0]
    for k, out_ref in zip(sending_order(len(outs)), outs):
        lanes = pl.ds(pl.multiple_of((me ^ k) * width, LANES), width)
        query = proj_ref[0, 0, :, lanes].astype(F32)
        key_rows = proj_ref[0, 1, :, lanes].astype(F32)
        value = proj_ref[0, 2, :, lanes].astype(F32)
        grad_in = grad_ref[0, :, lanes].astype(F32)
        out_ref[:rows, :] = (key_rows * value).astype(BF16)
        out_ref[rows : 2 * rows, :] = (grad_in * query).astype(BF16)
        if marked:
            out_ref[2 * rows :, :LANES] = marks_ref[...]
            if width > LANES:
                out_ref[2 * rows :, LANES:] = jnp.zeros(
                    (marks_ref.shape[0], width - LANES), BF16
                )


def multiply(index, width, peers, me_at, meta, qkv_proj, cotangent, marks):
    rows = cotangent.shape[1]
    span = peers * width
    marked = marks is not None
    extra = marks.shape[0] if marked else 0
    in_specs = [
        smem(),
        pl.BlockSpec((1, 3, rows, span), lambda _: (0, 0, 0, index)),
        pl.BlockSpec((1, rows, span), lambda _: (0, 0, index)),
    ]
    args = [meta, qkv_proj, cotangent]
    if marked:
        in_specs.append(whole_block(*marks.shape))
        args.append(marks)
    out = (2 * rows + extra, width)
    side = (3, rows, span)
    return pl.pallas_call(
        functools.partial(multiply_kernel, marked, me_at),
        out_shape=[jax.ShapeDtypeStruct(out, BF16)] * peers + [jax.ShapeDtypeStruct(side, BF16)],
        in_specs=in_specs,
        out_specs=[whole_block(*out)] * peers + [whole_block(*side)],
        compiler_params=params(),
        cost_estimate=pl.CostEstimate(
            flops=2 * rows * span, bytes_accessed=18 * rows * span, transcendentals=0
        ),
        grid=(1,),
        name="multiply",
    )(*args)


def first_row(meta_ref, peers, source, block):
    block_rows = LANES // peers
    row = meta_ref[source * peers + block] * block_rows
    return pl.multiple_of(row, block_rows)


def masks_kernel(me_at, meta_ref, *refs):
    marks_refs, (out_ref, seq, across) = refs[:-3], refs[-3:]
    peers = len(marks_refs)
    tile = LANES
    block_rows = tile // peers
    me = meta_ref[me_at]
    row_ids = lax.broadcasted_iota(jnp.int32, (tile, tile), 0)
    lane_ids = lax.broadcasted_iota(jnp.int32, (tile, tile), 1)
    eye = (row_ids == lane_ids).astype(BF16)
    lower = (row_ids >= lane_ids).astype(BF16)
    for k, marks_ref in zip(sending_order(peers), marks_refs):
        spread = lax.dot_general(
            eye, marks_ref[...], (((1,), (1,)), ((), ())), preferred_element_type=F32
        )
        column = jnp.broadcast_to(spread[:, :1], (tile, tile))
        for block in range(peers):
            first = first_row(meta_ref, peers, me ^ k, block)
            seq[pl.ds(first, block_rows), :] = column[
                block * block_rows : (block + 1) * block_rows
            ]
    carry = jnp.zeros((1, tile), F32)
    for b in range(peers):
        rows = slice(b * tile, (b + 1) * tile)
        count = (
            jnp.dot(lower, seq[rows, :].astype(BF16), preferred_element_type=F32) + carry
        )
        carry = count[tile - 1 :, :]
        seq[rows, :] = count
        across[rows, :] = count.T
    for b in range(peers):
        here = seq[b * tile : (b + 1) * tile, :]

        def same(other):
            return (here == across[other * tile : (other + 1) * tile, :]).astype(F32).astype(BF16)

        out_ref[b, 0, :, :tile] = same(max(b - 1, 0))
        out_ref[b, 0, :, tile:] = same(b)
        out_ref[b, 1, :, :tile] = same(b)
        out_ref[b, 1, :, tile:] = same(min(b + 1, peers - 1))


def document_masks(me_at, meta, received, mark_rows):
    peers = len(received)
    tile = LANES
    last = received[0].shape[0] // mark_rows - 1
    out = (peers, 2, tile, 2 * tile)
    return pl.pallas_call(
        functools.partial(masks_kernel, me_at),
        out_shape=jax.ShapeDtypeStruct(out, BF16),
        in_specs=[smem()] + [pl.BlockSpec((mark_rows, tile), lambda _: (last, 0))] * peers,
        out_specs=whole_block(*out),
        scratch_shapes=[
            pltpu.VMEM((peers * tile, tile), F32),
            pltpu.VMEM((peers * tile, tile), F32),
        ],
        compiler_params=params(),
        cost_estimate=pl.CostEstimate(
            flops=8 * peers * tile * tile, bytes_accessed=8 * peers * tile * tile, transcendentals=0
        ),
        grid=(1,),
        name="masks",
    )(meta, *received)


def conv_kernel(group_size, me_at, meta_ref, mask_ref, base_ref, *refs):
    rows32, rows16, toep = refs[-3:]
    peers = (len(refs) - 3) // 2
    recv, outs = refs[:peers], refs[peers : 2 * peers]
    tile = LANES
    width = outs[0].shape[1]
    groups = base_ref.shape[1]
    block_rows = tile // peers
    me = meta_ref[me_at]
    rows16[0, :tile, :] = jnp.zeros((tile, width), BF16)
    rows16[1, peers * tile :, :] = jnp.zeros((tile, width), BF16)

    for half in range(2):
        for group in range(groups):
            base = jnp.broadcast_to(base_ref[half, group : group + 1, :], (tile, 2 * tile))
            toep[half, group] = pltpu.roll(base, 0, 1, stride=1, stride_axis=0).astype(BF16)

    for k, recv_ref in zip(sending_order(peers), recv):
        firsts = [first_row(meta_ref, peers, me ^ k, block) for block in range(peers)]
        for half in range(2):
            arrived = recv_ref[half * tile : (half + 1) * tile, :].astype(F32)
            for block in range(peers):
                rows32[half, pl.ds(firsts[block], block_rows), :] = arrived[
                    block * block_rows : (block + 1) * block_rows
                ]
    rows16[0, tile:, :] = rows32[0].astype(BF16)
    rows16[1, : peers * tile, :] = rows32[1].astype(BF16)

    tile_groups = tile // group_size
    lane_group = lax.broadcasted_iota(jnp.int32, (tile, tile), 1) // group_size

    def one_tile(b, carry):
        first = pl.multiple_of(b * tile, tile)
        for half in range(2):
            mask = mask_ref[b, half]
            for sub in range(width // tile):
                lanes = slice(sub * tile, (sub + 1) * tile)
                window = rows16[half, pl.ds(first, 2 * tile), lanes]
                total = jnp.zeros((tile, tile), F32)
                for group in range(tile_groups):
                    part = jnp.dot(
                        toep[half, sub * tile_groups + group] * mask,
                        window,
                        preferred_element_type=F32,
                    )
                    total = jnp.where(lane_group == group, part, total)
                rows32[half, pl.ds(first, tile), lanes] = total
        return carry

    lax.fori_loop(0, peers, one_tile, 0)

    for k, out_ref in zip(sending_order(peers), outs):
        firsts = [first_row(meta_ref, peers, me ^ k, block) for block in range(peers)]
        for half in range(2):
            pieces = [rows32[half, pl.ds(first, block_rows), :] for first in firsts]
            out_ref[half * tile : (half + 1) * tile, :] = jnp.concatenate(pieces, axis=0).astype(
                BF16
            )


def convolve(group_size, me_at, meta, received, masks, bases):
    peers = len(received)
    tile = LANES
    width = received[0].shape[1]
    groups = bases.shape[1]
    out = (2 * tile, width)
    return pl.pallas_call(
        functools.partial(conv_kernel, group_size, me_at),
        out_shape=[jax.ShapeDtypeStruct(out, BF16)] * peers,
        in_specs=[smem(), whole_block(*masks.shape), whole_block(*bases.shape)]
        + [whole_block(*received[0].shape)] * peers,
        out_specs=[whole_block(*out)] * peers,
        scratch_shapes=[
            pltpu.VMEM((2, peers * tile, width), F32),
            pltpu.VMEM((2, (peers + 1) * tile, width), BF16),
            pltpu.VMEM((2, groups, tile, 2 * tile), BF16),
        ],
        compiler_params=params(),
        cost_estimate=pl.CostEstimate(
            flops=8 * groups * peers * tile**3,
            bytes_accessed=8 * peers * tile * width + 4 * peers * tile**2,
            transcendentals=0,
        ),
        grid=(1,),
        name="convolve",
    )(meta, masks, bases, *received)


def gradients_kernel(me_at, tp_at, meta_ref, side_ref, *refs):
    backs, (keep_ref, cross_ref) = refs[:-2], refs[-2:]
    rows = side_ref.shape[1]
    width = backs[0].shape[1]
    part = keep_ref.shape[1]
    me = meta_ref[me_at]
    mine = meta_ref[tp_at]
    for out_ref, index in ((keep_ref, mine), (cross_ref, 1 - mine)):
        first = pl.multiple_of(index * part, part)
        at = pl.ds(first, part)
        later = pl.ds(pl.multiple_of(first + rows, part), part)
        for k, back_ref in zip(sending_order(len(backs)), backs):
            lanes = pl.ds(pl.multiple_of((me ^ k) * width, LANES), width)
            medium = back_ref[at, :].astype(F32)
            mixed_grad = back_ref[later, :].astype(F32)
            key_rows = side_ref[0, at, lanes].astype(F32)
            value = side_ref[1, at, lanes].astype(F32)
            grad_in = side_ref[2, at, lanes].astype(F32)
            out_ref[0, :, lanes] = (grad_in * medium).astype(BF16)
            out_ref[1, :, lanes] = (mixed_grad * value).astype(BF16)
            out_ref[2, :, lanes] = (mixed_grad * key_rows).astype(BF16)


def gradients(me_at, tp_at, tp_count, meta, backs, side):
    peers = len(backs)
    _, rows, span = side.shape
    out = (3, rows // tp_count, span)
    return pl.pallas_call(
        functools.partial(gradients_kernel, me_at, tp_at),
        out_shape=[jax.ShapeDtypeStruct(out, BF16)] * 2,
        in_specs=[smem(), whole_block(*side.shape)] + [whole_block(*backs[0].shape)] * peers,
        out_specs=[whole_block(*out)] * 2,
        compiler_params=params(),
        cost_estimate=pl.CostEstimate(
            flops=3 * rows * span, bytes_accessed=16 * rows * span, transcendentals=0
        ),
        grid=(1,),
        name="gradients",
    )(meta, side, *backs)


def assemble_kernel(tp_at, half_width, meta_ref, *refs):
    pieces, out_ref = refs[:-1], refs[-1]
    mine = meta_ref[tp_at]
    done = 0
    for keep, cross in zip(pieces[::2], pieces[1::2]):
        width = keep.shape[2]
        for piece, index in ((keep, mine), (cross, 1 - mine)):
            first = pl.multiple_of(index * half_width + done, LANES)
            out_ref[0, 0, :, pl.ds(first, width)] = piece[0]
        done += width


def assemble(tp_at, channels, tp_count, meta, pieces):
    three, part, _ = pieces[0].shape
    out = (1, three, part, tp_count * channels)
    return pl.pallas_call(
        functools.partial(assemble_kernel, tp_at, channels),
        out_shape=jax.ShapeDtypeStruct(out, BF16),
        grid=(three,),
        in_specs=[smem()] + [pl.BlockSpec((1,) + p.shape[1:], lambda i: (i, 0, 0)) for p in pieces],
        out_specs=pl.BlockSpec((1, 1) + out[2:], lambda i: (0, i, 0, 0)),
        compiler_params=params(),
        cost_estimate=pl.CostEstimate(
            flops=0, bytes_accessed=4 * three * part * tp_count * channels, transcendentals=0
        ),
        name="assemble",
    )(meta, *pieces)


def exchanged(arrays):
    peers = len(arrays)
    return [
        lax.ppermute(array, "ctx", [(i, i ^ k) for i in range(peers)]) if k else array
        for k, array in zip(sending_order(peers), arrays)
    ]


def back_to_previous(arrays):
    peers = len(arrays)
    pipes = lax.axis_size("pipe")
    return [
        lax.ppermute(
            array,
            ("pipe", "ctx"),
            [
                (pipe * peers + i, (pipe - 1) % pipes * peers + (i ^ k))
                for pipe in range(pipes)
                for i in range(peers)
            ],
        )
        for k, array in zip(sending_order(peers), arrays)
    ]


def shards(qkv_proj, cotangent, block_dest, doc_start, mr_filter):
    peers = lax.axis_size("ctx")
    pipes = lax.axis_size("pipe")
    tp_count = lax.axis_size("tp")
    channels = cotangent.shape[2]
    group_count, taps = mr_filter.shape[1:]
    group_size = channels // group_count
    units = channels // (peers * LANES)
    chunks = math.gcd(units, CHUNKS)
    width = channels // (peers * chunks)
    chunk_groups = width // group_size

    dest = lax.dynamic_index_in_dim(block_dest, lax.axis_index("pipe"), 0, keepdims=False)
    me_at = dest.shape[0]
    tp_at = me_at + 1
    here = [lax.axis_index("ctx"), lax.axis_index("tp")]
    meta = jnp.concatenate([dest, jnp.stack(here).astype(jnp.int32)])
    marks = jnp.broadcast_to(doc_start.astype(BF16), (16, doc_start.shape[1]))

    filt = lax.dynamic_index_in_dim(
        mr_filter[0].astype(F32).reshape(chunks, peers, chunk_groups, taps),
        lax.axis_index("ctx"),
        1,
        keepdims=False,
    )
    causal = jnp.pad(filt[:, :, ::-1], ((0, 0), (0, 0), (1, taps - 1)))
    anti = jnp.pad(filt, ((0, 0), (0, 0), (0, taps)))
    bases = jnp.stack([causal, anti], axis=1)

    to_previous = [(pipe, (pipe - 1) % pipes) for pipe in range(pipes)]
    received, sides = [], []
    for chunk in range(chunks):
        *products, side = multiply(
            chunk, width, peers, me_at, meta, qkv_proj, cotangent, marks if chunk == 0 else None
        )
        received.append(exchanged(products))
        sides.append(lax.ppermute(side, "pipe", to_previous))
    masks = document_masks(me_at, meta, received[0], marks.shape[0])
    backs = []
    for chunk in range(chunks):
        convolved = convolve(group_size, me_at, meta, received[chunk], masks, bases[chunk])
        backs.append(back_to_previous(convolved))

    pieces = []
    for chunk in range(chunks):
        keep, cross = gradients(me_at, tp_at, tp_count, meta, backs[chunk], sides[chunk])
        pieces.append(keep)
        pieces.append(lax.ppermute(cross, "tp", [(0, 1), (1, 0)]))
    return assemble(tp_at, channels, tp_count, meta, pieces)


def solution(mesh):
    placed = (
        P("pipe", None, "ctx", "tp"),
        P("pipe", "ctx", "tp"),
        P(),
        P("pipe", "ctx"),
        P("pipe", "tp", None),
    )
    return jax.shard_map(
        shards,
        mesh=mesh,
        in_specs=placed,
        out_specs=P("pipe", None, ("ctx", "tp"), None),
        check_vma=False,
    )
```

```python
import functools
import math

import jax
import jax.numpy as jnp
from jax import lax
from jax.experimental import pallas as pl
from jax.experimental.pallas import tpu as pltpu
from jax.sharding import PartitionSpec as P

LANES = 128
CHUNKS = 2
VMEM_BYTES = 60 * 1024 * 1024
F32 = jnp.float32
BF16 = jnp.bfloat16


def params():
    return pltpu.CompilerParams(vmem_limit_bytes=VMEM_BYTES)


def whole_block(*shape):
    return pl.BlockSpec(shape, lambda _: (0,) * len(shape))


def smem():
    return pl.BlockSpec(memory_space=pltpu.SMEM)


def sending_order(peers):
    half = peers // 2
    return [k for i in range(half) for k in (half + i, i)]


def multiply_kernel(marked, me_at, meta_ref, proj_ref, grad_ref, *rest):
    marks_ref, outs = (rest[0], rest[1:-1]) if marked else (None, rest[:-1])
    side_ref = rest[-1]
    rows = grad_ref.shape[1]
    width = outs[0].shape[1]
    me = meta_ref[me_at]
    side_ref[0] = proj_ref[0, 1]
    side_ref[1] = proj_ref[0, 2]
    side_ref[2] = grad_ref[0]
    for k, out_ref in zip(sending_order(len(outs)), outs):
        lanes = pl.ds(pl.multiple_of((me ^ k) * width, LANES), width)
        query = proj_ref[0, 0, :, lanes].astype(F32)
        key_rows = proj_ref[0, 1, :, lanes].astype(F32)
        value = proj_ref[0, 2, :, lanes].astype(F32)
        grad_in = grad_ref[0, :, lanes].astype(F32)
        out_ref[:rows, :] = (key_rows * value).astype(BF16)
        out_ref[rows : 2 * rows, :] = (grad_in * query).astype(BF16)
        if marked:
            out_ref[2 * rows :, :LANES] = marks_ref[...]
            if width > LANES:
                out_ref[2 * rows :, LANES:] = jnp.zeros(
                    (marks_ref.shape[0], width - LANES), BF16
                )


def multiply(index, width, peers, me_at, meta, qkv_proj, cotangent, marks):
    rows = cotangent.shape[1]
    span = peers * width
    marked = marks is not None
    extra = marks.shape[0] if marked else 0
    in_specs = [
        smem(),
        pl.BlockSpec((1, 3, rows, span), lambda _: (0, 0, 0, index)),
        pl.BlockSpec((1, rows, span), lambda _: (0, 0, index)),
    ]
    args = [meta, qkv_proj, cotangent]
    if marked:
        in_specs.append(whole_block(*marks.shape))
        args.append(marks)
    out = (2 * rows + extra, width)
    side = (3, rows, span)
    return pl.pallas_call(
        functools.partial(multiply_kernel, marked, me_at),
        out_shape=[jax.ShapeDtypeStruct(out, BF16)] * peers + [jax.ShapeDtypeStruct(side, BF16)],
        in_specs=in_specs,
        out_specs=[whole_block(*out)] * peers + [whole_block(*side)],
        compiler_params=params(),
        cost_estimate=pl.CostEstimate(
            flops=2 * rows * span, bytes_accessed=18 * rows * span, transcendentals=0
        ),
        grid=(1,),
        name="multiply",
    )(*args)


def first_row(meta_ref, peers, source, block):
    block_rows = LANES // peers
    row = meta_ref[source * peers + block] * block_rows
    return pl.multiple_of(row, block_rows)


def masks_kernel(me_at, meta_ref, *refs):
    marks_refs, (out_ref, seq, across) = refs[:-3], refs[-3:]
    peers = len(marks_refs)
    tile = LANES
    block_rows = tile // peers
    me = meta_ref[me_at]
    row_ids = lax.broadcasted_iota(jnp.int32, (tile, tile), 0)
    lane_ids = lax.broadcasted_iota(jnp.int32, (tile, tile), 1)
    eye = (row_ids == lane_ids).astype(BF16)
    lower = (row_ids >= lane_ids).astype(BF16)
    for k, marks_ref in zip(sending_order(peers), marks_refs):
        spread = lax.dot_general(
            eye, marks_ref[...], (((1,), (1,)), ((), ())), preferred_element_type=F32
        )
        column = jnp.broadcast_to(spread[:, :1], (tile, tile))
        for block in range(peers):
            first = first_row(meta_ref, peers, me ^ k, block)
            seq[pl.ds(first, block_rows), :] = column[
                block * block_rows : (block + 1) * block_rows
            ]
    carry = jnp.zeros((1, tile), F32)
    for b in range(peers):
        rows = slice(b * tile, (b + 1) * tile)
        count = (
            jnp.dot(lower, seq[rows, :].astype(BF16), preferred_element_type=F32) + carry
        )
        carry = count[tile - 1 :, :]
        seq[rows, :] = count
        across[rows, :] = count.T
    for b in range(peers):
        here = seq[b * tile : (b + 1) * tile, :]

        def same(other):
            return (here == across[other * tile : (other + 1) * tile, :]).astype(F32).astype(BF16)

        out_ref[b, 0, :, :tile] = same(max(b - 1, 0))
        out_ref[b, 0, :, tile:] = same(b)
        out_ref[b, 1, :, :tile] = same(b)
        out_ref[b, 1, :, tile:] = same(min(b + 1, peers - 1))


def document_masks(me_at, meta, received, mark_rows):
    peers = len(received)
    tile = LANES
    last = received[0].shape[0] // mark_rows - 1
    out = (peers, 2, tile, 2 * tile)
    return pl.pallas_call(
        functools.partial(masks_kernel, me_at),
        out_shape=jax.ShapeDtypeStruct(out, BF16),
        in_specs=[smem()] + [pl.BlockSpec((mark_rows, tile), lambda _: (last, 0))] * peers,
        out_specs=whole_block(*out),
        scratch_shapes=[
            pltpu.VMEM((peers * tile, tile), F32),
            pltpu.VMEM((peers * tile, tile), F32),
        ],
        compiler_params=params(),
        cost_estimate=pl.CostEstimate(
            flops=8 * peers * tile * tile, bytes_accessed=8 * peers * tile * tile, transcendentals=0
        ),
        grid=(1,),
        name="masks",
    )(meta, *received)


def conv_kernel(group_size, me_at, meta_ref, mask_ref, base_ref, *refs):
    rows32, rows16, toep = refs[-3:]
    peers = (len(refs) - 3) // 2
    recv, outs = refs[:peers], refs[peers : 2 * peers]
    tile = LANES
    width = outs[0].shape[1]
    groups = base_ref.shape[1]
    block_rows = tile // peers
    me = meta_ref[me_at]
    rows16[0, :tile, :] = jnp.zeros((tile, width), BF16)
    rows16[1, peers * tile :, :] = jnp.zeros((tile, width), BF16)

    for half in range(2):
        for group in range(groups):
            base = jnp.broadcast_to(base_ref[half, group : group + 1, :], (tile, 2 * tile))
            toep[half, group] = pltpu.roll(base, 0, 1, stride=1, stride_axis=0).astype(BF16)

    for k, recv_ref in zip(sending_order(peers), recv):
        firsts = [first_row(meta_ref, peers, me ^ k, block) for block in range(peers)]
        for half in range(2):
            arrived = recv_ref[half * tile : (half + 1) * tile, :].astype(F32)
            for block in range(peers):
                rows32[half, pl.ds(firsts[block], block_rows), :] = arrived[
                    block * block_rows : (block + 1) * block_rows
                ]
    rows16[0, tile:, :] = rows32[0].astype(BF16)
    rows16[1, : peers * tile, :] = rows32[1].astype(BF16)

    tile_groups = tile // group_size
    lane_group = lax.broadcasted_iota(jnp.int32, (tile, tile), 1) // group_size

    def one_tile(b, carry):
        first = pl.multiple_of(b * tile, tile)
        for half in range(2):
            mask = mask_ref[b, half]
            for sub in range(width // tile):
                lanes = slice(sub * tile, (sub + 1) * tile)
                window = rows16[half, pl.ds(first, 2 * tile), lanes]
                total = jnp.zeros((tile, tile), F32)
                for group in range(tile_groups):
                    part = jnp.dot(
                        toep[half, sub * tile_groups + group] * mask,
                        window,
                        preferred_element_type=F32,
                    )
                    total = jnp.where(lane_group == group, part, total)
                rows32[half, pl.ds(first, tile), lanes] = total
        return carry

    lax.fori_loop(0, peers, one_tile, 0)

    for k, out_ref in zip(sending_order(peers), outs):
        firsts = [first_row(meta_ref, peers, me ^ k, block) for block in range(peers)]
        for half in range(2):
            pieces = [rows32[half, pl.ds(first, block_rows), :] for first in firsts]
            out_ref[half * tile : (half + 1) * tile, :] = jnp.concatenate(pieces, axis=0).astype(
                BF16
            )


def convolve(group_size, me_at, meta, received, masks, bases):
    peers = len(received)
    tile = LANES
    width = received[0].shape[1]
    groups = bases.shape[1]
    out = (2 * tile, width)
    return pl.pallas_call(
        functools.partial(conv_kernel, group_size, me_at),
        out_shape=[jax.ShapeDtypeStruct(out, BF16)] * peers,
        in_specs=[smem(), whole_block(*masks.shape), whole_block(*bases.shape)]
        + [whole_block(*received[0].shape)] * peers,
        out_specs=[whole_block(*out)] * peers,
        scratch_shapes=[
            pltpu.VMEM((2, peers * tile, width), F32),
            pltpu.VMEM((2, (peers + 1) * tile, width), BF16),
            pltpu.VMEM((2, groups, tile, 2 * tile), BF16),
        ],
        compiler_params=params(),
        cost_estimate=pl.CostEstimate(
            flops=8 * groups * peers * tile**3,
            bytes_accessed=8 * peers * tile * width + 4 * peers * tile**2,
            transcendentals=0,
        ),
        grid=(1,),
        name="convolve",
    )(meta, masks, bases, *received)


def gradients_kernel(me_at, tp_at, meta_ref, side_ref, *refs):
    backs, (keep_ref, cross_ref) = refs[:-2], refs[-2:]
    rows = side_ref.shape[2]
    width = backs[0].shape[1]
    part = keep_ref.shape[1]
    me = meta_ref[me_at]
    mine = meta_ref[tp_at]
    for out_ref, index in ((keep_ref, mine), (cross_ref, 1 - mine)):
        first = pl.multiple_of(index * part, part)
        at = pl.ds(first, part)
        later = pl.ds(pl.multiple_of(first + rows, part), part)
        for k, back_ref in zip(sending_order(len(backs)), backs):
            lanes = pl.ds(pl.multiple_of((me ^ k) * width, LANES), width)
            medium = back_ref[at, :].astype(F32)
            mixed_grad = back_ref[later, :].astype(F32)
            key_rows = side_ref[0, 0, at, lanes].astype(F32)
            value = side_ref[0, 1, at, lanes].astype(F32)
            grad_in = side_ref[0, 2, at, lanes].astype(F32)
            out_ref[0, :, lanes] = (grad_in * medium).astype(BF16)
            out_ref[1, :, lanes] = (mixed_grad * value).astype(BF16)
            out_ref[2, :, lanes] = (mixed_grad * key_rows).astype(BF16)


def gradients(me_at, tp_at, from_at, tp_count, meta, backs, side):
    peers = len(backs)
    _, _, rows, span = side.shape
    out = (3, rows // tp_count, span)

    def chosen(_, meta_ref):
        return (meta_ref[from_at], 0, 0, 0)

    def only(shape):
        return pl.BlockSpec(shape, lambda _, meta_ref: (0,) * len(shape))

    return pl.pallas_call(
        functools.partial(gradients_kernel, me_at, tp_at),
        out_shape=[jax.ShapeDtypeStruct(out, BF16)] * 2,
        grid_spec=pltpu.PrefetchScalarGridSpec(
            num_scalar_prefetch=1,
            grid=(1,),
            in_specs=[pl.BlockSpec((1, 3, rows, span), chosen)] + [only(backs[0].shape)] * peers,
            out_specs=[only(out)] * 2,
        ),
        compiler_params=params(),
        cost_estimate=pl.CostEstimate(
            flops=3 * rows * span, bytes_accessed=16 * rows * span, transcendentals=0
        ),
        name="gradients",
    )(meta, side, *backs)


def assemble_kernel(tp_at, half_width, meta_ref, *refs):
    pieces, out_ref = refs[:-1], refs[-1]
    mine = meta_ref[tp_at]
    done = 0
    for keep, cross in zip(pieces[::2], pieces[1::2]):
        width = keep.shape[2]
        for piece, index in ((keep, mine), (cross, 1 - mine)):
            first = pl.multiple_of(index * half_width + done, LANES)
            out_ref[0, 0, :, pl.ds(first, width)] = piece[0]
        done += width


def assemble(tp_at, channels, tp_count, meta, pieces):
    three, part, _ = pieces[0].shape
    out = (1, three, part, tp_count * channels)
    return pl.pallas_call(
        functools.partial(assemble_kernel, tp_at, channels),
        out_shape=jax.ShapeDtypeStruct(out, BF16),
        grid=(three,),
        in_specs=[smem()] + [pl.BlockSpec((1,) + p.shape[1:], lambda i: (i, 0, 0)) for p in pieces],
        out_specs=pl.BlockSpec((1, 1) + out[2:], lambda i: (0, i, 0, 0)),
        compiler_params=params(),
        cost_estimate=pl.CostEstimate(
            flops=0, bytes_accessed=4 * three * part * tp_count * channels, transcendentals=0
        ),
        name="assemble",
    )(meta, *pieces)


def exchanged(arrays):
    peers = len(arrays)
    return [
        lax.ppermute(array, "ctx", [(i, i ^ k) for i in range(peers)]) if k else array
        for k, array in zip(sending_order(peers), arrays)
    ]


def back_to_previous(arrays):
    peers = len(arrays)
    pipes = lax.axis_size("pipe")
    return [
        lax.ppermute(
            array,
            ("pipe", "ctx"),
            [
                (pipe * peers + i, (pipe - 1) % pipes * peers + (i ^ k))
                for pipe in range(pipes)
                for i in range(peers)
            ],
        )
        for k, array in zip(sending_order(peers), arrays)
    ]


def shards(qkv_proj, cotangent, block_dest, doc_start, mr_filter):
    peers = lax.axis_size("ctx")
    pipes = lax.axis_size("pipe")
    tp_count = lax.axis_size("tp")
    channels = cotangent.shape[2]
    group_count, taps = mr_filter.shape[1:]
    group_size = channels // group_count
    units = channels // (peers * LANES)
    chunks = math.gcd(units, CHUNKS)
    width = channels // (peers * chunks)
    chunk_groups = width // group_size

    dest = lax.dynamic_index_in_dim(block_dest, lax.axis_index("pipe"), 0, keepdims=False)
    me_at = dest.shape[0]
    tp_at = me_at + 1
    from_at = me_at + 2
    source_pipe = 1 - lax.axis_index("pipe") if pipes == 2 else jnp.int32(0)
    here = [lax.axis_index("ctx"), lax.axis_index("tp"), source_pipe]
    meta = jnp.concatenate([dest, jnp.stack(here).astype(jnp.int32)])
    marks = jnp.broadcast_to(doc_start.astype(BF16), (16, doc_start.shape[1]))

    filt = lax.dynamic_index_in_dim(
        mr_filter[0].astype(F32).reshape(chunks, peers, chunk_groups, taps),
        lax.axis_index("ctx"),
        1,
        keepdims=False,
    )
    causal = jnp.pad(filt[:, :, ::-1], ((0, 0), (0, 0), (1, taps - 1)))
    anti = jnp.pad(filt, ((0, 0), (0, 0), (0, taps)))
    bases = jnp.stack([causal, anti], axis=1)

    to_previous = [(pipe, (pipe - 1) % pipes) for pipe in range(pipes)]
    received, sides = [], []
    for chunk in range(chunks):
        *products, side = multiply(
            chunk, width, peers, me_at, meta, qkv_proj, cotangent, marks if chunk == 0 else None
        )
        received.append(exchanged(products))
        if pipes == 2:
            sides.append(lax.all_gather(side, "pipe"))
        else:
            sides.append(lax.ppermute(side, "pipe", to_previous)[None])
    masks = document_masks(me_at, meta, received[0], marks.shape[0])
    backs = []
    for chunk in range(chunks):
        convolved = convolve(group_size, me_at, meta, received[chunk], masks, bases[chunk])
        backs.append(back_to_previous(convolved))

    pieces = []
    for chunk in range(chunks):
        keep, cross = gradients(
            me_at, tp_at, from_at, tp_count, meta, backs[chunk], sides[chunk]
        )
        pieces.append(keep)
        pieces.append(lax.ppermute(cross, "tp", [(0, 1), (1, 0)]))
    return assemble(tp_at, channels, tp_count, meta, pieces)


def solution(mesh):
    placed = (
        P("pipe", None, "ctx", "tp"),
        P("pipe", "ctx", "tp"),
        P(),
        P("pipe", "ctx"),
        P("pipe", "tp", None),
    )
    return jax.shard_map(
        shards,
        mesh=mesh,
        in_specs=placed,
        out_specs=P("pipe", None, ("ctx", "tp"), None),
        check_vma=False,
    )
```

```python
import functools
import math

import jax
import jax.numpy as jnp
from jax import lax
from jax.experimental import pallas as pl
from jax.experimental.pallas import tpu as pltpu
from jax.sharding import PartitionSpec as P

LANES = 128
CHUNKS = 2
MARK_ROWS = 16
VMEM_BYTES = 60 * 1024 * 1024
F32 = jnp.float32
BF16 = jnp.bfloat16


def params():
    return pltpu.CompilerParams(vmem_limit_bytes=VMEM_BYTES)


def whole_block(*shape):
    return pl.BlockSpec(shape, lambda _: (0,) * len(shape))


def smem():
    return pl.BlockSpec(memory_space=pltpu.SMEM)


def sending_order(peers):
    half = peers // 2
    return [k for i in range(half) for k in (half + i, i)]


def multiply_kernel(stacked, marked, sided, *refs):
    refs = list(refs)
    proj_ref, grad_ref = refs[:2]
    marks_ref = refs[2] if marked else None
    outs = refs[3 if marked else 2 :]
    if sided:
        side_ref = outs.pop()
        side_ref[0] = proj_ref[0, 1]
        side_ref[1] = proj_ref[0, 2]
        side_ref[2] = grad_ref[0]
    rows = grad_ref.shape[1]
    width = outs[0].shape[-1]
    me = lax.axis_index("ctx")
    if stacked:
        peers = outs[0].shape[0]
        places = [(peer, outs[0].at[peer]) for peer in range(peers)]
    else:
        peers = len(outs)
        places = [(me ^ k, out_ref) for k, out_ref in zip(sending_order(peers), outs)]
    span = peers * width
    begin = grad_ref.shape[2] - span
    for peer, out_ref in places:
        lanes = pl.ds(pl.multiple_of(begin + peer * width, LANES), width)
        query = proj_ref[0, 0, :, lanes].astype(F32)
        key_rows = proj_ref[0, 1, :, lanes].astype(F32)
        value = proj_ref[0, 2, :, lanes].astype(F32)
        grad_in = grad_ref[0, :, lanes].astype(F32)
        out_ref[:rows, :] = (key_rows * value).astype(BF16)
        out_ref[rows : 2 * rows, :] = (grad_in * query).astype(BF16)
        if marked:
            extra = out_ref.shape[0] - 2 * rows
            marks = marks_ref[...].astype(F32)
            out_ref[2 * rows :, :LANES] = jnp.broadcast_to(marks, (extra, LANES)).astype(BF16)
            if width > LANES:
                out_ref[2 * rows :, LANES:] = jnp.zeros((extra, width - LANES), BF16)


def multiply(index, width, peers, qkv_proj, cotangent, marks, stacked, sided):
    _, rows, channels = cotangent.shape
    span = peers * width
    taken = channels if sided else span
    block = 0 if sided else index
    marked = marks is not None
    in_specs = [
        pl.BlockSpec((1, 3, rows, taken), lambda _: (0, 0, 0, block)),
        pl.BlockSpec((1, rows, taken), lambda _: (0, 0, block)),
    ]
    args = [qkv_proj, cotangent]
    if marked:
        in_specs.append(whole_block(*marks.shape))
        args.append(marks)
    out = (2 * rows + (MARK_ROWS if marked else 0), width)
    shapes = [(peers,) + out] if stacked else [out] * peers
    if sided:
        shapes.append((3, rows, channels))
    return pl.pallas_call(
        functools.partial(multiply_kernel, stacked, marked, sided),
        out_shape=[jax.ShapeDtypeStruct(shape, BF16) for shape in shapes],
        in_specs=in_specs,
        out_specs=[whole_block(*shape) for shape in shapes],
        compiler_params=params(),
        cost_estimate=pl.CostEstimate(
            flops=2 * rows * span, bytes_accessed=14 * rows * taken, transcendentals=0
        ),
        grid=(1,),
        name="multiply",
    )(*args)


def first_row(meta_ref, peers, source, block):
    block_rows = LANES // peers
    row = meta_ref[source * peers + block] * block_rows
    return pl.multiple_of(row, block_rows)


def masks_kernel(me_at, meta_ref, *refs):
    marks_refs, (out_ref, seq, across) = refs[:-3], refs[-3:]
    peers = len(marks_refs)
    tile = LANES
    block_rows = tile // peers
    me = meta_ref[me_at]
    row_ids = lax.broadcasted_iota(jnp.int32, (tile, tile), 0)
    lane_ids = lax.broadcasted_iota(jnp.int32, (tile, tile), 1)
    eye = (row_ids == lane_ids).astype(BF16)
    lower = (row_ids >= lane_ids).astype(BF16)
    for k, marks_ref in zip(sending_order(peers), marks_refs):
        spread = lax.dot_general(
            eye, marks_ref[...], (((1,), (1,)), ((), ())), preferred_element_type=F32
        )
        column = jnp.broadcast_to(spread[:, :1], (tile, tile))
        for block in range(peers):
            first = first_row(meta_ref, peers, me ^ k, block)
            seq[pl.ds(first, block_rows), :] = column[
                block * block_rows : (block + 1) * block_rows
            ]
    carry = jnp.zeros((1, tile), F32)
    for b in range(peers):
        rows = slice(b * tile, (b + 1) * tile)
        count = (
            jnp.dot(lower, seq[rows, :].astype(BF16), preferred_element_type=F32) + carry
        )
        carry = count[tile - 1 :, :]
        seq[rows, :] = count
        across[rows, :] = count.T
    for b in range(peers):
        here = seq[b * tile : (b + 1) * tile, :]

        def same(other):
            return (here == across[other * tile : (other + 1) * tile, :]).astype(F32).astype(BF16)

        out_ref[b, 0, :, :tile] = same(max(b - 1, 0))
        out_ref[b, 0, :, tile:] = same(b)
        out_ref[b, 1, :, :tile] = same(b)
        out_ref[b, 1, :, tile:] = same(min(b + 1, peers - 1))


def document_masks(me_at, meta, received, mark_rows):
    peers = len(received)
    tile = LANES
    last = received[0].shape[0] // mark_rows - 1
    out = (peers, 2, tile, 2 * tile)
    return pl.pallas_call(
        functools.partial(masks_kernel, me_at),
        out_shape=jax.ShapeDtypeStruct(out, BF16),
        in_specs=[smem()] + [pl.BlockSpec((mark_rows, tile), lambda _: (last, 0))] * peers,
        out_specs=whole_block(*out),
        scratch_shapes=[
            pltpu.VMEM((peers * tile, tile), F32),
            pltpu.VMEM((peers * tile, tile), F32),
        ],
        compiler_params=params(),
        cost_estimate=pl.CostEstimate(
            flops=8 * peers * tile * tile, bytes_accessed=8 * peers * tile * tile, transcendentals=0
        ),
        grid=(1,),
        name="masks",
    )(meta, *received)


def conv_kernel(group_size, me_at, peers, meta_ref, mask_ref, base_ref, *refs):
    rows32, rows16, toep = refs[-3:]
    recv, outs = refs[: -3 - peers], refs[-3 - peers : -3]
    me = meta_ref[me_at]
    if len(recv) == 1:
        arrivals = [(source, recv[0].at[source]) for source in range(peers)]
    else:
        arrivals = [(me ^ k, recv_ref) for k, recv_ref in zip(sending_order(peers), recv)]
    tile = LANES
    width = outs[0].shape[1]
    groups = base_ref.shape[1]
    block_rows = tile // peers
    rows16[0, :tile, :] = jnp.zeros((tile, width), BF16)
    rows16[1, peers * tile :, :] = jnp.zeros((tile, width), BF16)

    for half in range(2):
        for group in range(groups):
            base = jnp.broadcast_to(base_ref[half, group : group + 1, :], (tile, 2 * tile))
            toep[half, group] = pltpu.roll(base, 0, 1, stride=1, stride_axis=0).astype(BF16)

    for source, recv_ref in arrivals:
        firsts = [first_row(meta_ref, peers, source, block) for block in range(peers)]
        for half in range(2):
            arrived = recv_ref[half * tile : (half + 1) * tile, :].astype(F32)
            for block in range(peers):
                rows32[half, pl.ds(firsts[block], block_rows), :] = arrived[
                    block * block_rows : (block + 1) * block_rows
                ]
    rows16[0, tile:, :] = rows32[0].astype(BF16)
    rows16[1, : peers * tile, :] = rows32[1].astype(BF16)

    tile_groups = tile // group_size
    lane_group = lax.broadcasted_iota(jnp.int32, (tile, tile), 1) // group_size

    def one_tile(b, carry):
        first = pl.multiple_of(b * tile, tile)
        for half in range(2):
            mask = mask_ref[b, half]
            for sub in range(width // tile):
                lanes = slice(sub * tile, (sub + 1) * tile)
                window = rows16[half, pl.ds(first, 2 * tile), lanes]
                total = jnp.zeros((tile, tile), F32)
                for group in range(tile_groups):
                    part = jnp.dot(
                        toep[half, sub * tile_groups + group] * mask,
                        window,
                        preferred_element_type=F32,
                    )
                    total = jnp.where(lane_group == group, part, total)
                rows32[half, pl.ds(first, tile), lanes] = total
        return carry

    lax.fori_loop(0, peers, one_tile, 0)

    for k, out_ref in zip(sending_order(peers), outs):
        firsts = [first_row(meta_ref, peers, me ^ k, block) for block in range(peers)]
        for half in range(2):
            pieces = [rows32[half, pl.ds(first, block_rows), :] for first in firsts]
            out_ref[half * tile : (half + 1) * tile, :] = jnp.concatenate(pieces, axis=0).astype(
                BF16
            )


def convolve(group_size, me_at, meta, received, masks, bases):
    peers = masks.shape[0]
    tile = LANES
    width = received[0].shape[-1]
    groups = bases.shape[1]
    out = (2 * tile, width)
    return pl.pallas_call(
        functools.partial(conv_kernel, group_size, me_at, peers),
        out_shape=[jax.ShapeDtypeStruct(out, BF16)] * peers,
        in_specs=[smem(), whole_block(*masks.shape), whole_block(*bases.shape)]
        + [whole_block(*r.shape) for r in received],
        out_specs=[whole_block(*out)] * peers,
        scratch_shapes=[
            pltpu.VMEM((2, peers * tile, width), F32),
            pltpu.VMEM((2, (peers + 1) * tile, width), BF16),
            pltpu.VMEM((2, groups, tile, 2 * tile), BF16),
        ],
        compiler_params=params(),
        cost_estimate=pl.CostEstimate(
            flops=8 * groups * peers * tile**3,
            bytes_accessed=8 * peers * tile * width + 4 * peers * tile**2,
            transcendentals=0,
        ),
        grid=(1,),
        name="convolve",
    )(meta, masks, bases, *received)


def gradients_kernel(me_at, tp_at, meta_ref, side_ref, *refs):
    result_ref, cross_ref = refs[-2:]
    peers = count_backs(refs)
    rows = side_ref.shape[1]
    width = side_ref.shape[2] // peers
    part = cross_ref.shape[1]
    me = meta_ref[me_at]
    mine = meta_ref[tp_at]
    for out_ref, index in ((cross_ref, 1 - mine), (result_ref.at[0], mine)):
        first = pl.multiple_of(index * part, part)
        at = pl.ds(first, part)
        later = pl.ds(pl.multiple_of(first + rows, part), part)
        for k, back_ref in zip(sending_order(peers), refs):
            lanes = pl.ds(pl.multiple_of((me ^ k) * width, LANES), width)
            medium = back_ref[at, :].astype(F32)
            mixed_grad = back_ref[later, :].astype(F32)
            key_rows = side_ref[0, at, lanes].astype(F32)
            value = side_ref[1, at, lanes].astype(F32)
            grad_in = side_ref[2, at, lanes].astype(F32)
            out_ref[0, :, lanes] = (grad_in * medium).astype(BF16)
            out_ref[1, :, lanes] = (mixed_grad * value).astype(BF16)
            out_ref[2, :, lanes] = (mixed_grad * key_rows).astype(BF16)


def count_backs(refs):
    return sum(1 for ref in refs if len(ref.shape) == 2)


def fixed(shape):
    return pl.BlockSpec(shape, lambda _, meta_ref: (0,) * len(shape))


def result_block(shape, chunk, chunks, tp_at, mine):
    def place(_, meta_ref):
        owner = meta_ref[tp_at] if mine else 1 - meta_ref[tp_at]
        return (0, 0, 0, owner * chunks + chunk)

    return pl.BlockSpec((1,) + shape, place)


def gradients(chunk, chunks, me_at, tp_at, tp_count, meta, backs, side, result):
    peers = len(backs)
    _, rows, channels = side.shape
    span = channels // chunks
    out = (3, rows // tp_count, span)
    whole = (1, 3, rows // tp_count, channels * tp_count)
    in_specs = [pl.BlockSpec((3, rows, span), lambda _, meta_ref: (0, 0, chunk))]
    in_specs += [fixed(backs[0].shape)] * peers
    args = [meta, side, *backs]
    aliases = {}
    if result is not None:
        aliases = {len(args): 0}
        args.append(result)
        in_specs.append(pl.BlockSpec(memory_space=pl.ANY))
    return pl.pallas_call(
        functools.partial(gradients_kernel, me_at, tp_at),
        out_shape=[jax.ShapeDtypeStruct(whole, BF16), jax.ShapeDtypeStruct(out, BF16)],
        grid_spec=pltpu.PrefetchScalarGridSpec(
            num_scalar_prefetch=1,
            grid=(1,),
            in_specs=in_specs,
            out_specs=[result_block(out, chunk, chunks, tp_at, True), fixed(out)],
        ),
        input_output_aliases=aliases,
        compiler_params=params(),
        cost_estimate=pl.CostEstimate(
            flops=3 * rows * span, bytes_accessed=16 * rows * span, transcendentals=0
        ),
        name="gradients",
    )(*args)


def place_kernel(meta_ref, cross_ref, held_ref, result_ref):
    result_ref[0] = cross_ref[...]


def place(chunk, chunks, tp_at, meta, cross, result):
    return pl.pallas_call(
        place_kernel,
        out_shape=jax.ShapeDtypeStruct(result.shape, BF16),
        grid_spec=pltpu.PrefetchScalarGridSpec(
            num_scalar_prefetch=1,
            grid=(1,),
            in_specs=[fixed(cross.shape), pl.BlockSpec(memory_space=pl.ANY)],
            out_specs=result_block(cross.shape, chunk, chunks, tp_at, False),
        ),
        input_output_aliases={2: 0},
        compiler_params=params(),
        cost_estimate=pl.CostEstimate(
            flops=0, bytes_accessed=4 * math.prod(cross.shape), transcendentals=0
        ),
        name="place",
    )(meta, cross, result)


def exchanged(arrays):
    peers = len(arrays)
    return [
        lax.ppermute(array, "ctx", [(i, i ^ k) for i in range(peers)]) if k else array
        for k, array in zip(sending_order(peers), arrays)
    ]


def back_to_previous(arrays):
    peers = len(arrays)
    pipes = lax.axis_size("pipe")
    return [
        lax.ppermute(
            array,
            ("pipe", "ctx"),
            [
                (pipe * peers + i, (pipe - 1) % pipes * peers + (i ^ k))
                for pipe in range(pipes)
                for i in range(peers)
            ],
        )
        for k, array in zip(sending_order(peers), arrays)
    ]


def shards(qkv_proj, cotangent, block_dest, doc_start, mr_filter):
    peers = lax.axis_size("ctx")
    pipes = lax.axis_size("pipe")
    tp_count = lax.axis_size("tp")
    channels = cotangent.shape[2]
    group_count, taps = mr_filter.shape[1:]
    group_size = channels // group_count
    units = channels // (peers * LANES)
    chunks = math.gcd(units, CHUNKS)
    width = channels // (peers * chunks)
    chunk_groups = width // group_size

    dest = lax.dynamic_index_in_dim(block_dest, lax.axis_index("pipe"), 0, keepdims=False)
    me_at = dest.shape[0]
    tp_at = me_at + 1
    here = [lax.axis_index("ctx"), lax.axis_index("tp")]
    meta = jnp.concatenate([dest, jnp.stack(here).astype(jnp.int32)])

    filt = lax.dynamic_index_in_dim(
        mr_filter[0].astype(F32).reshape(chunks, peers, chunk_groups, taps),
        lax.axis_index("ctx"),
        1,
        keepdims=False,
    )
    causal = jnp.pad(filt[:, :, ::-1], ((0, 0), (0, 0), (1, taps - 1)))
    anti = jnp.pad(filt, ((0, 0), (0, 0), (0, taps)))
    bases = jnp.stack([causal, anti], axis=1)

    to_previous = [(pipe, (pipe - 1) % pipes) for pipe in range(pipes)]
    received = []
    for chunk in range(chunks):
        stacked = chunk > 0
        products = multiply(
            chunk,
            width,
            peers,
            qkv_proj,
            cotangent,
            doc_start if chunk == 0 else None,
            stacked,
            chunk == chunks - 1,
        )
        products = list(products)
        if chunk == chunks - 1:
            side = lax.ppermute(products.pop(), "pipe", to_previous)
        if stacked:
            received.append([lax.all_to_all(products[0], "ctx", 0, 0, tiled=True)])
        else:
            received.append(exchanged(products))
    masks = document_masks(me_at, meta, received[0], MARK_ROWS)
    backs = []
    for chunk in range(chunks):
        convolved = convolve(group_size, me_at, meta, received[chunk], masks, bases[chunk])
        backs.append(back_to_previous(convolved))

    result, held = None, []
    for chunk in range(chunks):
        result, cross = gradients(
            chunk, chunks, me_at, tp_at, tp_count, meta, backs[chunk], side, result
        )
        held.append(lax.ppermute(cross, "tp", [(0, 1), (1, 0)]))
    for chunk in range(chunks):
        result = place(chunk, chunks, tp_at, meta, held[chunk], result)
    return result


def solution(mesh):
    placed = (
        P("pipe", None, "ctx", "tp"),
        P("pipe", "ctx", "tp"),
        P(),
        P("pipe", "ctx"),
        P("pipe", "tp", None),
    )
    return jax.shard_map(
        shards,
        mesh=mesh,
        in_specs=placed,
        out_specs=P("pipe", None, ("ctx", "tp"), None),
        check_vma=False,
    )
```

```python
import functools
import math

import jax
import jax.numpy as jnp
from jax import lax
from jax.experimental import pallas as pl
from jax.experimental.pallas import tpu as pltpu
from jax.sharding import PartitionSpec as P

LANES = 128
CHUNKS = 2
MARK_ROWS = 16
VMEM_BYTES = 60 * 1024 * 1024
F32 = jnp.float32
BF16 = jnp.bfloat16


def params():
    return pltpu.CompilerParams(vmem_limit_bytes=VMEM_BYTES)


def whole_block(*shape):
    return pl.BlockSpec(shape, lambda _: (0,) * len(shape))


def smem():
    return pl.BlockSpec(memory_space=pltpu.SMEM)


def sending_order(peers):
    half = peers // 2
    return [k for i in range(half) for k in (half + i, i)]


def multiply_kernel(marked, sided, *refs):
    refs = list(refs)
    proj_ref, grad_ref = refs[:2]
    marks_ref = refs[2] if marked else None
    side_ref = refs.pop() if sided else None
    out_ref = refs[-1]
    if sided:
        side_ref[0] = proj_ref[0, 1]
        side_ref[1] = proj_ref[0, 2]
        side_ref[2] = grad_ref[0]
    rows = grad_ref.shape[1]
    peers, all_rows, width = out_ref.shape
    begin = grad_ref.shape[2] - peers * width
    for peer in range(peers):
        lanes = slice(begin + peer * width, begin + (peer + 1) * width)
        query = proj_ref[0, 0, :, lanes].astype(F32)
        key_rows = proj_ref[0, 1, :, lanes].astype(F32)
        value = proj_ref[0, 2, :, lanes].astype(F32)
        grad_in = grad_ref[0, :, lanes].astype(F32)
        out_ref[peer, :rows, :] = (key_rows * value).astype(BF16)
        out_ref[peer, rows : 2 * rows, :] = (grad_in * query).astype(BF16)
        if marked:
            extra = all_rows - 2 * rows
            marks = jnp.broadcast_to(marks_ref[...].astype(F32), (extra, LANES)).astype(BF16)
            out_ref[peer, 2 * rows :, :LANES] = marks
            if width > LANES:
                out_ref[peer, 2 * rows :, LANES:] = jnp.zeros((extra, width - LANES), BF16)


def multiply(index, width, peers, qkv_proj, cotangent, marks, sided, after):
    _, rows, channels = cotangent.shape
    span = peers * width
    taken = channels if sided else span
    block = 0 if sided else index
    marked = marks is not None
    in_specs = [
        pl.BlockSpec((1, 3, rows, taken), lambda _: (0, 0, 0, block)),
        pl.BlockSpec((1, rows, taken), lambda _: (0, 0, block)),
    ]
    args = [qkv_proj, cotangent]
    if marked:
        in_specs.append(whole_block(*marks.shape))
        args.append(marks)
    if after is not None:
        in_specs.append(pl.BlockSpec(memory_space=pl.ANY))
        args.append(after)
    shapes = [(peers, 2 * rows + (MARK_ROWS if marked else 0), width)]
    if sided:
        shapes.append((3, rows, channels))
    return pl.pallas_call(
        functools.partial(multiply_kernel, marked, sided),
        out_shape=[jax.ShapeDtypeStruct(shape, BF16) for shape in shapes],
        in_specs=in_specs,
        out_specs=[whole_block(*shape) for shape in shapes],
        compiler_params=params(),
        cost_estimate=pl.CostEstimate(
            flops=2 * rows * span, bytes_accessed=14 * rows * taken, transcendentals=0
        ),
        grid=(1,),
        name="multiply",
    )(*args)


def first_row(meta_ref, peers, source, block):
    block_rows = LANES // peers
    row = meta_ref[source * peers + block] * block_rows
    return pl.multiple_of(row, block_rows)


def masks_kernel(meta_ref, marks_ref, out_ref, seq, across):
    peers = marks_ref.shape[0]
    tile = LANES
    block_rows = tile // peers
    row_ids = lax.broadcasted_iota(jnp.int32, (tile, tile), 0)
    lane_ids = lax.broadcasted_iota(jnp.int32, (tile, tile), 1)
    eye = (row_ids == lane_ids).astype(BF16)
    lower = (row_ids >= lane_ids).astype(BF16)
    for source in range(peers):
        spread = lax.dot_general(
            eye, marks_ref[source], (((1,), (1,)), ((), ())), preferred_element_type=F32
        )
        column = jnp.broadcast_to(spread[:, :1], (tile, tile))
        for block in range(peers):
            first = first_row(meta_ref, peers, source, block)
            seq[pl.ds(first, block_rows), :] = column[
                block * block_rows : (block + 1) * block_rows
            ]
    carry = jnp.zeros((1, tile), F32)
    for b in range(peers):
        rows = slice(b * tile, (b + 1) * tile)
        count = (
            jnp.dot(lower, seq[rows, :].astype(BF16), preferred_element_type=F32) + carry
        )
        carry = count[tile - 1 :, :]
        seq[rows, :] = count
        across[rows, :] = count.T
    for b in range(peers):
        here = seq[b * tile : (b + 1) * tile, :]

        def same(other):
            return (here == across[other * tile : (other + 1) * tile, :]).astype(F32).astype(BF16)

        out_ref[b, 0, :, :tile] = same(max(b - 1, 0))
        out_ref[b, 0, :, tile:] = same(b)
        out_ref[b, 1, :, :tile] = same(b)
        out_ref[b, 1, :, tile:] = same(min(b + 1, peers - 1))


def document_masks(meta, received):
    peers, all_rows, _ = received.shape
    tile = LANES
    last = all_rows // MARK_ROWS - 1
    out = (peers, 2, tile, 2 * tile)
    return pl.pallas_call(
        masks_kernel,
        out_shape=jax.ShapeDtypeStruct(out, BF16),
        in_specs=[smem(), pl.BlockSpec((peers, MARK_ROWS, tile), lambda _: (0, last, 0))],
        out_specs=whole_block(*out),
        scratch_shapes=[
            pltpu.VMEM((peers * tile, tile), F32),
            pltpu.VMEM((peers * tile, tile), F32),
        ],
        compiler_params=params(),
        cost_estimate=pl.CostEstimate(
            flops=8 * peers * tile * tile, bytes_accessed=8 * peers * tile * tile, transcendentals=0
        ),
        grid=(1,),
        name="masks",
    )(meta, received)


def conv_kernel(group_size, me_at, meta_ref, mask_ref, base_ref, recv_ref, *refs):
    outs, (rows32, rows16, toep) = refs[:-3], refs[-3:]
    peers = len(outs)
    me = meta_ref[me_at]
    tile = LANES
    width = outs[0].shape[1]
    groups = base_ref.shape[1]
    block_rows = tile // peers
    rows16[0, :tile, :] = jnp.zeros((tile, width), BF16)
    rows16[1, peers * tile :, :] = jnp.zeros((tile, width), BF16)

    for half in range(2):
        for group in range(groups):
            base = jnp.broadcast_to(base_ref[half, group : group + 1, :], (tile, 2 * tile))
            toep[half, group] = pltpu.roll(base, 0, 1, stride=1, stride_axis=0).astype(BF16)

    for source in range(peers):
        firsts = [first_row(meta_ref, peers, source, block) for block in range(peers)]
        for half in range(2):
            arrived = recv_ref[source, half * tile : (half + 1) * tile, :].astype(F32)
            for block in range(peers):
                rows32[half, pl.ds(firsts[block], block_rows), :] = arrived[
                    block * block_rows : (block + 1) * block_rows
                ]
    rows16[0, tile:, :] = rows32[0].astype(BF16)
    rows16[1, : peers * tile, :] = rows32[1].astype(BF16)

    tile_groups = tile // group_size
    lane_group = lax.broadcasted_iota(jnp.int32, (tile, tile), 1) // group_size

    def one_tile(b, carry):
        first = pl.multiple_of(b * tile, tile)
        for half in range(2):
            mask = mask_ref[b, half]
            for sub in range(width // tile):
                lanes = slice(sub * tile, (sub + 1) * tile)
                window = rows16[half, pl.ds(first, 2 * tile), lanes]
                total = jnp.zeros((tile, tile), F32)
                for group in range(tile_groups):
                    part = jnp.dot(
                        toep[half, sub * tile_groups + group] * mask,
                        window,
                        preferred_element_type=F32,
                    )
                    total = jnp.where(lane_group == group, part, total)
                rows32[half, pl.ds(first, tile), lanes] = total
        return carry

    lax.fori_loop(0, peers, one_tile, 0)

    for k, out_ref in zip(sending_order(peers), outs):
        firsts = [first_row(meta_ref, peers, me ^ k, block) for block in range(peers)]
        for half in range(2):
            pieces = [rows32[half, pl.ds(first, block_rows), :] for first in firsts]
            out_ref[half * tile : (half + 1) * tile, :] = jnp.concatenate(pieces, axis=0).astype(
                BF16
            )


def convolve(group_size, me_at, meta, received, masks, bases):
    peers, _, width = received.shape
    tile = LANES
    groups = bases.shape[1]
    out = (2 * tile, width)
    return pl.pallas_call(
        functools.partial(conv_kernel, group_size, me_at),
        out_shape=[jax.ShapeDtypeStruct(out, BF16)] * peers,
        in_specs=[
            smem(),
            whole_block(*masks.shape),
            whole_block(*bases.shape),
            whole_block(*received.shape),
        ],
        out_specs=[whole_block(*out)] * peers,
        scratch_shapes=[
            pltpu.VMEM((2, peers * tile, width), F32),
            pltpu.VMEM((2, (peers + 1) * tile, width), BF16),
            pltpu.VMEM((2, groups, tile, 2 * tile), BF16),
        ],
        compiler_params=params(),
        cost_estimate=pl.CostEstimate(
            flops=8 * groups * peers * tile**3,
            bytes_accessed=8 * peers * tile * width + 4 * peers * tile**2,
            transcendentals=0,
        ),
        grid=(1,),
        name="convolve",
    )(meta, masks, bases, received)


def gradients_kernel(me_at, tp_at, meta_ref, side_ref, *refs):
    result_ref, cross_ref = refs[-2:]
    peers = count_backs(refs)
    rows = side_ref.shape[1]
    width = side_ref.shape[2] // peers
    part = cross_ref.shape[1]
    me = meta_ref[me_at]
    mine = meta_ref[tp_at]
    for out_ref, index in ((cross_ref, 1 - mine), (result_ref.at[0], mine)):
        first = pl.multiple_of(index * part, part)
        at = pl.ds(first, part)
        later = pl.ds(pl.multiple_of(first + rows, part), part)
        for k, back_ref in zip(sending_order(peers), refs):
            lanes = pl.ds(pl.multiple_of((me ^ k) * width, LANES), width)
            medium = back_ref[at, :].astype(F32)
            mixed_grad = back_ref[later, :].astype(F32)
            key_rows = side_ref[0, at, lanes].astype(F32)
            value = side_ref[1, at, lanes].astype(F32)
            grad_in = side_ref[2, at, lanes].astype(F32)
            out_ref[0, :, lanes] = (grad_in * medium).astype(BF16)
            out_ref[1, :, lanes] = (mixed_grad * value).astype(BF16)
            out_ref[2, :, lanes] = (mixed_grad * key_rows).astype(BF16)


def count_backs(refs):
    return sum(1 for ref in refs if len(ref.shape) == 2)


def fixed(shape):
    return pl.BlockSpec(shape, lambda _, meta_ref: (0,) * len(shape))


def result_block(shape, chunk, chunks, tp_at, mine):
    def place(_, meta_ref):
        owner = meta_ref[tp_at] if mine else 1 - meta_ref[tp_at]
        return (0, 0, 0, owner * chunks + chunk)

    return pl.BlockSpec((1,) + shape, place)


def gradients(chunk, chunks, me_at, tp_at, tp_count, meta, backs, side, result):
    peers = len(backs)
    _, rows, channels = side.shape
    span = channels // chunks
    out = (3, rows // tp_count, span)
    whole = (1, 3, rows // tp_count, channels * tp_count)
    in_specs = [pl.BlockSpec((3, rows, span), lambda _, meta_ref: (0, 0, chunk))]
    in_specs += [fixed(backs[0].shape)] * peers
    args = [meta, side, *backs]
    aliases = {}
    if result is not None:
        aliases = {len(args): 0}
        args.append(result)
        in_specs.append(pl.BlockSpec(memory_space=pl.ANY))
    return pl.pallas_call(
        functools.partial(gradients_kernel, me_at, tp_at),
        out_shape=[jax.ShapeDtypeStruct(whole, BF16), jax.ShapeDtypeStruct(out, BF16)],
        grid_spec=pltpu.PrefetchScalarGridSpec(
            num_scalar_prefetch=1,
            grid=(1,),
            in_specs=in_specs,
            out_specs=[result_block(out, chunk, chunks, tp_at, True), fixed(out)],
        ),
        input_output_aliases=aliases,
        compiler_params=params(),
        cost_estimate=pl.CostEstimate(
            flops=3 * rows * span, bytes_accessed=16 * rows * span, transcendentals=0
        ),
        name="gradients",
    )(*args)


def place_kernel(meta_ref, cross_ref, held_ref, result_ref):
    result_ref[0] = cross_ref[...]


def place(chunk, chunks, tp_at, meta, cross, result):
    return pl.pallas_call(
        place_kernel,
        out_shape=jax.ShapeDtypeStruct(result.shape, BF16),
        grid_spec=pltpu.PrefetchScalarGridSpec(
            num_scalar_prefetch=1,
            grid=(1,),
            in_specs=[fixed(cross.shape), pl.BlockSpec(memory_space=pl.ANY)],
            out_specs=result_block(cross.shape, chunk, chunks, tp_at, False),
        ),
        input_output_aliases={2: 0},
        compiler_params=params(),
        cost_estimate=pl.CostEstimate(
            flops=0, bytes_accessed=4 * math.prod(cross.shape), transcendentals=0
        ),
        name="place",
    )(meta, cross, result)


def back_to_previous(arrays):
    peers = len(arrays)
    pipes = lax.axis_size("pipe")
    return [
        lax.ppermute(
            array,
            ("pipe", "ctx"),
            [
                (pipe * peers + i, (pipe - 1) % pipes * peers + (i ^ k))
                for pipe in range(pipes)
                for i in range(peers)
            ],
        )
        for k, array in zip(sending_order(peers), arrays)
    ]


def shards(qkv_proj, cotangent, block_dest, doc_start, mr_filter):
    peers = lax.axis_size("ctx")
    pipes = lax.axis_size("pipe")
    tp_count = lax.axis_size("tp")
    channels = cotangent.shape[2]
    group_count, taps = mr_filter.shape[1:]
    group_size = channels // group_count
    units = channels // (peers * LANES)
    chunks = math.gcd(units, CHUNKS)
    width = channels // (peers * chunks)
    chunk_groups = width // group_size

    dest = lax.dynamic_index_in_dim(block_dest, lax.axis_index("pipe"), 0, keepdims=False)
    me_at = dest.shape[0]
    tp_at = me_at + 1
    here = [lax.axis_index("ctx"), lax.axis_index("tp")]
    meta = jnp.concatenate([dest, jnp.stack(here).astype(jnp.int32)])

    filt = lax.dynamic_index_in_dim(
        mr_filter[0].astype(F32).reshape(chunks, peers, chunk_groups, taps),
        lax.axis_index("ctx"),
        1,
        keepdims=False,
    )
    causal = jnp.pad(filt[:, :, ::-1], ((0, 0), (0, 0), (1, taps - 1)))
    anti = jnp.pad(filt, ((0, 0), (0, 0), (0, taps)))
    bases = jnp.stack([causal, anti], axis=1)

    to_previous = [(pipe, (pipe - 1) % pipes) for pipe in range(pipes)]
    received = []
    products = None
    for chunk in range(chunks):
        last = chunk == chunks - 1
        products, *side = multiply(
            chunk,
            width,
            peers,
            qkv_proj,
            cotangent,
            doc_start if chunk == 0 else None,
            last,
            products,
        )
        received.append(lax.all_to_all(products, "ctx", 0, 0, tiled=True))
    side = lax.ppermute(side[0], "pipe", to_previous)
    masks = document_masks(meta, received[0])
    backs = []
    for chunk in range(chunks):
        convolved = convolve(group_size, me_at, meta, received[chunk], masks, bases[chunk])
        backs.append(back_to_previous(convolved))

    result = None
    for chunk in range(chunks):
        result, cross = gradients(
            chunk, chunks, me_at, tp_at, tp_count, meta, backs[chunk], side, result
        )
        cross = lax.ppermute(cross, "tp", [(0, 1), (1, 0)])
        result = place(chunk, chunks, tp_at, meta, cross, result)
    return result


def solution(mesh):
    placed = (
        P("pipe", None, "ctx", "tp"),
        P("pipe", "ctx", "tp"),
        P(),
        P("pipe", "ctx"),
        P("pipe", "tp", None),
    )
    return jax.shard_map(
        shards,
        mesh=mesh,
        in_specs=placed,
        out_specs=P("pipe", None, ("ctx", "tp"), None),
        check_vma=False,
    )
```

```python
import functools
import math

import jax
import jax.numpy as jnp
from jax import lax
from jax.experimental import pallas as pl
from jax.experimental.pallas import tpu as pltpu
from jax.sharding import PartitionSpec as P

LANES = 128
CHUNKS = 2
MARK_ROWS = 16
OUT_FIRST = 5
BACK_FIRST = 4
GRADIENTS_AFTER = 7
F32 = jnp.float32
BF16 = jnp.bfloat16


def params(mebibytes):
    return pltpu.CompilerParams(vmem_limit_bytes=mebibytes * 1024 * 1024)


def whole_block(*shape):
    return pl.BlockSpec(shape, lambda _: (0,) * len(shape))


def smem():
    return pl.BlockSpec(memory_space=pltpu.SMEM)


def sending_order(peers):
    half = peers // 2
    return [k for i in range(half) for k in (half + i, i)]


def multiply_kernel(chunks, proj_ref, grad_ref, marks_ref, *refs):
    arrived, made, in_sems, out_sems, side_sems = refs[-5:]
    side_ref = refs[-6]
    outs = refs[:-6]
    peers = len(outs) // chunks
    rows = grad_ref.shape[1]
    width = outs[0].shape[1]
    span = peers * width
    me = lax.axis_index("ctx")
    loads, stores = [], []
    for chunk in range(chunks):
        lanes = pl.ds(chunk * span, span)
        for array in range(4):
            source = grad_ref.at[0, :, lanes] if array == 3 else proj_ref.at[0, array, :, lanes]
            loads.append(
                pltpu.make_async_copy(
                    source, arrived.at[array, :, lanes], in_sems.at[chunk, array]
                )
            )
    for load in loads:
        load.start()
    marks = jnp.broadcast_to(marks_ref[...].astype(F32), (MARK_ROWS, LANES)).astype(BF16)
    for chunk in range(chunks):
        for load in loads[4 * chunk : 4 * chunk + 4]:
            load.wait()
        for j, k in enumerate(sending_order(peers)):
            at = chunk * peers + j
            first = pl.multiple_of(chunk * span + (me ^ k) * width, LANES)
            query, key_rows, value, grad_in = [
                arrived[array, :, pl.ds(first, width)].astype(F32) for array in range(4)
            ]
            made[at, :rows, :] = (key_rows * value).astype(BF16)
            made[at, rows : 2 * rows, :] = (grad_in * query).astype(BF16)
            if chunk == 0:
                made[at, 2 * rows :, :LANES] = marks
                if width > LANES:
                    made[at, 2 * rows :, LANES:] = jnp.zeros((MARK_ROWS, width - LANES), BF16)
            source = made.at[at] if chunk == 0 else made.at[at, : 2 * rows]
            stores.append(pltpu.make_async_copy(source, outs[at], out_sems.at[at]))
            stores[-1].start()
        lanes = pl.ds(chunk * span, span)
        for array in range(3):
            stores.append(
                pltpu.make_async_copy(
                    arrived.at[array + 1, :, lanes],
                    side_ref.at[array, :, lanes],
                    side_sems.at[chunk, array],
                )
            )
            stores[-1].start()
    for store in stores:
        store.wait()


def multiply(chunks, width, peers, qkv_proj, cotangent, marks):
    _, rows, channels = cotangent.shape
    anywhere = pl.BlockSpec(memory_space=pl.ANY)
    tall = 2 * rows + MARK_ROWS
    shapes = [(tall if chunk == 0 else 2 * rows, width) for chunk in range(chunks)]
    shapes = [shape for shape in shapes for _ in range(peers)] + [(3, rows, channels)]
    made = pl.pallas_call(
        functools.partial(multiply_kernel, chunks),
        out_shape=[jax.ShapeDtypeStruct(shape, BF16) for shape in shapes],
        in_specs=[anywhere, anywhere, pl.BlockSpec(memory_space=pltpu.VMEM)],
        out_specs=[anywhere] * len(shapes),
        scratch_shapes=[
            pltpu.VMEM((4, rows, channels), BF16),
            pltpu.VMEM((chunks * peers, tall, width), BF16),
            pltpu.SemaphoreType.DMA((chunks, 4)),
            pltpu.SemaphoreType.DMA((chunks * peers,)),
            pltpu.SemaphoreType.DMA((chunks, 3)),
        ],
        compiler_params=params(60),
        cost_estimate=pl.CostEstimate(
            flops=2 * rows * channels, bytes_accessed=18 * rows * channels, transcendentals=0
        ),
        name="multiply",
    )(qkv_proj, cotangent, marks)
    return [list(made[c * peers : (c + 1) * peers]) for c in range(chunks)], made[-1]


def first_row(meta_ref, peers, source, block):
    block_rows = LANES // peers
    row = meta_ref[source * peers + block] * block_rows
    return pl.multiple_of(row, block_rows)


def masks_kernel(me_at, meta_ref, *refs):
    marks_refs, (out_ref, seq, across) = refs[:-3], refs[-3:]
    peers = len(marks_refs)
    tile = LANES
    block_rows = tile // peers
    me = meta_ref[me_at]
    row_ids = lax.broadcasted_iota(jnp.int32, (tile, tile), 0)
    lane_ids = lax.broadcasted_iota(jnp.int32, (tile, tile), 1)
    eye = (row_ids == lane_ids).astype(BF16)
    lower = (row_ids >= lane_ids).astype(BF16)
    for k, marks_ref in zip(sending_order(peers), marks_refs):
        spread = lax.dot_general(
            eye, marks_ref[...], (((1,), (1,)), ((), ())), preferred_element_type=F32
        )
        column = jnp.broadcast_to(spread[:, :1], (tile, tile))
        for block in range(peers):
            first = first_row(meta_ref, peers, me ^ k, block)
            seq[pl.ds(first, block_rows), :] = column[
                block * block_rows : (block + 1) * block_rows
            ]
    carry = jnp.zeros((1, tile), F32)
    for b in range(peers):
        rows = slice(b * tile, (b + 1) * tile)
        count = (
            jnp.dot(lower, seq[rows, :].astype(BF16), preferred_element_type=F32) + carry
        )
        carry = count[tile - 1 :, :]
        seq[rows, :] = count
        across[rows, :] = count.T
    for b in range(peers):
        here = seq[b * tile : (b + 1) * tile, :]

        def same(other):
            return (here == across[other * tile : (other + 1) * tile, :]).astype(F32).astype(BF16)

        out_ref[b, 0, :, :tile] = same(max(b - 1, 0))
        out_ref[b, 0, :, tile:] = same(b)
        out_ref[b, 1, :, :tile] = same(b)
        out_ref[b, 1, :, tile:] = same(min(b + 1, peers - 1))


def document_masks(me_at, meta, received, mark_rows):
    peers = len(received)
    tile = LANES
    last = received[0].shape[0] // mark_rows - 1
    out = (peers, 2, tile, 2 * tile)
    return pl.pallas_call(
        functools.partial(masks_kernel, me_at),
        out_shape=jax.ShapeDtypeStruct(out, BF16),
        in_specs=[smem()] + [pl.BlockSpec((mark_rows, tile), lambda _: (last, 0))] * peers,
        out_specs=whole_block(*out),
        scratch_shapes=[
            pltpu.VMEM((peers * tile, tile), F32),
            pltpu.VMEM((peers * tile, tile), F32),
        ],
        compiler_params=params(24),
        cost_estimate=pl.CostEstimate(
            flops=8 * peers * tile * tile, bytes_accessed=8 * peers * tile * tile, transcendentals=0
        ),
        grid=(1,),
        name="masks",
    )(meta, *received)


def conv_kernel(group_size, me_at, peers, passing, meta_ref, mask_ref, base_ref, *refs):
    rows32, rows16, toep = refs[-3:]
    recv = refs[:peers]
    outs = refs[peers + passing : 2 * peers + passing]
    me = meta_ref[me_at]
    arrivals = [(me ^ k, recv_ref) for k, recv_ref in zip(sending_order(peers), recv)]
    tile = LANES
    width = outs[0].shape[1]
    groups = base_ref.shape[1]
    block_rows = tile // peers
    rows16[0, :tile, :] = jnp.zeros((tile, width), BF16)
    rows16[1, peers * tile :, :] = jnp.zeros((tile, width), BF16)

    for half in range(2):
        for group in range(groups):
            base = jnp.broadcast_to(base_ref[half, group : group + 1, :], (tile, 2 * tile))
            toep[half, group] = pltpu.roll(base, 0, 1, stride=1, stride_axis=0).astype(BF16)

    for source, recv_ref in arrivals:
        firsts = [first_row(meta_ref, peers, source, block) for block in range(peers)]
        for half in range(2):
            arrived = recv_ref[half * tile : (half + 1) * tile, :].astype(F32)
            for block in range(peers):
                rows32[half, pl.ds(firsts[block], block_rows), :] = arrived[
                    block * block_rows : (block + 1) * block_rows
                ]
    rows16[0, tile:, :] = rows32[0].astype(BF16)
    rows16[1, : peers * tile, :] = rows32[1].astype(BF16)

    tile_groups = tile // group_size
    lane_group = lax.broadcasted_iota(jnp.int32, (tile, tile), 1) // group_size

    def one_tile(b, carry):
        first = pl.multiple_of(b * tile, tile)
        for half in range(2):
            mask = mask_ref[b, half]
            for sub in range(width // tile):
                lanes = slice(sub * tile, (sub + 1) * tile)
                window = rows16[half, pl.ds(first, 2 * tile), lanes]
                total = jnp.zeros((tile, tile), F32)
                for group in range(tile_groups):
                    part = jnp.dot(
                        toep[half, sub * tile_groups + group] * mask,
                        window,
                        preferred_element_type=F32,
                    )
                    total = jnp.where(lane_group == group, part, total)
                rows32[half, pl.ds(first, tile), lanes] = total
        return carry

    lax.fori_loop(0, peers, one_tile, 0)

    for k, out_ref in zip(sending_order(peers), outs):
        firsts = [first_row(meta_ref, peers, me ^ k, block) for block in range(peers)]
        for half in range(2):
            pieces = [rows32[half, pl.ds(first, block_rows), :] for first in firsts]
            out_ref[half * tile : (half + 1) * tile, :] = jnp.concatenate(pieces, axis=0).astype(
                BF16
            )


def convolve(group_size, me_at, meta, received, masks, bases, passing):
    peers = masks.shape[0]
    tile = LANES
    width = received[0].shape[-1]
    groups = bases.shape[1]
    out = (2 * tile, width)
    anywhere = [pl.BlockSpec(memory_space=pl.ANY)] * len(passing)
    outs = pl.pallas_call(
        functools.partial(conv_kernel, group_size, me_at, peers, len(passing)),
        out_shape=[jax.ShapeDtypeStruct(out, BF16)] * peers
        + [jax.ShapeDtypeStruct(p.shape, BF16) for p in passing],
        in_specs=[smem(), whole_block(*masks.shape), whole_block(*bases.shape)]
        + [whole_block(*r.shape) for r in received]
        + anywhere,
        out_specs=[whole_block(*out)] * peers + anywhere,
        input_output_aliases={3 + peers + i: peers + i for i in range(len(passing))},
        scratch_shapes=[
            pltpu.VMEM((2, peers * tile, width), F32),
            pltpu.VMEM((2, (peers + 1) * tile, width), BF16),
            pltpu.VMEM((2, groups, tile, 2 * tile), BF16),
        ],
        compiler_params=params(24),
        cost_estimate=pl.CostEstimate(
            flops=8 * groups * peers * tile**3,
            bytes_accessed=8 * peers * tile * width + 4 * peers * tile**2,
            transcendentals=0,
        ),
        grid=(1,),
        name="convolve",
    )(meta, masks, bases, *received, *passing)
    return list(outs[:peers]), list(outs[peers:])


def gradients_kernel(me_at, tp_at, peers, meta_ref, side_ref, *refs):
    result_ref, cross_ref = refs[-2:]
    rows = side_ref.shape[1]
    width = side_ref.shape[2] // peers
    part = cross_ref.shape[1]
    me = meta_ref[me_at]
    mine = meta_ref[tp_at]
    for out_ref, index in ((cross_ref, 1 - mine), (result_ref.at[0], mine)):
        first = pl.multiple_of(index * part, part)
        at = pl.ds(first, part)
        later = pl.ds(pl.multiple_of(first + rows, part), part)
        for k, back_ref in zip(sending_order(peers), refs):
            lanes = pl.ds(pl.multiple_of((me ^ k) * width, LANES), width)
            medium = back_ref[at, :].astype(F32)
            mixed_grad = back_ref[later, :].astype(F32)
            key_rows = side_ref[0, at, lanes].astype(F32)
            value = side_ref[1, at, lanes].astype(F32)
            grad_in = side_ref[2, at, lanes].astype(F32)
            out_ref[0, :, lanes] = (grad_in * medium).astype(BF16)
            out_ref[1, :, lanes] = (mixed_grad * value).astype(BF16)
            out_ref[2, :, lanes] = (mixed_grad * key_rows).astype(BF16)


def fixed(shape):
    return pl.BlockSpec(shape, lambda _, meta_ref: (0,) * len(shape))


def result_block(shape, chunk, chunks, tp_at, mine):
    def place(_, meta_ref):
        owner = meta_ref[tp_at] if mine else 1 - meta_ref[tp_at]
        return (0, 0, 0, owner * chunks + chunk)

    return pl.BlockSpec((1,) + shape, place)


def gradients(chunk, chunks, me_at, tp_at, tp_count, meta, backs, side, others):
    peers = len(backs)
    _, rows, channels = side.shape
    span = channels // chunks
    out = (3, rows // tp_count, span)
    whole = (1, 3, rows // tp_count, channels * tp_count)
    in_specs = [pl.BlockSpec((3, rows, span), lambda _, meta_ref: (0, 0, chunk))]
    in_specs += [fixed(backs[0].shape)] * peers
    args = [meta, side, *backs]
    aliases = {} if chunk == 0 else {len(args): 0}
    for other in others:
        args.append(other)
        in_specs.append(pl.BlockSpec(memory_space=pl.ANY))
    return pl.pallas_call(
        functools.partial(gradients_kernel, me_at, tp_at, peers),
        out_shape=[jax.ShapeDtypeStruct(whole, BF16), jax.ShapeDtypeStruct(out, BF16)],
        grid_spec=pltpu.PrefetchScalarGridSpec(
            num_scalar_prefetch=1,
            grid=(1,),
            in_specs=in_specs,
            out_specs=[result_block(out, chunk, chunks, tp_at, True), fixed(out)],
        ),
        input_output_aliases=aliases,
        compiler_params=params(24),
        cost_estimate=pl.CostEstimate(
            flops=3 * rows * span, bytes_accessed=16 * rows * span, transcendentals=0
        ),
        name="gradients",
    )(*args)


def place_kernel(meta_ref, cross_ref, held_ref, result_ref):
    result_ref[0] = cross_ref[...]


def place(chunk, chunks, tp_at, meta, cross, result):
    return pl.pallas_call(
        place_kernel,
        out_shape=jax.ShapeDtypeStruct(result.shape, BF16),
        grid_spec=pltpu.PrefetchScalarGridSpec(
            num_scalar_prefetch=1,
            grid=(1,),
            in_specs=[fixed(cross.shape), pl.BlockSpec(memory_space=pl.ANY)],
            out_specs=result_block(cross.shape, chunk, chunks, tp_at, False),
        ),
        input_output_aliases={2: 0},
        compiler_params=params(24),
        cost_estimate=pl.CostEstimate(
            flops=0, bytes_accessed=4 * math.prod(cross.shape), transcendentals=0
        ),
        name="place",
    )(meta, cross, result)


def swap(array, k):
    peers = lax.axis_size("ctx")
    return lax.ppermute(array, "ctx", [(i, i ^ k) for i in range(peers)]) if k else array


def swap_to_previous(array, k):
    peers = lax.axis_size("ctx")
    pipes = lax.axis_size("pipe")
    pairs = [
        (pipe * peers + i, (pipe - 1) % pipes * peers + (i ^ k))
        for pipe in range(pipes)
        for i in range(peers)
    ]
    return lax.ppermute(array, ("pipe", "ctx"), pairs)


def shards(qkv_proj, cotangent, block_dest, doc_start, mr_filter):
    peers = lax.axis_size("ctx")
    pipes = lax.axis_size("pipe")
    tp_count = lax.axis_size("tp")
    channels = cotangent.shape[2]
    group_count, taps = mr_filter.shape[1:]
    group_size = channels // group_count
    units = channels // (peers * LANES)
    chunks = math.gcd(units, CHUNKS)
    width = channels // (peers * chunks)
    chunk_groups = width // group_size

    dest = lax.dynamic_index_in_dim(block_dest, lax.axis_index("pipe"), 0, keepdims=False)
    me_at = dest.shape[0]
    tp_at = me_at + 1
    here = [lax.axis_index("ctx"), lax.axis_index("tp")]
    meta = jnp.concatenate([dest, jnp.stack(here).astype(jnp.int32)])

    filt = lax.dynamic_index_in_dim(
        mr_filter[0].astype(F32).reshape(chunks, peers, chunk_groups, taps),
        lax.axis_index("ctx"),
        1,
        keepdims=False,
    )
    causal = jnp.pad(filt[:, :, ::-1], ((0, 0), (0, 0), (1, taps - 1)))
    anti = jnp.pad(filt, ((0, 0), (0, 0), (0, taps)))
    bases = jnp.stack([causal, anti], axis=1)

    to_previous = [(pipe, (pipe - 1) % pipes) for pipe in range(pipes)]
    order = sending_order(peers)
    products, side = multiply(chunks, width, peers, qkv_proj, cotangent, doc_start)
    received = [swap(array, k) for array, k in zip(products[0], order)]
    side = lax.ppermute(side, "pipe", to_previous)

    first_out, first_back = OUT_FIRST * peers // 8, BACK_FIRST * peers // 8
    masks = document_masks(me_at, meta, received, MARK_ROWS)
    backs, late = [], []
    for chunk in range(chunks):
        coming = products[chunk + 1] if chunk + 1 < chunks else []
        waiting = coming[first_out:]
        convolved, passed = convolve(
            group_size, me_at, meta, received, masks, bases[chunk], waiting + late
        )
        received = [
            swap(array, k)
            for array, k in zip(coming[:first_out] + passed[: len(waiting)], order)
        ]
        if chunk:
            backs[-1] += [
                swap_to_previous(array, k)
                for array, k in zip(passed[len(waiting) :], order[first_back:])
            ]
        now = first_back if coming else peers
        backs.append([swap_to_previous(array, k) for array, k in zip(convolved[:now], order)])
        late = convolved[now:]

    result = None
    for chunk in range(chunks):
        others = [result] if chunk else backs[1][:GRADIENTS_AFTER] if chunks > 1 else []
        result, cross = gradients(
            chunk, chunks, me_at, tp_at, tp_count, meta, backs[chunk], side, others
        )
        cross = lax.ppermute(cross, "tp", [(0, 1), (1, 0)])
        result = place(chunk, chunks, tp_at, meta, cross, result)
    return result


def solution(mesh):
    placed = (
        P("pipe", None, "ctx", "tp"),
        P("pipe", "ctx", "tp"),
        P(),
        P("pipe", "ctx"),
        P("pipe", "tp", None),
    )
    return jax.shard_map(
        shards,
        mesh=mesh,
        in_specs=placed,
        out_specs=P("pipe", None, ("ctx", "tp"), None),
        check_vma=False,
    )
```

```python
import functools
import math

import jax
import jax.numpy as jnp
from jax import lax
from jax.experimental import pallas as pl
from jax.experimental.pallas import tpu as pltpu
from jax.sharding import PartitionSpec as P

LANES = 128
MARK_ROWS = 16
OUT_FIRST = 5
BACK_FIRST = 5
QUERY_AFTER = 3
F32 = jnp.float32
BF16 = jnp.bfloat16


def params(mebibytes):
    return pltpu.CompilerParams(vmem_limit_bytes=mebibytes * 1024 * 1024)


def cost(flops, moved):
    return pl.CostEstimate(flops=flops, bytes_accessed=moved, transcendentals=0)


def whole_block(*shape):
    return pl.BlockSpec(shape, lambda *_: (0,) * len(shape))


def smem():
    return pl.BlockSpec(memory_space=pltpu.SMEM)


def anywhere():
    return pl.BlockSpec(memory_space=pl.ANY)


def in_hbm():
    return pl.BlockSpec(memory_space=pltpu.HBM)


def bf16(shape):
    return jax.ShapeDtypeStruct(shape, BF16)


def sending_order(peers):
    half = peers // 2
    return [k for i in range(half) for k in (half + i, i)]


def multiply_kernel(peers, proj_ref, grad_ref, marks_ref, *refs):
    outs, side_ref = refs[: 2 * peers], refs[2 * peers]
    arrived, made, in_sems, out_sems, side_sems = refs[-5:]
    rows = grad_ref.shape[1]
    width = outs[0].shape[1]
    me = lax.axis_index("ctx")
    sources = [proj_ref.at[0, 1], proj_ref.at[0, 2], proj_ref.at[0, 0], grad_ref.at[0]]
    loads = [
        pltpu.make_async_copy(source, arrived.at[i], in_sems.at[i])
        for i, source in enumerate(sources)
    ]
    for load in loads:
        load.start()
    marks = jnp.broadcast_to(marks_ref[...].astype(F32), (MARK_ROWS, LANES)).astype(BF16)
    stores = []
    for half in range(2):
        loads[2 * half].wait()
        loads[2 * half + 1].wait()
        for j, k in enumerate(sending_order(peers)):
            at = half * peers + j
            lanes = pl.ds(pl.multiple_of((me ^ k) * width, LANES), width)
            one = arrived[2 * half, :, lanes].astype(F32)
            other = arrived[2 * half + 1, :, lanes].astype(F32)
            made[at, :rows, :] = (one * other).astype(BF16)
            if half == 0:
                made[at, rows:, :LANES] = marks
                made[at, rows:, LANES:] = jnp.zeros((MARK_ROWS, width - LANES), BF16)
            source = made.at[at] if half == 0 else made.at[at, :rows]
            stores.append(pltpu.make_async_copy(source, outs[at], out_sems.at[at]))
            stores[-1].start()
        if half == 0:
            for i in range(2):
                stores.append(
                    pltpu.make_async_copy(arrived.at[i], side_ref.at[i], side_sems.at[i])
                )
                stores[-1].start()
    for store in stores:
        store.wait()


def multiply(peers, qkv_proj, cotangent, marks):
    _, rows, channels = cotangent.shape
    width = channels // peers
    tall = rows + MARK_ROWS
    shapes = [(tall, width)] * peers + [(rows, width)] * peers + [(2, rows, channels)]
    made = pl.pallas_call(
        functools.partial(multiply_kernel, peers),
        out_shape=[bf16(shape) for shape in shapes],
        in_specs=[anywhere(), anywhere(), pl.BlockSpec(memory_space=pltpu.VMEM)],
        out_specs=[anywhere()] * len(shapes),
        scratch_shapes=[
            pltpu.VMEM((4, rows, channels), BF16),
            pltpu.VMEM((2 * peers, tall, width), BF16),
            pltpu.SemaphoreType.DMA((4,)),
            pltpu.SemaphoreType.DMA((2 * peers,)),
            pltpu.SemaphoreType.DMA((2,)),
        ],
        compiler_params=params(60),
        cost_estimate=cost(2 * rows * channels, 16 * rows * channels),
        name="multiply",
    )(qkv_proj, cotangent, marks)
    return list(made[:peers]), list(made[peers : 2 * peers]), made[-1]


def first_row(meta_ref, peers, source, block):
    block_rows = LANES // peers
    row = meta_ref[source * peers + block] * block_rows
    return pl.multiple_of(row, block_rows)


def masks_kernel(me_at, meta_ref, *refs):
    marks_refs, (before_ref, after_ref, seq, across) = refs[:-4], refs[-4:]
    peers = len(marks_refs)
    tile = LANES
    block_rows = tile // peers
    me = meta_ref[me_at]
    row_ids = lax.broadcasted_iota(jnp.int32, (tile, tile), 0)
    lane_ids = lax.broadcasted_iota(jnp.int32, (tile, tile), 1)
    eye = (row_ids == lane_ids).astype(BF16)
    lower = (row_ids >= lane_ids).astype(BF16)
    for k, marks_ref in zip(sending_order(peers), marks_refs):
        spread = lax.dot_general(
            eye, marks_ref[...], (((1,), (1,)), ((), ())), preferred_element_type=F32
        )
        column = jnp.broadcast_to(spread[:, :1], (tile, tile))
        for block in range(peers):
            first = first_row(meta_ref, peers, me ^ k, block)
            seq[pl.ds(first, block_rows), :] = column[
                block * block_rows : (block + 1) * block_rows
            ]
    carry = jnp.zeros((1, tile), F32)
    for b in range(peers):
        rows = slice(b * tile, (b + 1) * tile)
        count = (
            jnp.dot(lower, seq[rows, :].astype(BF16), preferred_element_type=F32) + carry
        )
        carry = count[tile - 1 :, :]
        seq[rows, :] = count
        across[rows, :] = count.T
    for b in range(peers):
        here = seq[b * tile : (b + 1) * tile, :]

        def same(other):
            return (here == across[other * tile : (other + 1) * tile, :]).astype(F32).astype(BF16)

        before_ref[b, :, :tile] = same(max(b - 1, 0))
        before_ref[b, :, tile:] = same(b)
        after_ref[b, :, :tile] = same(b)
        after_ref[b, :, tile:] = same(min(b + 1, peers - 1))


def document_masks(me_at, meta, received):
    peers = len(received)
    tile = LANES
    last = received[0].shape[0] // MARK_ROWS - 1
    out = (peers, tile, 2 * tile)
    return pl.pallas_call(
        functools.partial(masks_kernel, me_at),
        out_shape=[bf16(out)] * 2,
        in_specs=[smem()] + [pl.BlockSpec((MARK_ROWS, tile), lambda _: (last, 0))] * peers,
        out_specs=[whole_block(*out)] * 2,
        scratch_shapes=[
            pltpu.VMEM((peers * tile, tile), F32),
            pltpu.VMEM((peers * tile, tile), F32),
        ],
        compiler_params=params(24),
        cost_estimate=cost(8 * peers * tile * tile, 8 * peers * tile * tile),
        grid=(1,),
        name="masks",
    )(meta, *received)


def conv_kernel(group_size, me_at, causal, passing, meta_ref, mask_ref, base_ref, *refs):
    rows32, rows16, toep = refs[-3:]
    peers = mask_ref.shape[0]
    recv = refs[:peers]
    outs = refs[peers + passing : 2 * peers + passing]
    tile = LANES
    width = outs[0].shape[1]
    groups = base_ref.shape[0]
    block_rows = tile // peers
    me = meta_ref[me_at]
    length = peers * tile
    pad, begin = (0, tile) if causal else (length, 0)
    rows16[pad : pad + tile, :] = jnp.zeros((tile, width), BF16)

    for group in range(groups):
        base = jnp.broadcast_to(base_ref[group : group + 1, :], (tile, 2 * tile))
        toep[group] = pltpu.roll(base, 0, 1, stride=1, stride_axis=0).astype(BF16)

    for k, recv_ref in zip(sending_order(peers), recv):
        arrived = recv_ref[:tile, :].astype(F32)
        for block in range(peers):
            first = first_row(meta_ref, peers, me ^ k, block)
            rows32[pl.ds(first, block_rows), :] = arrived[
                block * block_rows : (block + 1) * block_rows
            ]
    rows16[begin : begin + length, :] = rows32[...].astype(BF16)

    tile_groups = tile // group_size
    lane_group = lax.broadcasted_iota(jnp.int32, (tile, tile), 1) // group_size

    def one_tile(b, carry):
        first = pl.multiple_of(b * tile, tile)
        mask = mask_ref[b]
        for sub in range(width // tile):
            lanes = slice(sub * tile, (sub + 1) * tile)
            window = rows16[pl.ds(first, 2 * tile), lanes]
            total = jnp.zeros((tile, tile), F32)
            for group in range(tile_groups):
                part = jnp.dot(
                    toep[sub * tile_groups + group] * mask, window, preferred_element_type=F32
                )
                total = jnp.where(lane_group == group, part, total)
            rows32[pl.ds(first, tile), lanes] = total
        return carry

    lax.fori_loop(0, peers, one_tile, 0)

    for k, out_ref in zip(sending_order(peers), outs):
        pieces = [
            rows32[pl.ds(first_row(meta_ref, peers, me ^ k, block), block_rows), :]
            for block in range(peers)
        ]
        out_ref[...] = jnp.concatenate(pieces, axis=0).astype(BF16)


def convolve(group_size, me_at, causal, meta, received, masks, bases, passing):
    peers = masks.shape[0]
    tile = LANES
    width = received[0].shape[1]
    groups = bases.shape[0]
    out = (tile, width)
    held = [in_hbm()] * len(passing)
    outs = pl.pallas_call(
        functools.partial(conv_kernel, group_size, me_at, causal, len(passing)),
        out_shape=[bf16(out)] * peers + [bf16(p.shape) for p in passing],
        in_specs=[smem(), whole_block(*masks.shape), whole_block(*bases.shape)]
        + [whole_block(*r.shape) for r in received]
        + held,
        out_specs=[whole_block(*out)] * peers + held,
        input_output_aliases={3 + peers + i: peers + i for i in range(len(passing))},
        scratch_shapes=[
            pltpu.VMEM((peers * tile, width), F32),
            pltpu.VMEM(((peers + 1) * tile, width), BF16),
            pltpu.VMEM((groups, tile, 2 * tile), BF16),
        ],
        compiler_params=params(24),
        cost_estimate=cost(
            4 * groups * peers * tile**3, 4 * peers * tile * width + 4 * peers * tile**2
        ),
        grid=(1,),
        name="convolve",
    )(meta, masks, bases, *received, *passing)
    return list(outs[:peers]), list(outs[peers:])


def query_gradient_kernel(me_at, tp_at, peers, meta_ref, grad_ref, *refs):
    keep_ref, cross_ref = refs[-2:]
    width = grad_ref.shape[2] // peers
    part = keep_ref.shape[0]
    me = meta_ref[me_at]
    mine = meta_ref[tp_at]
    for out_ref, index in ((cross_ref, 1 - mine), (keep_ref, mine)):
        at = pl.ds(pl.multiple_of(index * part, part), part)
        for k, back_ref in zip(sending_order(peers), refs):
            lanes = pl.ds(pl.multiple_of((me ^ k) * width, LANES), width)
            medium = back_ref[at, :].astype(F32)
            grad_in = grad_ref[0, at, lanes].astype(F32)
            out_ref[:, lanes] = (grad_in * medium).astype(BF16)


def query_gradient(me_at, tp_at, tp_count, meta, backs, cotangent, others):
    peers = len(backs)
    _, rows, channels = cotangent.shape
    out = (rows // tp_count, channels)
    return pl.pallas_call(
        functools.partial(query_gradient_kernel, me_at, tp_at, peers),
        out_shape=[bf16(out)] * 2,
        grid_spec=pltpu.PrefetchScalarGridSpec(
            num_scalar_prefetch=1,
            grid=(1,),
            in_specs=[whole_block(*cotangent.shape)]
            + [whole_block(*b.shape) for b in backs]
            + [anywhere() for _ in others],
            out_specs=[whole_block(*out)] * 2,
        ),
        compiler_params=params(24),
        cost_estimate=cost(rows * channels, 6 * rows * channels),
        name="query_gradient",
    )(meta, cotangent, *backs, *others)


def place_query_kernel(tp_at, meta_ref, keep_ref, cross_ref, held_ref, result_ref):
    mine = meta_ref[tp_at]
    width = keep_ref.shape[1]
    for piece, index in ((keep_ref, mine), (cross_ref, 1 - mine)):
        result_ref[0, 0, :, pl.ds(pl.multiple_of(index * width, LANES), width)] = piece[...]


def place_query(tp_at, meta, keep, cross, result):
    part, channels = keep.shape
    whole = result.shape
    return pl.pallas_call(
        functools.partial(place_query_kernel, tp_at),
        out_shape=bf16(whole),
        grid_spec=pltpu.PrefetchScalarGridSpec(
            num_scalar_prefetch=1,
            grid=(1,),
            in_specs=[whole_block(*keep.shape), whole_block(*cross.shape), anywhere()],
            out_specs=pl.BlockSpec((1, 1) + whole[2:], lambda *_: (0, 0, 0, 0)),
        ),
        input_output_aliases={3: 0},
        compiler_params=params(24),
        cost_estimate=cost(0, 8 * part * channels),
        name="place_query",
    )(meta, keep, cross, result)


def key_value_gradients_kernel(me_at, tp_at, peers, meta_ref, side_ref, *refs):
    result_ref, cross_ref = refs[-2:]
    width = side_ref.shape[2] // peers
    part = cross_ref.shape[1]
    me = meta_ref[me_at]
    mine = meta_ref[tp_at]
    for out_ref, index in ((cross_ref.at[0], 1 - mine), (result_ref.at[0, 0], mine)):
        at = pl.ds(pl.multiple_of(index * part, part), part)
        for k, back_ref in zip(sending_order(peers), refs):
            lanes = pl.ds(pl.multiple_of((me ^ k) * width, LANES), width)
            mixed_grad = back_ref[at, :].astype(F32)
            factor = side_ref[0, at, lanes].astype(F32)
            out_ref[:, lanes] = (mixed_grad * factor).astype(BF16)


def key_value_gradients(me_at, tp_at, tp_count, meta, backs, side):
    peers = len(backs)
    _, rows, channels = side.shape
    part = rows // tp_count
    return pl.pallas_call(
        functools.partial(key_value_gradients_kernel, me_at, tp_at, peers),
        out_shape=[bf16((1, 3, part, channels * tp_count)), bf16((2, part, channels))],
        grid_spec=pltpu.PrefetchScalarGridSpec(
            num_scalar_prefetch=1,
            grid=(2,),
            in_specs=[pl.BlockSpec((1, rows, channels), lambda i, _: (1 - i, 0, 0))]
            + [whole_block(*b.shape) for b in backs],
            out_specs=[
                pl.BlockSpec((1, 1, part, channels), lambda i, meta_ref: (0, 1 + i, 0, meta_ref[tp_at])),
                pl.BlockSpec((1, part, channels), lambda i, _: (i, 0, 0)),
            ],
        ),
        compiler_params=params(24),
        cost_estimate=cost(2 * rows * channels, 10 * rows * channels),
        name="key_value_gradients",
    )(meta, side, *backs)


def place_crossed_kernel(meta_ref, cross_ref, held_ref, result_ref):
    result_ref[0, 0] = cross_ref[0]


def place_crossed(tp_at, meta, cross, result):
    _, part, channels = cross.shape
    return pl.pallas_call(
        place_crossed_kernel,
        out_shape=bf16(result.shape),
        grid_spec=pltpu.PrefetchScalarGridSpec(
            num_scalar_prefetch=1,
            grid=(2,),
            in_specs=[pl.BlockSpec((1, part, channels), lambda i, _: (i, 0, 0)), anywhere()],
            out_specs=pl.BlockSpec(
                (1, 1, part, channels), lambda i, meta_ref: (0, 1 + i, 0, 1 - meta_ref[tp_at])
            ),
        ),
        input_output_aliases={2: 0},
        compiler_params=params(24),
        cost_estimate=cost(0, 4 * math.prod(cross.shape)),
        name="place_crossed",
    )(meta, cross, result)


def swap(array, k):
    peers = lax.axis_size("ctx")
    return lax.ppermute(array, "ctx", [(i, i ^ k) for i in range(peers)]) if k else array


def swap_to_previous(array, k):
    peers = lax.axis_size("ctx")
    pipes = lax.axis_size("pipe")
    pairs = [
        (pipe * peers + i, (pipe - 1) % pipes * peers + (i ^ k))
        for pipe in range(pipes)
        for i in range(peers)
    ]
    return lax.ppermute(array, ("pipe", "ctx"), pairs)


def shards(qkv_proj, cotangent, block_dest, doc_start, mr_filter):
    peers = lax.axis_size("ctx")
    pipes = lax.axis_size("pipe")
    tp_count = lax.axis_size("tp")
    channels = cotangent.shape[2]
    group_count, taps = mr_filter.shape[1:]
    group_size = channels // group_count

    dest = lax.dynamic_index_in_dim(block_dest, lax.axis_index("pipe"), 0, keepdims=False)
    me_at = dest.shape[0]
    tp_at = me_at + 1
    here = [lax.axis_index("ctx"), lax.axis_index("tp")]
    meta = jnp.concatenate([dest, jnp.stack(here).astype(jnp.int32)])

    filt = lax.dynamic_index_in_dim(
        mr_filter[0].astype(F32).reshape(peers, group_count // peers, taps),
        lax.axis_index("ctx"),
        0,
        keepdims=False,
    )
    base_before = jnp.pad(filt[:, ::-1], ((0, 0), (1, taps - 1)))
    base_after = jnp.pad(filt, ((0, 0), (0, taps)))

    to_previous = [(pipe, (pipe - 1) % pipes) for pipe in range(pipes)]
    straight = [
        (pipe * tp_count + tp, target * tp_count + tp)
        for pipe, target in to_previous
        for tp in range(tp_count)
    ]
    crossed = [(source, target ^ 1) for source, target in straight]
    order = sending_order(peers)
    first_out, first_back = OUT_FIRST * peers // 8, BACK_FIRST * peers // 8

    mixed, gated, side = multiply(peers, qkv_proj, cotangent, doc_start)
    received = [swap(array, k) for array, k in zip(mixed, order)]
    side = lax.ppermute(side, "pipe", to_previous)
    mask_before, mask_after = document_masks(me_at, meta, received)

    medium, late = convolve(
        group_size, me_at, True, meta, received, mask_before, base_before, gated[first_out:]
    )
    received = [swap(array, k) for array, k in zip(gated[:first_out] + late, order)]
    mixed_grad, late = convolve(
        group_size, me_at, False, meta, received, mask_after, base_after, medium[first_back:]
    )
    medium = [swap(array, k) for array, k in zip(medium[:first_back] + late, order)]
    mixed_grad = [swap_to_previous(array, k) for array, k in zip(mixed_grad, order)]

    keep, cross = query_gradient(
        me_at, tp_at, tp_count, meta, medium, cotangent, mixed_grad[:QUERY_AFTER] + [side]
    )
    keep = lax.ppermute(keep, ("pipe", "tp"), straight)
    cross = lax.ppermute(cross, ("pipe", "tp"), crossed)
    result, other = key_value_gradients(me_at, tp_at, tp_count, meta, mixed_grad, side)
    other = lax.ppermute(other, "tp", [(0, 1), (1, 0)])
    result = place_query(tp_at, meta, keep, cross, result)
    return place_crossed(tp_at, meta, other, result)


def solution(mesh):
    placed = (
        P("pipe", None, "ctx", "tp"),
        P("pipe", "ctx", "tp"),
        P(),
        P("pipe", "ctx"),
        P("pipe", "tp", None),
    )
    return jax.shard_map(
        shards,
        mesh=mesh,
        in_specs=placed,
        out_specs=P("pipe", None, ("ctx", "tp"), None),
        check_vma=False,
    )
```

```python
import functools
import math

import jax
import jax.numpy as jnp
from jax import lax
from jax.experimental import pallas as pl
from jax.experimental.pallas import tpu as pltpu
from jax.sharding import PartitionSpec as P

LANES = 128
MARK_ROWS = 16
OUT_FIRST = 5
BACK_FIRST = 5
QUERY_AFTER = 4
F32 = jnp.float32
BF16 = jnp.bfloat16


def params(mebibytes):
    return pltpu.CompilerParams(vmem_limit_bytes=mebibytes * 1024 * 1024)


def cost(flops, moved):
    return pl.CostEstimate(flops=flops, bytes_accessed=moved, transcendentals=0)


def whole_block(*shape):
    return pl.BlockSpec(shape, lambda *_: (0,) * len(shape))


def smem():
    return pl.BlockSpec(memory_space=pltpu.SMEM)


def anywhere():
    return pl.BlockSpec(memory_space=pl.ANY)


def bf16(shape):
    return jax.ShapeDtypeStruct(shape, BF16)


def sending_order(peers):
    half = peers // 2
    return [k for i in range(half) for k in (i, half + i)]


def multiply_kernel(peers, proj_ref, grad_ref, marks_ref, *refs):
    outs, side_ref = refs[: 2 * peers], refs[2 * peers]
    arrived, made, in_sems, out_sems, side_sems = refs[-5:]
    rows = grad_ref.shape[1]
    width = outs[0].shape[1]
    me = lax.axis_index("ctx")
    sources = [proj_ref.at[0, 1], proj_ref.at[0, 2], proj_ref.at[0, 0], grad_ref.at[0]]
    loads = [
        pltpu.make_async_copy(source, arrived.at[i], in_sems.at[i])
        for i, source in enumerate(sources)
    ]
    for load in loads:
        load.start()
    marks = jnp.broadcast_to(marks_ref[...].astype(F32), (MARK_ROWS, LANES)).astype(BF16)
    stores = []
    for half in range(2):
        loads[2 * half].wait()
        loads[2 * half + 1].wait()
        for j, k in enumerate(sending_order(peers)):
            at = half * peers + j
            lanes = pl.ds(pl.multiple_of((me ^ k) * width, LANES), width)
            one = arrived[2 * half, :, lanes].astype(F32)
            other = arrived[2 * half + 1, :, lanes].astype(F32)
            made[at, :rows, :] = (one * other).astype(BF16)
            if half == 0:
                made[at, rows:, :LANES] = marks
                made[at, rows:, LANES:] = jnp.zeros((MARK_ROWS, width - LANES), BF16)
            source = made.at[at] if half == 0 else made.at[at, :rows]
            stores.append(pltpu.make_async_copy(source, outs[at], out_sems.at[at]))
            stores[-1].start()
        if half == 0:
            for i in range(2):
                stores.append(
                    pltpu.make_async_copy(arrived.at[i], side_ref.at[i], side_sems.at[i])
                )
                stores[-1].start()
    for store in stores:
        store.wait()


def multiply(peers, qkv_proj, cotangent, marks):
    _, rows, channels = cotangent.shape
    width = channels // peers
    tall = rows + MARK_ROWS
    shapes = [(tall, width)] * peers + [(rows, width)] * peers + [(2, rows, channels)]
    made = pl.pallas_call(
        functools.partial(multiply_kernel, peers),
        out_shape=[bf16(shape) for shape in shapes],
        in_specs=[anywhere(), anywhere(), pl.BlockSpec(memory_space=pltpu.VMEM)],
        out_specs=[anywhere()] * len(shapes),
        scratch_shapes=[
            pltpu.VMEM((4, rows, channels), BF16),
            pltpu.VMEM((2 * peers, tall, width), BF16),
            pltpu.SemaphoreType.DMA((4,)),
            pltpu.SemaphoreType.DMA((2 * peers,)),
            pltpu.SemaphoreType.DMA((2,)),
        ],
        compiler_params=params(60),
        cost_estimate=cost(2 * rows * channels, 16 * rows * channels),
        name="multiply",
    )(qkv_proj, cotangent, marks)
    return list(made[:peers]), list(made[peers : 2 * peers]), made[-1]


def first_row(meta_ref, peers, source, block):
    block_rows = LANES // peers
    row = meta_ref[source * peers + block] * block_rows
    return pl.multiple_of(row, block_rows)


def masks_kernel(me_at, meta_ref, *refs):
    marks_refs, (before_ref, after_ref, seq, across) = refs[:-4], refs[-4:]
    peers = len(marks_refs)
    tile = LANES
    block_rows = tile // peers
    me = meta_ref[me_at]
    row_ids = lax.broadcasted_iota(jnp.int32, (tile, tile), 0)
    lane_ids = lax.broadcasted_iota(jnp.int32, (tile, tile), 1)
    eye = (row_ids == lane_ids).astype(BF16)
    lower = (row_ids >= lane_ids).astype(BF16)
    for k, marks_ref in zip(sending_order(peers), marks_refs):
        spread = lax.dot_general(
            eye, marks_ref[...], (((1,), (1,)), ((), ())), preferred_element_type=F32
        )
        column = jnp.broadcast_to(spread[:, :1], (tile, tile))
        for block in range(peers):
            first = first_row(meta_ref, peers, me ^ k, block)
            seq[pl.ds(first, block_rows), :] = column[
                block * block_rows : (block + 1) * block_rows
            ]
    carry = jnp.zeros((1, tile), F32)
    for b in range(peers):
        rows = slice(b * tile, (b + 1) * tile)
        count = (
            jnp.dot(lower, seq[rows, :].astype(BF16), preferred_element_type=F32) + carry
        )
        carry = count[tile - 1 :, :]
        seq[rows, :] = count
        across[rows, :] = count.T
    for b in range(peers):
        here = seq[b * tile : (b + 1) * tile, :]

        def same(other):
            return (here == across[other * tile : (other + 1) * tile, :]).astype(F32).astype(BF16)

        before_ref[b, :, :tile] = same(max(b - 1, 0))
        before_ref[b, :, tile:] = same(b)
        after_ref[b, :, :tile] = same(b)
        after_ref[b, :, tile:] = same(min(b + 1, peers - 1))


def document_masks(me_at, meta, received):
    peers = len(received)
    tile = LANES
    last = received[0].shape[0] // MARK_ROWS - 1
    out = (peers, tile, 2 * tile)
    return pl.pallas_call(
        functools.partial(masks_kernel, me_at),
        out_shape=[bf16(out)] * 2,
        in_specs=[smem()] + [pl.BlockSpec((MARK_ROWS, tile), lambda _: (last, 0))] * peers,
        out_specs=[whole_block(*out)] * 2,
        scratch_shapes=[
            pltpu.VMEM((peers * tile, tile), F32),
            pltpu.VMEM((peers * tile, tile), F32),
        ],
        compiler_params=params(24),
        cost_estimate=cost(8 * peers * tile * tile, 8 * peers * tile * tile),
        grid=(1,),
        name="masks",
    )(meta, *received)


def conv_kernel(group_size, me_at, causal, meta_ref, mask_ref, base_ref, *refs):
    rows32, rows16, toep = refs[-3:]
    peers = mask_ref.shape[0]
    recv = refs[:peers]
    outs = refs[peers : 2 * peers]
    tile = LANES
    width = outs[0].shape[1]
    groups = base_ref.shape[0]
    block_rows = tile // peers
    me = meta_ref[me_at]
    length = peers * tile
    pad, begin = (0, tile) if causal else (length, 0)
    rows16[pad : pad + tile, :] = jnp.zeros((tile, width), BF16)

    for group in range(groups):
        base = jnp.broadcast_to(base_ref[group : group + 1, :], (tile, 2 * tile))
        toep[group] = pltpu.roll(base, 0, 1, stride=1, stride_axis=0).astype(BF16)

    for k, recv_ref in zip(sending_order(peers), recv):
        arrived = recv_ref[:tile, :].astype(F32)
        for block in range(peers):
            first = first_row(meta_ref, peers, me ^ k, block)
            rows32[pl.ds(first, block_rows), :] = arrived[
                block * block_rows : (block + 1) * block_rows
            ]
    rows16[begin : begin + length, :] = rows32[...].astype(BF16)

    tile_groups = tile // group_size
    lane_group = lax.broadcasted_iota(jnp.int32, (tile, tile), 1) // group_size

    def one_tile(b, carry):
        first = pl.multiple_of(b * tile, tile)
        mask = mask_ref[b]
        for sub in range(width // tile):
            lanes = slice(sub * tile, (sub + 1) * tile)
            window = rows16[pl.ds(first, 2 * tile), lanes]
            total = jnp.zeros((tile, tile), F32)
            for group in range(tile_groups):
                part = jnp.dot(
                    toep[sub * tile_groups + group] * mask, window, preferred_element_type=F32
                )
                total = jnp.where(lane_group == group, part, total)
            rows32[pl.ds(first, tile), lanes] = total
        return carry

    lax.fori_loop(0, peers, one_tile, 0)

    for k, out_ref in zip(sending_order(peers), outs):
        pieces = [
            rows32[pl.ds(first_row(meta_ref, peers, me ^ k, block), block_rows), :]
            for block in range(peers)
        ]
        out_ref[...] = jnp.concatenate(pieces, axis=0).astype(BF16)


def convolve(group_size, me_at, causal, meta, received, masks, bases):
    peers = masks.shape[0]
    tile = LANES
    width = received[0].shape[1]
    groups = bases.shape[0]
    out = (tile, width)
    outs = pl.pallas_call(
        functools.partial(conv_kernel, group_size, me_at, causal),
        out_shape=[bf16(out)] * peers,
        in_specs=[smem(), whole_block(*masks.shape), whole_block(*bases.shape)]
        + [whole_block(*r.shape) for r in received],
        out_specs=[whole_block(*out)] * peers,
        scratch_shapes=[
            pltpu.VMEM((peers * tile, width), F32),
            pltpu.VMEM(((peers + 1) * tile, width), BF16),
            pltpu.VMEM((groups, tile, 2 * tile), BF16),
        ],
        compiler_params=params(24),
        cost_estimate=cost(
            4 * groups * peers * tile**3, 4 * peers * tile * width + 4 * peers * tile**2
        ),
        grid=(1,),
        name="convolve",
    )(meta, masks, bases, *received)
    return list(outs)


def query_gradient_kernel(me_at, peers, meta_ref, grad_ref, *refs):
    out_ref = refs[-1]
    width = grad_ref.shape[2] // peers
    me = meta_ref[me_at]
    for k, back_ref in zip(sending_order(peers), refs):
        lanes = pl.ds(pl.multiple_of((me ^ k) * width, LANES), width)
        medium = back_ref[...].astype(F32)
        out_ref[:, lanes] = (grad_ref[0, :, lanes].astype(F32) * medium).astype(BF16)


def query_gradient(me_at, meta, backs, cotangent, others):
    peers = len(backs)
    _, rows, channels = cotangent.shape
    return pl.pallas_call(
        functools.partial(query_gradient_kernel, me_at, peers),
        out_shape=bf16((rows, channels)),
        in_specs=[smem(), whole_block(*cotangent.shape)]
        + [whole_block(*b.shape) for b in backs]
        + [anywhere() for _ in others],
        out_specs=whole_block(rows, channels),
        grid=(1,),
        compiler_params=params(24),
        cost_estimate=cost(rows * channels, 6 * rows * channels),
        name="query_gradient",
    )(meta, cotangent, *backs, *others)


def gradients_kernel(me_at, tp_at, peers, meta_ref, query_ref, side_ref, *refs):
    result_ref, cross_ref = refs[-2:]
    width = side_ref.shape[2] // peers
    part = cross_ref.shape[1]
    me = meta_ref[me_at]
    mine = meta_ref[tp_at]
    step = pl.program_id(0)
    for out_ref, index in ((cross_ref.at[0], 1 - mine), (result_ref.at[0, 0], mine)):
        at = pl.ds(pl.multiple_of(index * part, part), part)

        @pl.when(step == 0)
        def _():
            out_ref[...] = query_ref[at, :]

        @pl.when(step > 0)
        def _():
            for k, back_ref in zip(sending_order(peers), refs):
                lanes = pl.ds(pl.multiple_of((me ^ k) * width, LANES), width)
                mixed_grad = back_ref[at, :].astype(F32)
                factor = side_ref[0, at, lanes].astype(F32)
                out_ref[:, lanes] = (mixed_grad * factor).astype(BF16)


def gradients(me_at, tp_at, tp_count, meta, query, side, backs):
    peers = len(backs)
    _, rows, channels = side.shape
    part = rows // tp_count

    def mine(i, meta_ref):
        return (0, i, 0, meta_ref[tp_at])

    return pl.pallas_call(
        functools.partial(gradients_kernel, me_at, tp_at, peers),
        out_shape=[bf16((1, 3, part, channels * tp_count)), bf16((3, part, channels))],
        grid_spec=pltpu.PrefetchScalarGridSpec(
            num_scalar_prefetch=1,
            grid=(3,),
            in_specs=[
                whole_block(rows, channels),
                pl.BlockSpec((1, rows, channels), lambda i, _: (1 - i // 2, 0, 0)),
            ]
            + [whole_block(*b.shape) for b in backs],
            out_specs=[
                pl.BlockSpec((1, 1, part, channels), mine),
                pl.BlockSpec((1, part, channels), lambda i, _: (i, 0, 0)),
            ],
        ),
        compiler_params=params(24),
        cost_estimate=cost(2 * rows * channels, 14 * rows * channels),
        name="gradients",
    )(meta, query, side, *backs)


def place_crossed_kernel(meta_ref, cross_ref, held_ref, result_ref):
    result_ref[0, 0] = cross_ref[0]


def place_crossed(tp_at, meta, cross, result):
    three, part, channels = cross.shape

    def other(i, meta_ref):
        return (0, i, 0, 1 - meta_ref[tp_at])

    return pl.pallas_call(
        place_crossed_kernel,
        out_shape=bf16(result.shape),
        grid_spec=pltpu.PrefetchScalarGridSpec(
            num_scalar_prefetch=1,
            grid=(three,),
            in_specs=[pl.BlockSpec((1, part, channels), lambda i, _: (i, 0, 0)), anywhere()],
            out_specs=pl.BlockSpec((1, 1, part, channels), other),
        ),
        input_output_aliases={2: 0},
        compiler_params=params(24),
        cost_estimate=cost(0, 4 * math.prod(cross.shape)),
        name="place_crossed",
    )(meta, cross, result)


def swap(array, k):
    peers = lax.axis_size("ctx")
    return lax.ppermute(array, "ctx", [(i, i ^ k) for i in range(peers)]) if k else array


def swap_to_previous(array, k):
    peers = lax.axis_size("ctx")
    pipes = lax.axis_size("pipe")
    pairs = [
        (pipe * peers + i, (pipe - 1) % pipes * peers + (i ^ k))
        for pipe in range(pipes)
        for i in range(peers)
    ]
    return lax.ppermute(array, ("pipe", "ctx"), pairs)


def shards(qkv_proj, cotangent, block_dest, doc_start, mr_filter):
    peers = lax.axis_size("ctx")
    pipes = lax.axis_size("pipe")
    tp_count = lax.axis_size("tp")
    channels = cotangent.shape[2]
    group_count, taps = mr_filter.shape[1:]
    group_size = channels // group_count

    dest = lax.dynamic_index_in_dim(block_dest, lax.axis_index("pipe"), 0, keepdims=False)
    me_at = dest.shape[0]
    tp_at = me_at + 1
    here = [lax.axis_index("ctx"), lax.axis_index("tp")]
    meta = jnp.concatenate([dest, jnp.stack(here).astype(jnp.int32)])

    filt = lax.dynamic_index_in_dim(
        mr_filter[0].astype(F32).reshape(peers, group_count // peers, taps),
        lax.axis_index("ctx"),
        0,
        keepdims=False,
    )
    base_before = jnp.pad(filt[:, ::-1], ((0, 0), (1, taps - 1)))
    base_after = jnp.pad(filt, ((0, 0), (0, taps)))

    to_previous = [(pipe, (pipe - 1) % pipes) for pipe in range(pipes)]
    order = sending_order(peers)
    first_out, first_back = OUT_FIRST * peers // 8, BACK_FIRST * peers // 8

    mixed, gated, side = multiply(peers, qkv_proj, cotangent, doc_start)
    received = [swap(array, k) for array, k in zip(mixed, order)]
    side = lax.ppermute(side, "pipe", to_previous)
    mask_before, mask_after = document_masks(me_at, meta, received)

    medium = convolve(group_size, me_at, True, meta, received, mask_before, base_before)
    medium, late = lax.optimization_barrier((medium, gated[first_out:]))
    received = [swap(array, k) for array, k in zip(gated[:first_out] + late, order)]
    mixed_grad = convolve(group_size, me_at, False, meta, received, mask_after, base_after)
    mixed_grad, late = lax.optimization_barrier((mixed_grad, medium[first_back:]))
    medium = [swap(array, k) for array, k in zip(medium[:first_back] + late, order)]
    mixed_grad = [swap_to_previous(array, k) for array, k in zip(mixed_grad, order)]

    query = query_gradient(me_at, meta, medium, cotangent, mixed_grad[:QUERY_AFTER] + [side])
    query = lax.ppermute(query, "pipe", to_previous)
    result, cross = gradients(me_at, tp_at, tp_count, meta, query, side, mixed_grad)
    cross = lax.ppermute(cross, "tp", [(0, 1), (1, 0)])
    return place_crossed(tp_at, meta, cross, result)


def solution(mesh):
    placed = (
        P("pipe", None, "ctx", "tp"),
        P("pipe", "ctx", "tp"),
        P(),
        P("pipe", "ctx"),
        P("pipe", "tp", None),
    )
    return jax.shard_map(
        shards,
        mesh=mesh,
        in_specs=placed,
        out_specs=P("pipe", None, ("ctx", "tp"), None),
        check_vma=False,
    )
```

```python
import functools
import math

import jax
import jax.numpy as jnp
from jax import lax
from jax.experimental import pallas as pl
from jax.experimental.pallas import tpu as pltpu
from jax.sharding import PartitionSpec as P

LANES = 128
MARK_ROWS = 16
F32 = jnp.float32
BF16 = jnp.bfloat16


def params(mebibytes):
    return pltpu.CompilerParams(vmem_limit_bytes=mebibytes * 1024 * 1024)


def cost(flops, moved):
    return pl.CostEstimate(flops=flops, bytes_accessed=moved, transcendentals=0)


def whole_block(*shape):
    return pl.BlockSpec(shape, lambda *_: (0,) * len(shape))


def smem():
    return pl.BlockSpec(memory_space=pltpu.SMEM)


def anywhere():
    return pl.BlockSpec(memory_space=pl.ANY)


def bf16(shape):
    return jax.ShapeDtypeStruct(shape, BF16)


def sending_order(peers):
    half = peers // 2
    return [k for i in range(half) for k in (i, half + i)]


def multiply_kernel(proj_ref, grad_ref, marks_ref, *refs):
    outs, side_ref = refs[:2], refs[2]
    arrived, made, in_sems, out_sems, side_sems = refs[-5:]
    rows = grad_ref.shape[1]
    peers, _, width = outs[0].shape
    sources = [proj_ref.at[0, 1], proj_ref.at[0, 2], proj_ref.at[0, 0], grad_ref.at[0]]
    loads = [
        pltpu.make_async_copy(source, arrived.at[i], in_sems.at[i])
        for i, source in enumerate(sources)
    ]
    for load in loads:
        load.start()
    marks = jnp.broadcast_to(marks_ref[...].astype(F32), (MARK_ROWS, LANES)).astype(BF16)
    stores = []
    for half in range(2):
        loads[2 * half].wait()
        loads[2 * half + 1].wait()
        for peer in range(peers):
            at = half * peers + peer
            lanes = slice(peer * width, (peer + 1) * width)
            one = arrived[2 * half, :, lanes].astype(F32)
            other = arrived[2 * half + 1, :, lanes].astype(F32)
            made[at, :rows, :] = (one * other).astype(BF16)
            if half == 0:
                made[at, rows:, :LANES] = marks
                made[at, rows:, LANES:] = jnp.zeros((MARK_ROWS, width - LANES), BF16)
            source = made.at[at] if half == 0 else made.at[at, :rows]
            stores.append(pltpu.make_async_copy(source, outs[half].at[peer], out_sems.at[at]))
            stores[-1].start()
        if half == 0:
            for i in range(2):
                stores.append(
                    pltpu.make_async_copy(arrived.at[i], side_ref.at[i], side_sems.at[i])
                )
                stores[-1].start()
    for store in stores:
        store.wait()


def multiply(peers, qkv_proj, cotangent, marks):
    _, rows, channels = cotangent.shape
    width = channels // peers
    tall = rows + MARK_ROWS
    shapes = [(peers, tall, width), (peers, rows, width), (2, rows, channels)]
    return pl.pallas_call(
        multiply_kernel,
        out_shape=[bf16(shape) for shape in shapes],
        in_specs=[anywhere(), anywhere(), pl.BlockSpec(memory_space=pltpu.VMEM)],
        out_specs=[anywhere()] * len(shapes),
        scratch_shapes=[
            pltpu.VMEM((4, rows, channels), BF16),
            pltpu.VMEM((2 * peers, tall, width), BF16),
            pltpu.SemaphoreType.DMA((4,)),
            pltpu.SemaphoreType.DMA((2 * peers,)),
            pltpu.SemaphoreType.DMA((2,)),
        ],
        compiler_params=params(60),
        cost_estimate=cost(2 * rows * channels, 16 * rows * channels),
        name="multiply",
    )(qkv_proj, cotangent, marks)


def first_row(meta_ref, peers, source, block):
    block_rows = LANES // peers
    row = meta_ref[source * peers + block] * block_rows
    return pl.multiple_of(row, block_rows)


def masks_kernel(meta_ref, marks_ref, before_ref, after_ref, seq, across):
    peers = marks_ref.shape[0]
    tile = LANES
    block_rows = tile // peers
    row_ids = lax.broadcasted_iota(jnp.int32, (tile, tile), 0)
    lane_ids = lax.broadcasted_iota(jnp.int32, (tile, tile), 1)
    eye = (row_ids == lane_ids).astype(BF16)
    lower = (row_ids >= lane_ids).astype(BF16)
    for source in range(peers):
        spread = lax.dot_general(
            eye, marks_ref[source], (((1,), (1,)), ((), ())), preferred_element_type=F32
        )
        column = jnp.broadcast_to(spread[:, :1], (tile, tile))
        for block in range(peers):
            first = first_row(meta_ref, peers, source, block)
            seq[pl.ds(first, block_rows), :] = column[
                block * block_rows : (block + 1) * block_rows
            ]
    carry = jnp.zeros((1, tile), F32)
    for b in range(peers):
        rows = slice(b * tile, (b + 1) * tile)
        count = (
            jnp.dot(lower, seq[rows, :].astype(BF16), preferred_element_type=F32) + carry
        )
        carry = count[tile - 1 :, :]
        seq[rows, :] = count
        across[rows, :] = count.T
    for b in range(peers):
        here = seq[b * tile : (b + 1) * tile, :]

        def same(other):
            return (here == across[other * tile : (other + 1) * tile, :]).astype(F32).astype(BF16)

        before_ref[b, :, :tile] = same(max(b - 1, 0))
        before_ref[b, :, tile:] = same(b)
        after_ref[b, :, :tile] = same(b)
        after_ref[b, :, tile:] = same(min(b + 1, peers - 1))


def document_masks(meta, received):
    peers, all_rows, _ = received.shape
    tile = LANES
    last = all_rows // MARK_ROWS - 1
    out = (peers, tile, 2 * tile)
    return pl.pallas_call(
        masks_kernel,
        out_shape=[bf16(out)] * 2,
        in_specs=[smem(), pl.BlockSpec((peers, MARK_ROWS, tile), lambda _: (0, last, 0))],
        out_specs=[whole_block(*out)] * 2,
        scratch_shapes=[
            pltpu.VMEM((peers * tile, tile), F32),
            pltpu.VMEM((peers * tile, tile), F32),
        ],
        compiler_params=params(24),
        cost_estimate=cost(8 * peers * tile * tile, 8 * peers * tile * tile),
        grid=(1,),
        name="masks",
    )(meta, received)


def conv_kernel(group_size, me_at, causal, meta_ref, mask_ref, base_ref, recv_ref, *refs):
    outs, (rows32, rows16, toep) = refs[:-3], refs[-3:]
    peers = len(outs)
    tile = LANES
    width = outs[0].shape[1]
    groups = base_ref.shape[0]
    block_rows = tile // peers
    me = meta_ref[me_at]
    length = peers * tile
    pad, begin = (0, tile) if causal else (length, 0)
    rows16[pad : pad + tile, :] = jnp.zeros((tile, width), BF16)

    for group in range(groups):
        base = jnp.broadcast_to(base_ref[group : group + 1, :], (tile, 2 * tile))
        toep[group] = pltpu.roll(base, 0, 1, stride=1, stride_axis=0).astype(BF16)

    for source in range(peers):
        arrived = recv_ref[source, :tile, :].astype(F32)
        for block in range(peers):
            first = first_row(meta_ref, peers, source, block)
            rows32[pl.ds(first, block_rows), :] = arrived[
                block * block_rows : (block + 1) * block_rows
            ]
    rows16[begin : begin + length, :] = rows32[...].astype(BF16)

    tile_groups = tile // group_size
    lane_group = lax.broadcasted_iota(jnp.int32, (tile, tile), 1) // group_size

    def one_tile(b, carry):
        first = pl.multiple_of(b * tile, tile)
        mask = mask_ref[b]
        for sub in range(width // tile):
            lanes = slice(sub * tile, (sub + 1) * tile)
            window = rows16[pl.ds(first, 2 * tile), lanes]
            total = jnp.zeros((tile, tile), F32)
            for group in range(tile_groups):
                part = jnp.dot(
                    toep[sub * tile_groups + group] * mask, window, preferred_element_type=F32
                )
                total = jnp.where(lane_group == group, part, total)
            rows32[pl.ds(first, tile), lanes] = total
        return carry

    lax.fori_loop(0, peers, one_tile, 0)

    for k, out_ref in zip(sending_order(peers), outs):
        pieces = [
            rows32[pl.ds(first_row(meta_ref, peers, me ^ k, block), block_rows), :]
            for block in range(peers)
        ]
        out_ref[...] = jnp.concatenate(pieces, axis=0).astype(BF16)


def convolve(group_size, me_at, causal, meta, received, masks, bases):
    peers, _, width = received.shape
    tile = LANES
    groups = bases.shape[0]
    out = (tile, width)
    outs = pl.pallas_call(
        functools.partial(conv_kernel, group_size, me_at, causal),
        out_shape=[bf16(out)] * peers,
        in_specs=[
            smem(),
            whole_block(*masks.shape),
            whole_block(*bases.shape),
            whole_block(*received.shape),
        ],
        out_specs=[whole_block(*out)] * peers,
        scratch_shapes=[
            pltpu.VMEM((peers * tile, width), F32),
            pltpu.VMEM(((peers + 1) * tile, width), BF16),
            pltpu.VMEM((groups, tile, 2 * tile), BF16),
        ],
        compiler_params=params(24),
        cost_estimate=cost(
            4 * groups * peers * tile**3, 4 * peers * tile * width + 4 * peers * tile**2
        ),
        grid=(1,),
        name="convolve",
    )(meta, masks, bases, received)
    return list(outs)


def query_gradient_kernel(me_at, peers, meta_ref, grad_ref, *refs):
    out_ref = refs[-1]
    width = grad_ref.shape[2] // peers
    me = meta_ref[me_at]
    for k, back_ref in zip(sending_order(peers), refs):
        lanes = pl.ds(pl.multiple_of((me ^ k) * width, LANES), width)
        medium = back_ref[...].astype(F32)
        out_ref[:, lanes] = (grad_ref[0, :, lanes].astype(F32) * medium).astype(BF16)


def query_gradient(me_at, meta, backs, cotangent, others):
    peers = len(backs)
    _, rows, channels = cotangent.shape
    return pl.pallas_call(
        functools.partial(query_gradient_kernel, me_at, peers),
        out_shape=bf16((rows, channels)),
        in_specs=[smem(), whole_block(*cotangent.shape)]
        + [whole_block(*b.shape) for b in backs]
        + [anywhere() for _ in others],
        out_specs=whole_block(rows, channels),
        grid=(1,),
        compiler_params=params(24),
        cost_estimate=cost(rows * channels, 6 * rows * channels),
        name="query_gradient",
    )(meta, cotangent, *backs, *others)


def gradients_kernel(me_at, tp_at, peers, meta_ref, query_ref, side_ref, *refs):
    result_ref, cross_ref = refs[-2:]
    width = side_ref.shape[2] // peers
    part = cross_ref.shape[1]
    me = meta_ref[me_at]
    mine = meta_ref[tp_at]
    step = pl.program_id(0)
    for out_ref, index in ((cross_ref.at[0], 1 - mine), (result_ref.at[0, 0], mine)):
        at = pl.ds(pl.multiple_of(index * part, part), part)

        @pl.when(step == 0)
        def _():
            out_ref[...] = query_ref[at, :]

        @pl.when(step > 0)
        def _():
            for k, back_ref in zip(sending_order(peers), refs):
                lanes = pl.ds(pl.multiple_of((me ^ k) * width, LANES), width)
                mixed_grad = back_ref[at, :].astype(F32)
                factor = side_ref[0, at, lanes].astype(F32)
                out_ref[:, lanes] = (mixed_grad * factor).astype(BF16)


def gradients(me_at, tp_at, tp_count, meta, query, side, backs):
    peers = len(backs)
    _, rows, channels = side.shape
    part = rows // tp_count

    def mine(i, meta_ref):
        return (0, i, 0, meta_ref[tp_at])

    return pl.pallas_call(
        functools.partial(gradients_kernel, me_at, tp_at, peers),
        out_shape=[bf16((1, 3, part, channels * tp_count)), bf16((3, part, channels))],
        grid_spec=pltpu.PrefetchScalarGridSpec(
            num_scalar_prefetch=1,
            grid=(3,),
            in_specs=[
                whole_block(rows, channels),
                pl.BlockSpec((1, rows, channels), lambda i, _: (1 - i // 2, 0, 0)),
            ]
            + [whole_block(*b.shape) for b in backs],
            out_specs=[
                pl.BlockSpec((1, 1, part, channels), mine),
                pl.BlockSpec((1, part, channels), lambda i, _: (i, 0, 0)),
            ],
        ),
        compiler_params=params(24),
        cost_estimate=cost(2 * rows * channels, 14 * rows * channels),
        name="gradients",
    )(meta, query, side, *backs)


def place_crossed_kernel(meta_ref, cross_ref, held_ref, result_ref):
    result_ref[0, 0] = cross_ref[0]


def place_crossed(tp_at, meta, cross, result):
    three, part, channels = cross.shape

    def other(i, meta_ref):
        return (0, i, 0, 1 - meta_ref[tp_at])

    return pl.pallas_call(
        place_crossed_kernel,
        out_shape=bf16(result.shape),
        grid_spec=pltpu.PrefetchScalarGridSpec(
            num_scalar_prefetch=1,
            grid=(three,),
            in_specs=[pl.BlockSpec((1, part, channels), lambda i, _: (i, 0, 0)), anywhere()],
            out_specs=pl.BlockSpec((1, 1, part, channels), other),
        ),
        input_output_aliases={2: 0},
        compiler_params=params(24),
        cost_estimate=cost(0, 4 * math.prod(cross.shape)),
        name="place_crossed",
    )(meta, cross, result)


def swap(array, k):
    peers = lax.axis_size("ctx")
    return lax.ppermute(array, "ctx", [(i, i ^ k) for i in range(peers)]) if k else array


def swap_to_previous(array, k):
    peers = lax.axis_size("ctx")
    pipes = lax.axis_size("pipe")
    pairs = [
        (pipe * peers + i, (pipe - 1) % pipes * peers + (i ^ k))
        for pipe in range(pipes)
        for i in range(peers)
    ]
    return lax.ppermute(array, ("pipe", "ctx"), pairs)


def shards(qkv_proj, cotangent, block_dest, doc_start, mr_filter):
    peers = lax.axis_size("ctx")
    pipes = lax.axis_size("pipe")
    tp_count = lax.axis_size("tp")
    channels = cotangent.shape[2]
    group_count, taps = mr_filter.shape[1:]
    group_size = channels // group_count

    dest = lax.dynamic_index_in_dim(block_dest, lax.axis_index("pipe"), 0, keepdims=False)
    me_at = dest.shape[0]
    tp_at = me_at + 1
    here = [lax.axis_index("ctx"), lax.axis_index("tp")]
    meta = jnp.concatenate([dest, jnp.stack(here).astype(jnp.int32)])

    filt = lax.dynamic_index_in_dim(
        mr_filter[0].astype(F32).reshape(peers, group_count // peers, taps),
        lax.axis_index("ctx"),
        0,
        keepdims=False,
    )
    base_before = jnp.pad(filt[:, ::-1], ((0, 0), (1, taps - 1)))
    base_after = jnp.pad(filt, ((0, 0), (0, taps)))

    to_previous = [(pipe, (pipe - 1) % pipes) for pipe in range(pipes)]
    order = sending_order(peers)

    mixed, gated, side = multiply(peers, qkv_proj, cotangent, doc_start)
    side = lax.ppermute(side, "pipe", to_previous)
    mixed = lax.all_to_all(mixed, "ctx", 0, 0, tiled=True)
    gated = lax.all_to_all(gated, "ctx", 0, 0, tiled=True)
    mask_before, mask_after = document_masks(meta, mixed)
    medium = convolve(group_size, me_at, True, meta, mixed, mask_before, base_before)
    medium = [swap(array, k) for array, k in zip(medium, order)]

    query = query_gradient(me_at, meta, medium, cotangent, [side])
    gated, query = lax.optimization_barrier((gated, query))
    query = lax.ppermute(query, "pipe", to_previous)
    mixed_grad = convolve(group_size, me_at, False, meta, gated, mask_after, base_after)
    mixed_grad = [swap_to_previous(array, k) for array, k in zip(mixed_grad, order)]
    result, cross = gradients(me_at, tp_at, tp_count, meta, query, side, mixed_grad)
    cross = lax.ppermute(cross, "tp", [(0, 1), (1, 0)])
    return place_crossed(tp_at, meta, cross, result)


def solution(mesh):
    placed = (
        P("pipe", None, "ctx", "tp"),
        P("pipe", "ctx", "tp"),
        P(),
        P("pipe", "ctx"),
        P("pipe", "tp", None),
    )
    return jax.shard_map(
        shards,
        mesh=mesh,
        in_specs=placed,
        out_specs=P("pipe", None, ("ctx", "tp"), None),
        check_vma=False,
    )
```

```python
import functools
import math

import jax
import jax.numpy as jnp
from jax import lax
from jax.experimental import pallas as pl
from jax.experimental.pallas import tpu as pltpu
from jax.sharding import PartitionSpec as P

LANES = 128
CHUNKS = 2
MARK_ROWS = 16
OUT_FIRST = 5
BACK_FIRST = 5
F32 = jnp.float32
BF16 = jnp.bfloat16


def params(mebibytes):
    return pltpu.CompilerParams(vmem_limit_bytes=mebibytes * 1024 * 1024)


def whole_block(*shape):
    return pl.BlockSpec(shape, lambda _: (0,) * len(shape))


def smem():
    return pl.BlockSpec(memory_space=pltpu.SMEM)


def sending_order(peers):
    half = peers // 2
    return [k for i in range(half) for k in (i, half + i)]


def multiply_kernel(chunks, proj_ref, grad_ref, marks_ref, *refs):
    arrived, made, in_sems, out_sems, side_sems = refs[-5:]
    side_ref = refs[-6]
    outs = refs[:-6]
    peers = len(outs) // chunks
    rows = grad_ref.shape[1]
    width = outs[0].shape[1]
    span = peers * width
    me = lax.axis_index("ctx")
    loads, stores = [], []
    for chunk in range(chunks):
        lanes = pl.ds(chunk * span, span)
        for array in range(4):
            source = grad_ref.at[0, :, lanes] if array == 3 else proj_ref.at[0, array, :, lanes]
            loads.append(
                pltpu.make_async_copy(
                    source, arrived.at[array, :, lanes], in_sems.at[chunk, array]
                )
            )
    for load in loads:
        load.start()
    marks = jnp.broadcast_to(marks_ref[...].astype(F32), (MARK_ROWS, LANES)).astype(BF16)
    for chunk in range(chunks):
        for load in loads[4 * chunk : 4 * chunk + 4]:
            load.wait()
        for j, k in enumerate(sending_order(peers)):
            at = chunk * peers + j
            first = pl.multiple_of(chunk * span + (me ^ k) * width, LANES)
            query, key_rows, value, grad_in = [
                arrived[array, :, pl.ds(first, width)].astype(F32) for array in range(4)
            ]
            made[at, :rows, :] = (key_rows * value).astype(BF16)
            made[at, rows : 2 * rows, :] = (grad_in * query).astype(BF16)
            if chunk == 0:
                made[at, 2 * rows :, :LANES] = marks
                if width > LANES:
                    made[at, 2 * rows :, LANES:] = jnp.zeros((MARK_ROWS, width - LANES), BF16)
            source = made.at[at] if chunk == 0 else made.at[at, : 2 * rows]
            stores.append(pltpu.make_async_copy(source, outs[at], out_sems.at[at]))
            stores[-1].start()
        lanes = pl.ds(chunk * span, span)
        for array in range(3):
            stores.append(
                pltpu.make_async_copy(
                    arrived.at[array + 1, :, lanes],
                    side_ref.at[array, :, lanes],
                    side_sems.at[chunk, array],
                )
            )
            stores[-1].start()
    for store in stores:
        store.wait()


def multiply(chunks, width, peers, qkv_proj, cotangent, marks):
    _, rows, channels = cotangent.shape
    anywhere = pl.BlockSpec(memory_space=pl.ANY)
    tall = 2 * rows + MARK_ROWS
    shapes = [(tall if chunk == 0 else 2 * rows, width) for chunk in range(chunks)]
    shapes = [shape for shape in shapes for _ in range(peers)] + [(3, rows, channels)]
    made = pl.pallas_call(
        functools.partial(multiply_kernel, chunks),
        out_shape=[jax.ShapeDtypeStruct(shape, BF16) for shape in shapes],
        in_specs=[anywhere, anywhere, pl.BlockSpec(memory_space=pltpu.VMEM)],
        out_specs=[anywhere] * len(shapes),
        scratch_shapes=[
            pltpu.VMEM((4, rows, channels), BF16),
            pltpu.VMEM((chunks * peers, tall, width), BF16),
            pltpu.SemaphoreType.DMA((chunks, 4)),
            pltpu.SemaphoreType.DMA((chunks * peers,)),
            pltpu.SemaphoreType.DMA((chunks, 3)),
        ],
        compiler_params=params(60),
        cost_estimate=pl.CostEstimate(
            flops=2 * rows * channels, bytes_accessed=18 * rows * channels, transcendentals=0
        ),
        name="multiply",
    )(qkv_proj, cotangent, marks)
    return [list(made[c * peers : (c + 1) * peers]) for c in range(chunks)], made[-1]


def first_row(meta_ref, peers, source, block):
    block_rows = LANES // peers
    row = meta_ref[source * peers + block] * block_rows
    return pl.multiple_of(row, block_rows)


def masks_kernel(me_at, meta_ref, *refs):
    marks_refs, (out_ref, seq, across) = refs[:-3], refs[-3:]
    peers = len(marks_refs)
    tile = LANES
    block_rows = tile // peers
    me = meta_ref[me_at]
    row_ids = lax.broadcasted_iota(jnp.int32, (tile, tile), 0)
    lane_ids = lax.broadcasted_iota(jnp.int32, (tile, tile), 1)
    eye = (row_ids == lane_ids).astype(BF16)
    lower = (row_ids >= lane_ids).astype(BF16)
    for k, marks_ref in zip(sending_order(peers), marks_refs):
        spread = lax.dot_general(
            eye, marks_ref[...], (((1,), (1,)), ((), ())), preferred_element_type=F32
        )
        column = jnp.broadcast_to(spread[:, :1], (tile, tile))
        for block in range(peers):
            first = first_row(meta_ref, peers, me ^ k, block)
            seq[pl.ds(first, block_rows), :] = column[
                block * block_rows : (block + 1) * block_rows
            ]
    carry = jnp.zeros((1, tile), F32)
    for b in range(peers):
        rows = slice(b * tile, (b + 1) * tile)
        count = (
            jnp.dot(lower, seq[rows, :].astype(BF16), preferred_element_type=F32) + carry
        )
        carry = count[tile - 1 :, :]
        seq[rows, :] = count
        across[rows, :] = count.T
    for b in range(peers):
        here = seq[b * tile : (b + 1) * tile, :]

        def same(other):
            return (here == across[other * tile : (other + 1) * tile, :]).astype(F32).astype(BF16)

        out_ref[b, 0, :, :tile] = same(max(b - 1, 0))
        out_ref[b, 0, :, tile:] = same(b)
        out_ref[b, 1, :, :tile] = same(b)
        out_ref[b, 1, :, tile:] = same(min(b + 1, peers - 1))


def document_masks(me_at, meta, received, mark_rows):
    peers = len(received)
    tile = LANES
    last = received[0].shape[0] // mark_rows - 1
    out = (peers, 2, tile, 2 * tile)
    return pl.pallas_call(
        functools.partial(masks_kernel, me_at),
        out_shape=jax.ShapeDtypeStruct(out, BF16),
        in_specs=[smem()] + [pl.BlockSpec((mark_rows, tile), lambda _: (last, 0))] * peers,
        out_specs=whole_block(*out),
        scratch_shapes=[
            pltpu.VMEM((peers * tile, tile), F32),
            pltpu.VMEM((peers * tile, tile), F32),
        ],
        compiler_params=params(24),
        cost_estimate=pl.CostEstimate(
            flops=8 * peers * tile * tile, bytes_accessed=8 * peers * tile * tile, transcendentals=0
        ),
        grid=(1,),
        name="masks",
    )(meta, *received)


def conv_kernel(group_size, me_at, peers, meta_ref, mask_ref, base_ref, *refs):
    rows32, rows16, toep = refs[-3:]
    recv = refs[:peers]
    outs = refs[peers : 2 * peers]
    me = meta_ref[me_at]
    arrivals = [(me ^ k, recv_ref) for k, recv_ref in zip(sending_order(peers), recv)]
    tile = LANES
    width = outs[0].shape[1]
    groups = base_ref.shape[1]
    block_rows = tile // peers
    rows16[0, :tile, :] = jnp.zeros((tile, width), BF16)
    rows16[1, peers * tile :, :] = jnp.zeros((tile, width), BF16)

    for half in range(2):
        for group in range(groups):
            base = jnp.broadcast_to(base_ref[half, group : group + 1, :], (tile, 2 * tile))
            toep[half, group] = pltpu.roll(base, 0, 1, stride=1, stride_axis=0).astype(BF16)

    for source, recv_ref in arrivals:
        firsts = [first_row(meta_ref, peers, source, block) for block in range(peers)]
        for half in range(2):
            arrived = recv_ref[half * tile : (half + 1) * tile, :].astype(F32)
            for block in range(peers):
                rows32[half, pl.ds(firsts[block], block_rows), :] = arrived[
                    block * block_rows : (block + 1) * block_rows
                ]
    rows16[0, tile:, :] = rows32[0].astype(BF16)
    rows16[1, : peers * tile, :] = rows32[1].astype(BF16)

    tile_groups = tile // group_size
    lane_group = lax.broadcasted_iota(jnp.int32, (tile, tile), 1) // group_size

    def one_tile(b, carry):
        first = pl.multiple_of(b * tile, tile)
        for half in range(2):
            mask = mask_ref[b, half]
            for sub in range(width // tile):
                lanes = slice(sub * tile, (sub + 1) * tile)
                window = rows16[half, pl.ds(first, 2 * tile), lanes]
                total = jnp.zeros((tile, tile), F32)
                for group in range(tile_groups):
                    part = jnp.dot(
                        toep[half, sub * tile_groups + group] * mask,
                        window,
                        preferred_element_type=F32,
                    )
                    total = jnp.where(lane_group == group, part, total)
                rows32[half, pl.ds(first, tile), lanes] = total
        return carry

    lax.fori_loop(0, peers, one_tile, 0)

    for k, out_ref in zip(sending_order(peers), outs):
        firsts = [first_row(meta_ref, peers, me ^ k, block) for block in range(peers)]
        for half in range(2):
            pieces = [rows32[half, pl.ds(first, block_rows), :] for first in firsts]
            out_ref[half * tile : (half + 1) * tile, :] = jnp.concatenate(pieces, axis=0).astype(
                BF16
            )


def convolve(group_size, me_at, meta, received, masks, bases):
    peers = masks.shape[0]
    tile = LANES
    width = received[0].shape[-1]
    groups = bases.shape[1]
    out = (2 * tile, width)
    outs = pl.pallas_call(
        functools.partial(conv_kernel, group_size, me_at, peers),
        out_shape=[jax.ShapeDtypeStruct(out, BF16)] * peers,
        in_specs=[smem(), whole_block(*masks.shape), whole_block(*bases.shape)]
        + [whole_block(*r.shape) for r in received],
        out_specs=[whole_block(*out)] * peers,
        scratch_shapes=[
            pltpu.VMEM((2, peers * tile, width), F32),
            pltpu.VMEM((2, (peers + 1) * tile, width), BF16),
            pltpu.VMEM((2, groups, tile, 2 * tile), BF16),
        ],
        compiler_params=params(24),
        cost_estimate=pl.CostEstimate(
            flops=8 * groups * peers * tile**3,
            bytes_accessed=8 * peers * tile * width + 4 * peers * tile**2,
            transcendentals=0,
        ),
        grid=(1,),
        name="convolve",
    )(meta, masks, bases, *received)
    return list(outs)


def gradients_kernel(me_at, tp_at, peers, meta_ref, side_ref, *refs):
    result_ref, cross_ref = refs[-2:]
    rows = side_ref.shape[1]
    width = side_ref.shape[2] // peers
    part = cross_ref.shape[1]
    me = meta_ref[me_at]
    mine = meta_ref[tp_at]
    for out_ref, index in ((cross_ref, 1 - mine), (result_ref.at[0], mine)):
        first = pl.multiple_of(index * part, part)
        at = pl.ds(first, part)
        later = pl.ds(pl.multiple_of(first + rows, part), part)
        for k, back_ref in zip(sending_order(peers), refs):
            lanes = pl.ds(pl.multiple_of((me ^ k) * width, LANES), width)
            medium = back_ref[at, :].astype(F32)
            mixed_grad = back_ref[later, :].astype(F32)
            key_rows = side_ref[0, at, lanes].astype(F32)
            value = side_ref[1, at, lanes].astype(F32)
            grad_in = side_ref[2, at, lanes].astype(F32)
            out_ref[0, :, lanes] = (grad_in * medium).astype(BF16)
            out_ref[1, :, lanes] = (mixed_grad * value).astype(BF16)
            out_ref[2, :, lanes] = (mixed_grad * key_rows).astype(BF16)


def fixed(shape):
    return pl.BlockSpec(shape, lambda _, meta_ref: (0,) * len(shape))


def result_block(shape, chunk, chunks, tp_at, mine):
    def place(_, meta_ref):
        owner = meta_ref[tp_at] if mine else 1 - meta_ref[tp_at]
        return (0, 0, 0, owner * chunks + chunk)

    return pl.BlockSpec((1,) + shape, place)


def gradients(chunk, chunks, me_at, tp_at, tp_count, meta, backs, side, others):
    peers = len(backs)
    _, rows, channels = side.shape
    span = channels // chunks
    out = (3, rows // tp_count, span)
    whole = (1, 3, rows // tp_count, channels * tp_count)
    in_specs = [pl.BlockSpec((3, rows, span), lambda _, meta_ref: (0, 0, chunk))]
    in_specs += [fixed(backs[0].shape)] * peers
    args = [meta, side, *backs]
    aliases = {} if chunk == 0 else {len(args): 0}
    for other in others:
        args.append(other)
        in_specs.append(pl.BlockSpec(memory_space=pl.ANY))
    return pl.pallas_call(
        functools.partial(gradients_kernel, me_at, tp_at, peers),
        out_shape=[jax.ShapeDtypeStruct(whole, BF16), jax.ShapeDtypeStruct(out, BF16)],
        grid_spec=pltpu.PrefetchScalarGridSpec(
            num_scalar_prefetch=1,
            grid=(1,),
            in_specs=in_specs,
            out_specs=[result_block(out, chunk, chunks, tp_at, True), fixed(out)],
        ),
        input_output_aliases=aliases,
        compiler_params=params(24),
        cost_estimate=pl.CostEstimate(
            flops=3 * rows * span, bytes_accessed=16 * rows * span, transcendentals=0
        ),
        name="gradients",
    )(*args)


def place_kernel(meta_ref, cross_ref, held_ref, result_ref):
    result_ref[0] = cross_ref[...]


def place(chunk, chunks, tp_at, meta, cross, result):
    return pl.pallas_call(
        place_kernel,
        out_shape=jax.ShapeDtypeStruct(result.shape, BF16),
        grid_spec=pltpu.PrefetchScalarGridSpec(
            num_scalar_prefetch=1,
            grid=(1,),
            in_specs=[fixed(cross.shape), pl.BlockSpec(memory_space=pl.ANY)],
            out_specs=result_block(cross.shape, chunk, chunks, tp_at, False),
        ),
        input_output_aliases={2: 0},
        compiler_params=params(24),
        cost_estimate=pl.CostEstimate(
            flops=0, bytes_accessed=4 * math.prod(cross.shape), transcendentals=0
        ),
        name="place",
    )(meta, cross, result)


def swap(array, k):
    peers = lax.axis_size("ctx")
    return lax.ppermute(array, "ctx", [(i, i ^ k) for i in range(peers)]) if k else array


def swap_to_previous(array, k):
    peers = lax.axis_size("ctx")
    pipes = lax.axis_size("pipe")
    pairs = [
        (pipe * peers + i, (pipe - 1) % pipes * peers + (i ^ k))
        for pipe in range(pipes)
        for i in range(peers)
    ]
    return lax.ppermute(array, ("pipe", "ctx"), pairs)


def shards(qkv_proj, cotangent, block_dest, doc_start, mr_filter):
    peers = lax.axis_size("ctx")
    pipes = lax.axis_size("pipe")
    tp_count = lax.axis_size("tp")
    channels = cotangent.shape[2]
    group_count, taps = mr_filter.shape[1:]
    group_size = channels // group_count
    units = channels // (peers * LANES)
    chunks = math.gcd(units, CHUNKS)
    width = channels // (peers * chunks)
    chunk_groups = width // group_size

    dest = lax.dynamic_index_in_dim(block_dest, lax.axis_index("pipe"), 0, keepdims=False)
    me_at = dest.shape[0]
    tp_at = me_at + 1
    here = [lax.axis_index("ctx"), lax.axis_index("tp")]
    meta = jnp.concatenate([dest, jnp.stack(here).astype(jnp.int32)])

    filt = lax.dynamic_index_in_dim(
        mr_filter[0].astype(F32).reshape(chunks, peers, chunk_groups, taps),
        lax.axis_index("ctx"),
        1,
        keepdims=False,
    )
    causal = jnp.pad(filt[:, :, ::-1], ((0, 0), (0, 0), (1, taps - 1)))
    anti = jnp.pad(filt, ((0, 0), (0, 0), (0, taps)))
    bases = jnp.stack([causal, anti], axis=1)

    to_previous = [(pipe, (pipe - 1) % pipes) for pipe in range(pipes)]
    order = sending_order(peers)
    products, side = multiply(chunks, width, peers, qkv_proj, cotangent, doc_start)
    received = [swap(array, k) for array, k in zip(products[0], order)]
    side = lax.ppermute(side, "pipe", to_previous)

    first_out, first_back = OUT_FIRST * peers // 8, BACK_FIRST * peers // 8
    masks = document_masks(me_at, meta, received, MARK_ROWS)
    backs, late = [], []
    for chunk in range(chunks):
        coming = products[chunk + 1] if chunk + 1 < chunks else []
        convolved = convolve(group_size, me_at, meta, received, masks, bases[chunk])
        convolved, waited, late = lax.optimization_barrier((convolved, coming[first_out:], late))
        received = [swap(array, k) for array, k in zip(coming[:first_out] + waited, order)]
        if chunk:
            backs[-1] += [
                swap_to_previous(array, k) for array, k in zip(late, order[first_back:])
            ]
        if coming:
            late = convolved[first_back:]
        else:
            last, side = lax.optimization_barrier((convolved[first_back:], side))
            convolved = convolved[:first_back] + last
        now = first_back if coming else peers
        backs.append([swap_to_previous(array, k) for array, k in zip(convolved[:now], order)])

    result, held = None, []
    for chunk in range(chunks):
        others = [result] if chunk else [array for back in backs[1:] for array in back]
        result, cross = gradients(
            chunk, chunks, me_at, tp_at, tp_count, meta, backs[chunk], side, others
        )
        held.append(lax.ppermute(cross, "tp", [(0, 1), (1, 0)]))
    for chunk in range(chunks):
        result = place(chunk, chunks, tp_at, meta, held[chunk], result)
    return result


def solution(mesh):
    placed = (
        P("pipe", None, "ctx", "tp"),
        P("pipe", "ctx", "tp"),
        P(),
        P("pipe", "ctx"),
        P("pipe", "tp", None),
    )
    return jax.shard_map(
        shards,
        mesh=mesh,
        in_specs=placed,
        out_specs=P("pipe", None, ("ctx", "tp"), None),
        check_vma=False,
    )
```

```python
import functools
import math

import jax
import jax.numpy as jnp
from jax import lax
from jax.experimental import pallas as pl
from jax.experimental.pallas import tpu as pltpu
from jax.sharding import PartitionSpec as P

LANES = 128
CHUNKS = 1
MARK_ROWS = 16
OUT_FIRST = 5
BACK_FIRST = 5
F32 = jnp.float32
BF16 = jnp.bfloat16


def params(mebibytes):
    return pltpu.CompilerParams(vmem_limit_bytes=mebibytes * 1024 * 1024)


def whole_block(*shape):
    return pl.BlockSpec(shape, lambda _: (0,) * len(shape))


def smem():
    return pl.BlockSpec(memory_space=pltpu.SMEM)


def sending_order(peers):
    half = peers // 2
    return [k for i in range(half) for k in (i, half + i)]


def multiply_kernel(chunks, proj_ref, grad_ref, marks_ref, *refs):
    arrived, made, in_sems, out_sems, side_sems = refs[-5:]
    side_ref = refs[-6]
    outs = refs[:-6]
    peers = len(outs) // chunks
    rows = grad_ref.shape[1]
    width = outs[0].shape[1]
    span = peers * width
    me = lax.axis_index("ctx")
    loads, stores = [], []
    for chunk in range(chunks):
        lanes = pl.ds(chunk * span, span)
        for array in range(4):
            source = grad_ref.at[0, :, lanes] if array == 3 else proj_ref.at[0, array, :, lanes]
            loads.append(
                pltpu.make_async_copy(
                    source, arrived.at[array, :, lanes], in_sems.at[chunk, array]
                )
            )
    for load in loads:
        load.start()
    marks = jnp.broadcast_to(marks_ref[...].astype(F32), (MARK_ROWS, LANES)).astype(BF16)
    for chunk in range(chunks):
        for load in loads[4 * chunk : 4 * chunk + 4]:
            load.wait()
        for j, k in enumerate(sending_order(peers)):
            at = chunk * peers + j
            first = pl.multiple_of(chunk * span + (me ^ k) * width, LANES)
            query, key_rows, value, grad_in = [
                arrived[array, :, pl.ds(first, width)].astype(F32) for array in range(4)
            ]
            made[at, :rows, :] = (key_rows * value).astype(BF16)
            made[at, rows : 2 * rows, :] = (grad_in * query).astype(BF16)
            if chunk == 0:
                made[at, 2 * rows :, :LANES] = marks
                if width > LANES:
                    made[at, 2 * rows :, LANES:] = jnp.zeros((MARK_ROWS, width - LANES), BF16)
            source = made.at[at] if chunk == 0 else made.at[at, : 2 * rows]
            stores.append(pltpu.make_async_copy(source, outs[at], out_sems.at[at]))
            stores[-1].start()
        lanes = pl.ds(chunk * span, span)
        for array in range(3):
            stores.append(
                pltpu.make_async_copy(
                    arrived.at[array + 1, :, lanes],
                    side_ref.at[array, :, lanes],
                    side_sems.at[chunk, array],
                )
            )
            stores[-1].start()
    for store in stores:
        store.wait()


def multiply(chunks, width, peers, qkv_proj, cotangent, marks):
    _, rows, channels = cotangent.shape
    anywhere = pl.BlockSpec(memory_space=pl.ANY)
    tall = 2 * rows + MARK_ROWS
    shapes = [(tall if chunk == 0 else 2 * rows, width) for chunk in range(chunks)]
    shapes = [shape for shape in shapes for _ in range(peers)] + [(3, rows, channels)]
    made = pl.pallas_call(
        functools.partial(multiply_kernel, chunks),
        out_shape=[jax.ShapeDtypeStruct(shape, BF16) for shape in shapes],
        in_specs=[anywhere, anywhere, pl.BlockSpec(memory_space=pltpu.VMEM)],
        out_specs=[anywhere] * len(shapes),
        scratch_shapes=[
            pltpu.VMEM((4, rows, channels), BF16),
            pltpu.VMEM((chunks * peers, tall, width), BF16),
            pltpu.SemaphoreType.DMA((chunks, 4)),
            pltpu.SemaphoreType.DMA((chunks * peers,)),
            pltpu.SemaphoreType.DMA((chunks, 3)),
        ],
        compiler_params=params(60),
        cost_estimate=pl.CostEstimate(
            flops=2 * rows * channels, bytes_accessed=18 * rows * channels, transcendentals=0
        ),
        name="multiply",
    )(qkv_proj, cotangent, marks)
    return [list(made[c * peers : (c + 1) * peers]) for c in range(chunks)], made[-1]


def first_row(meta_ref, peers, source, block):
    block_rows = LANES // peers
    row = meta_ref[source * peers + block] * block_rows
    return pl.multiple_of(row, block_rows)


def masks_kernel(me_at, meta_ref, *refs):
    marks_refs, (out_ref, seq, across) = refs[:-3], refs[-3:]
    peers = len(marks_refs)
    tile = LANES
    block_rows = tile // peers
    me = meta_ref[me_at]
    row_ids = lax.broadcasted_iota(jnp.int32, (tile, tile), 0)
    lane_ids = lax.broadcasted_iota(jnp.int32, (tile, tile), 1)
    eye = (row_ids == lane_ids).astype(BF16)
    lower = (row_ids >= lane_ids).astype(BF16)
    for k, marks_ref in zip(sending_order(peers), marks_refs):
        spread = lax.dot_general(
            eye, marks_ref[...], (((1,), (1,)), ((), ())), preferred_element_type=F32
        )
        column = jnp.broadcast_to(spread[:, :1], (tile, tile))
        for block in range(peers):
            first = first_row(meta_ref, peers, me ^ k, block)
            seq[pl.ds(first, block_rows), :] = column[
                block * block_rows : (block + 1) * block_rows
            ]
    carry = jnp.zeros((1, tile), F32)
    for b in range(peers):
        rows = slice(b * tile, (b + 1) * tile)
        count = (
            jnp.dot(lower, seq[rows, :].astype(BF16), preferred_element_type=F32) + carry
        )
        carry = count[tile - 1 :, :]
        seq[rows, :] = count
        across[rows, :] = count.T
    for b in range(peers):
        here = seq[b * tile : (b + 1) * tile, :]

        def same(other):
            return (here == across[other * tile : (other + 1) * tile, :]).astype(F32).astype(BF16)

        out_ref[b, 0, :, :tile] = same(max(b - 1, 0))
        out_ref[b, 0, :, tile:] = same(b)
        out_ref[b, 1, :, :tile] = same(b)
        out_ref[b, 1, :, tile:] = same(min(b + 1, peers - 1))


def document_masks(me_at, meta, received, mark_rows):
    peers = len(received)
    tile = LANES
    last = received[0].shape[0] // mark_rows - 1
    out = (peers, 2, tile, 2 * tile)
    return pl.pallas_call(
        functools.partial(masks_kernel, me_at),
        out_shape=jax.ShapeDtypeStruct(out, BF16),
        in_specs=[smem()] + [pl.BlockSpec((mark_rows, tile), lambda _: (last, 0))] * peers,
        out_specs=whole_block(*out),
        scratch_shapes=[
            pltpu.VMEM((peers * tile, tile), F32),
            pltpu.VMEM((peers * tile, tile), F32),
        ],
        compiler_params=params(24),
        cost_estimate=pl.CostEstimate(
            flops=8 * peers * tile * tile, bytes_accessed=8 * peers * tile * tile, transcendentals=0
        ),
        grid=(1,),
        name="masks",
    )(meta, *received)


def conv_kernel(group_size, me_at, peers, meta_ref, mask_ref, base_ref, *refs):
    rows32, rows16, toep = refs[-3:]
    recv = refs[:peers]
    outs = refs[peers : 2 * peers]
    me = meta_ref[me_at]
    arrivals = [(me ^ k, recv_ref) for k, recv_ref in zip(sending_order(peers), recv)]
    tile = LANES
    width = outs[0].shape[1]
    groups = base_ref.shape[1]
    block_rows = tile // peers
    rows16[0, :tile, :] = jnp.zeros((tile, width), BF16)
    rows16[1, peers * tile :, :] = jnp.zeros((tile, width), BF16)

    for half in range(2):
        for group in range(groups):
            base = jnp.broadcast_to(base_ref[half, group : group + 1, :], (tile, 2 * tile))
            toep[half, group] = pltpu.roll(base, 0, 1, stride=1, stride_axis=0).astype(BF16)

    for source, recv_ref in arrivals:
        firsts = [first_row(meta_ref, peers, source, block) for block in range(peers)]
        for half in range(2):
            arrived = recv_ref[half * tile : (half + 1) * tile, :].astype(F32)
            for block in range(peers):
                rows32[half, pl.ds(firsts[block], block_rows), :] = arrived[
                    block * block_rows : (block + 1) * block_rows
                ]
    rows16[0, tile:, :] = rows32[0].astype(BF16)
    rows16[1, : peers * tile, :] = rows32[1].astype(BF16)

    tile_groups = tile // group_size
    lane_group = lax.broadcasted_iota(jnp.int32, (tile, tile), 1) // group_size

    def one_tile(b, carry):
        first = pl.multiple_of(b * tile, tile)
        for half in range(2):
            mask = mask_ref[b, half]
            for sub in range(width // tile):
                lanes = slice(sub * tile, (sub + 1) * tile)
                window = rows16[half, pl.ds(first, 2 * tile), lanes]
                total = jnp.zeros((tile, tile), F32)
                for group in range(tile_groups):
                    part = jnp.dot(
                        toep[half, sub * tile_groups + group] * mask,
                        window,
                        preferred_element_type=F32,
                    )
                    total = jnp.where(lane_group == group, part, total)
                rows32[half, pl.ds(first, tile), lanes] = total
        return carry

    lax.fori_loop(0, peers, one_tile, 0)

    for k, out_ref in zip(sending_order(peers), outs):
        firsts = [first_row(meta_ref, peers, me ^ k, block) for block in range(peers)]
        for half in range(2):
            pieces = [rows32[half, pl.ds(first, block_rows), :] for first in firsts]
            out_ref[half * tile : (half + 1) * tile, :] = jnp.concatenate(pieces, axis=0).astype(
                BF16
            )


def convolve(group_size, me_at, meta, received, masks, bases):
    peers = masks.shape[0]
    tile = LANES
    width = received[0].shape[-1]
    groups = bases.shape[1]
    out = (2 * tile, width)
    outs = pl.pallas_call(
        functools.partial(conv_kernel, group_size, me_at, peers),
        out_shape=[jax.ShapeDtypeStruct(out, BF16)] * peers,
        in_specs=[smem(), whole_block(*masks.shape), whole_block(*bases.shape)]
        + [whole_block(*r.shape) for r in received],
        out_specs=[whole_block(*out)] * peers,
        scratch_shapes=[
            pltpu.VMEM((2, peers * tile, width), F32),
            pltpu.VMEM((2, (peers + 1) * tile, width), BF16),
            pltpu.VMEM((2, groups, tile, 2 * tile), BF16),
        ],
        compiler_params=params(40),
        cost_estimate=pl.CostEstimate(
            flops=8 * groups * peers * tile**3,
            bytes_accessed=8 * peers * tile * width + 4 * peers * tile**2,
            transcendentals=0,
        ),
        grid=(1,),
        name="convolve",
    )(meta, masks, bases, *received)
    return list(outs)


def gradients_kernel(me_at, tp_at, peers, meta_ref, side_ref, *refs):
    result_ref, cross_ref = refs[-2:]
    rows = side_ref.shape[1]
    width = side_ref.shape[2] // peers
    part = cross_ref.shape[1]
    me = meta_ref[me_at]
    mine = meta_ref[tp_at]
    for out_ref, index in ((cross_ref, 1 - mine), (result_ref.at[0], mine)):
        first = pl.multiple_of(index * part, part)
        at = pl.ds(first, part)
        later = pl.ds(pl.multiple_of(first + rows, part), part)
        for k, back_ref in zip(sending_order(peers), refs):
            lanes = pl.ds(pl.multiple_of((me ^ k) * width, LANES), width)
            medium = back_ref[at, :].astype(F32)
            mixed_grad = back_ref[later, :].astype(F32)
            key_rows = side_ref[0, at, lanes].astype(F32)
            value = side_ref[1, at, lanes].astype(F32)
            grad_in = side_ref[2, at, lanes].astype(F32)
            out_ref[0, :, lanes] = (grad_in * medium).astype(BF16)
            out_ref[1, :, lanes] = (mixed_grad * value).astype(BF16)
            out_ref[2, :, lanes] = (mixed_grad * key_rows).astype(BF16)


def fixed(shape):
    return pl.BlockSpec(shape, lambda _, meta_ref: (0,) * len(shape))


def result_block(shape, chunk, chunks, tp_at, mine):
    def place(_, meta_ref):
        owner = meta_ref[tp_at] if mine else 1 - meta_ref[tp_at]
        return (0, 0, 0, owner * chunks + chunk)

    return pl.BlockSpec((1,) + shape, place)


def gradients(chunk, chunks, me_at, tp_at, tp_count, meta, backs, side, others):
    peers = len(backs)
    _, rows, channels = side.shape
    span = channels // chunks
    out = (3, rows // tp_count, span)
    whole = (1, 3, rows // tp_count, channels * tp_count)
    in_specs = [pl.BlockSpec((3, rows, span), lambda _, meta_ref: (0, 0, chunk))]
    in_specs += [fixed(backs[0].shape)] * peers
    args = [meta, side, *backs]
    aliases = {} if chunk == 0 else {len(args): 0}
    for other in others:
        args.append(other)
        in_specs.append(pl.BlockSpec(memory_space=pl.ANY))
    return pl.pallas_call(
        functools.partial(gradients_kernel, me_at, tp_at, peers),
        out_shape=[jax.ShapeDtypeStruct(whole, BF16), jax.ShapeDtypeStruct(out, BF16)],
        grid_spec=pltpu.PrefetchScalarGridSpec(
            num_scalar_prefetch=1,
            grid=(1,),
            in_specs=in_specs,
            out_specs=[result_block(out, chunk, chunks, tp_at, True), fixed(out)],
        ),
        input_output_aliases=aliases,
        compiler_params=params(24),
        cost_estimate=pl.CostEstimate(
            flops=3 * rows * span, bytes_accessed=16 * rows * span, transcendentals=0
        ),
        name="gradients",
    )(*args)


def place_kernel(meta_ref, cross_ref, held_ref, result_ref):
    result_ref[0] = cross_ref[...]


def place(chunk, chunks, tp_at, meta, cross, result):
    return pl.pallas_call(
        place_kernel,
        out_shape=jax.ShapeDtypeStruct(result.shape, BF16),
        grid_spec=pltpu.PrefetchScalarGridSpec(
            num_scalar_prefetch=1,
            grid=(1,),
            in_specs=[fixed(cross.shape), pl.BlockSpec(memory_space=pl.ANY)],
            out_specs=result_block(cross.shape, chunk, chunks, tp_at, False),
        ),
        input_output_aliases={2: 0},
        compiler_params=params(24),
        cost_estimate=pl.CostEstimate(
            flops=0, bytes_accessed=4 * math.prod(cross.shape), transcendentals=0
        ),
        name="place",
    )(meta, cross, result)


def swap(array, k):
    peers = lax.axis_size("ctx")
    return lax.ppermute(array, "ctx", [(i, i ^ k) for i in range(peers)]) if k else array


def swap_to_previous(array, k):
    peers = lax.axis_size("ctx")
    pipes = lax.axis_size("pipe")
    pairs = [
        (pipe * peers + i, (pipe - 1) % pipes * peers + (i ^ k))
        for pipe in range(pipes)
        for i in range(peers)
    ]
    return lax.ppermute(array, ("pipe", "ctx"), pairs)


def shards(qkv_proj, cotangent, block_dest, doc_start, mr_filter):
    peers = lax.axis_size("ctx")
    pipes = lax.axis_size("pipe")
    tp_count = lax.axis_size("tp")
    channels = cotangent.shape[2]
    group_count, taps = mr_filter.shape[1:]
    group_size = channels // group_count
    units = channels // (peers * LANES)
    chunks = math.gcd(units, CHUNKS)
    width = channels // (peers * chunks)
    chunk_groups = width // group_size

    dest = lax.dynamic_index_in_dim(block_dest, lax.axis_index("pipe"), 0, keepdims=False)
    me_at = dest.shape[0]
    tp_at = me_at + 1
    here = [lax.axis_index("ctx"), lax.axis_index("tp")]
    meta = jnp.concatenate([dest, jnp.stack(here).astype(jnp.int32)])

    filt = lax.dynamic_index_in_dim(
        mr_filter[0].astype(F32).reshape(chunks, peers, chunk_groups, taps),
        lax.axis_index("ctx"),
        1,
        keepdims=False,
    )
    causal = jnp.pad(filt[:, :, ::-1], ((0, 0), (0, 0), (1, taps - 1)))
    anti = jnp.pad(filt, ((0, 0), (0, 0), (0, taps)))
    bases = jnp.stack([causal, anti], axis=1)

    to_previous = [(pipe, (pipe - 1) % pipes) for pipe in range(pipes)]
    order = sending_order(peers)
    products, side = multiply(chunks, width, peers, qkv_proj, cotangent, doc_start)
    received = [swap(array, k) for array, k in zip(products[0], order)]
    side = lax.ppermute(side, "pipe", to_previous)

    first_out, first_back = OUT_FIRST * peers // 8, BACK_FIRST * peers // 8
    masks = document_masks(me_at, meta, received, MARK_ROWS)
    backs, late = [], []
    for chunk in range(chunks):
        coming = products[chunk + 1] if chunk + 1 < chunks else []
        convolved = convolve(group_size, me_at, meta, received, masks, bases[chunk])
        convolved, waited, late = lax.optimization_barrier((convolved, coming[first_out:], late))
        received = [swap(array, k) for array, k in zip(coming[:first_out] + waited, order)]
        if chunk:
            backs[-1] += [
                swap_to_previous(array, k) for array, k in zip(late, order[first_back:])
            ]
        if coming:
            late = convolved[first_back:]
        else:
            last, side = lax.optimization_barrier((convolved[first_back:], side))
            convolved = convolved[:first_back] + last
        now = first_back if coming else peers
        backs.append([swap_to_previous(array, k) for array, k in zip(convolved[:now], order)])

    result, held = None, []
    for chunk in range(chunks):
        others = [result] if chunk else [array for back in backs[1:] for array in back]
        result, cross = gradients(
            chunk, chunks, me_at, tp_at, tp_count, meta, backs[chunk], side, others
        )
        held.append(lax.ppermute(cross, "tp", [(0, 1), (1, 0)]))
    for chunk in range(chunks):
        result = place(chunk, chunks, tp_at, meta, held[chunk], result)
    return result


def solution(mesh):
    placed = (
        P("pipe", None, "ctx", "tp"),
        P("pipe", "ctx", "tp"),
        P(),
        P("pipe", "ctx"),
        P("pipe", "tp", None),
    )
    return jax.shard_map(
        shards,
        mesh=mesh,
        in_specs=placed,
        out_specs=P("pipe", None, ("ctx", "tp"), None),
        check_vma=False,
    )
```

```python
import functools
import math

import jax
import jax.numpy as jnp
from jax import lax
from jax.experimental import pallas as pl
from jax.experimental.pallas import tpu as pltpu
from jax.sharding import PartitionSpec as P

LANES = 128
CHUNKS = 1
MARK_ROWS = 16
OUT_FIRST = 5
BACK_FIRST = 5
F32 = jnp.float32
BF16 = jnp.bfloat16


def params(mebibytes):
    return pltpu.CompilerParams(vmem_limit_bytes=mebibytes * 1024 * 1024)


def whole_block(*shape):
    return pl.BlockSpec(shape, lambda _: (0,) * len(shape))


def smem():
    return pl.BlockSpec(memory_space=pltpu.SMEM)


def sending_order(peers):
    half = peers // 2
    return [0, 1, *range(half, peers), *range(2, half)]


def multiply_kernel(chunks, proj_ref, grad_ref, marks_ref, *refs):
    arrived, made, in_sems, out_sems, side_sems = refs[-5:]
    side_ref = refs[-6]
    outs = refs[:-6]
    peers = len(outs) // chunks
    rows = grad_ref.shape[1]
    width = outs[0].shape[1]
    span = peers * width
    me = lax.axis_index("ctx")
    loads, stores = [], []
    for chunk in range(chunks):
        lanes = pl.ds(chunk * span, span)
        for array in range(4):
            source = grad_ref.at[0, :, lanes] if array == 3 else proj_ref.at[0, array, :, lanes]
            loads.append(
                pltpu.make_async_copy(
                    source, arrived.at[array, :, lanes], in_sems.at[chunk, array]
                )
            )
    for load in loads:
        load.start()
    marks = jnp.broadcast_to(marks_ref[...].astype(F32), (MARK_ROWS, LANES)).astype(BF16)
    for chunk in range(chunks):
        for load in loads[4 * chunk : 4 * chunk + 4]:
            load.wait()
        for j, k in enumerate(sending_order(peers)):
            at = chunk * peers + j
            first = pl.multiple_of(chunk * span + (me ^ k) * width, LANES)
            query, key_rows, value, grad_in = [
                arrived[array, :, pl.ds(first, width)].astype(F32) for array in range(4)
            ]
            made[at, :rows, :] = (key_rows * value).astype(BF16)
            made[at, rows : 2 * rows, :] = (grad_in * query).astype(BF16)
            if chunk == 0:
                made[at, 2 * rows :, :LANES] = marks
                if width > LANES:
                    made[at, 2 * rows :, LANES:] = jnp.zeros((MARK_ROWS, width - LANES), BF16)
            source = made.at[at] if chunk == 0 else made.at[at, : 2 * rows]
            stores.append(pltpu.make_async_copy(source, outs[at], out_sems.at[at]))
            stores[-1].start()
        lanes = pl.ds(chunk * span, span)
        for array in range(3):
            stores.append(
                pltpu.make_async_copy(
                    arrived.at[array + 1, :, lanes],
                    side_ref.at[array, :, lanes],
                    side_sems.at[chunk, array],
                )
            )
            stores[-1].start()
    for store in stores:
        store.wait()


def multiply(chunks, width, peers, qkv_proj, cotangent, marks):
    _, rows, channels = cotangent.shape
    anywhere = pl.BlockSpec(memory_space=pl.ANY)
    tall = 2 * rows + MARK_ROWS
    shapes = [(tall if chunk == 0 else 2 * rows, width) for chunk in range(chunks)]
    shapes = [shape for shape in shapes for _ in range(peers)] + [(3, rows, channels)]
    made = pl.pallas_call(
        functools.partial(multiply_kernel, chunks),
        out_shape=[jax.ShapeDtypeStruct(shape, BF16) for shape in shapes],
        in_specs=[anywhere, anywhere, pl.BlockSpec(memory_space=pltpu.VMEM)],
        out_specs=[anywhere] * len(shapes),
        scratch_shapes=[
            pltpu.VMEM((4, rows, channels), BF16),
            pltpu.VMEM((chunks * peers, tall, width), BF16),
            pltpu.SemaphoreType.DMA((chunks, 4)),
            pltpu.SemaphoreType.DMA((chunks * peers,)),
            pltpu.SemaphoreType.DMA((chunks, 3)),
        ],
        compiler_params=params(60),
        cost_estimate=pl.CostEstimate(
            flops=2 * rows * channels, bytes_accessed=18 * rows * channels, transcendentals=0
        ),
        name="multiply",
    )(qkv_proj, cotangent, marks)
    return [list(made[c * peers : (c + 1) * peers]) for c in range(chunks)], made[-1]


def first_row(meta_ref, peers, source, block):
    block_rows = LANES // peers
    row = meta_ref[source * peers + block] * block_rows
    return pl.multiple_of(row, block_rows)


def masks_kernel(me_at, meta_ref, *refs):
    marks_refs, (out_ref, seq, across) = refs[:-3], refs[-3:]
    peers = len(marks_refs)
    tile = LANES
    block_rows = tile // peers
    me = meta_ref[me_at]
    row_ids = lax.broadcasted_iota(jnp.int32, (tile, tile), 0)
    lane_ids = lax.broadcasted_iota(jnp.int32, (tile, tile), 1)
    eye = (row_ids == lane_ids).astype(BF16)
    lower = (row_ids >= lane_ids).astype(BF16)
    for k, marks_ref in zip(sending_order(peers), marks_refs):
        spread = lax.dot_general(
            eye, marks_ref[...], (((1,), (1,)), ((), ())), preferred_element_type=F32
        )
        column = jnp.broadcast_to(spread[:, :1], (tile, tile))
        for block in range(peers):
            first = first_row(meta_ref, peers, me ^ k, block)
            seq[pl.ds(first, block_rows), :] = column[
                block * block_rows : (block + 1) * block_rows
            ]
    carry = jnp.zeros((1, tile), F32)
    for b in range(peers):
        rows = slice(b * tile, (b + 1) * tile)
        count = (
            jnp.dot(lower, seq[rows, :].astype(BF16), preferred_element_type=F32) + carry
        )
        carry = count[tile - 1 :, :]
        seq[rows, :] = count
        across[rows, :] = count.T
    for b in range(peers):
        here = seq[b * tile : (b + 1) * tile, :]

        def same(other):
            return (here == across[other * tile : (other + 1) * tile, :]).astype(F32).astype(BF16)

        out_ref[b, 0, :, :tile] = same(max(b - 1, 0))
        out_ref[b, 0, :, tile:] = same(b)
        out_ref[b, 1, :, :tile] = same(b)
        out_ref[b, 1, :, tile:] = same(min(b + 1, peers - 1))


def document_masks(me_at, meta, received, mark_rows):
    peers = len(received)
    tile = LANES
    last = received[0].shape[0] // mark_rows - 1
    out = (peers, 2, tile, 2 * tile)
    return pl.pallas_call(
        functools.partial(masks_kernel, me_at),
        out_shape=jax.ShapeDtypeStruct(out, BF16),
        in_specs=[smem()] + [pl.BlockSpec((mark_rows, tile), lambda _: (last, 0))] * peers,
        out_specs=whole_block(*out),
        scratch_shapes=[
            pltpu.VMEM((peers * tile, tile), F32),
            pltpu.VMEM((peers * tile, tile), F32),
        ],
        compiler_params=params(24),
        cost_estimate=pl.CostEstimate(
            flops=8 * peers * tile * tile, bytes_accessed=8 * peers * tile * tile, transcendentals=0
        ),
        grid=(1,),
        name="masks",
    )(meta, *received)


def conv_kernel(group_size, me_at, peers, meta_ref, mask_ref, base_ref, *refs):
    rows32, rows16, toep = refs[-3:]
    recv = refs[:peers]
    outs = refs[peers : 2 * peers]
    me = meta_ref[me_at]
    arrivals = [(me ^ k, recv_ref) for k, recv_ref in zip(sending_order(peers), recv)]
    tile = LANES
    width = outs[0].shape[1]
    groups = base_ref.shape[1]
    block_rows = tile // peers
    rows16[0, :tile, :] = jnp.zeros((tile, width), BF16)
    rows16[1, peers * tile :, :] = jnp.zeros((tile, width), BF16)

    for half in range(2):
        for group in range(groups):
            base = jnp.broadcast_to(base_ref[half, group : group + 1, :], (tile, 2 * tile))
            toep[half, group] = pltpu.roll(base, 0, 1, stride=1, stride_axis=0).astype(BF16)

    for source, recv_ref in arrivals:
        firsts = [first_row(meta_ref, peers, source, block) for block in range(peers)]
        for half in range(2):
            arrived = recv_ref[half * tile : (half + 1) * tile, :].astype(F32)
            for block in range(peers):
                rows32[half, pl.ds(firsts[block], block_rows), :] = arrived[
                    block * block_rows : (block + 1) * block_rows
                ]
    rows16[0, tile:, :] = rows32[0].astype(BF16)
    rows16[1, : peers * tile, :] = rows32[1].astype(BF16)

    tile_groups = tile // group_size
    lane_group = lax.broadcasted_iota(jnp.int32, (tile, tile), 1) // group_size

    def one_tile(b, carry):
        first = pl.multiple_of(b * tile, tile)
        for half in range(2):
            mask = mask_ref[b, half]
            for sub in range(width // tile):
                lanes = slice(sub * tile, (sub + 1) * tile)
                window = rows16[half, pl.ds(first, 2 * tile), lanes]
                total = jnp.zeros((tile, tile), F32)
                for group in range(tile_groups):
                    part = jnp.dot(
                        toep[half, sub * tile_groups + group] * mask,
                        window,
                        preferred_element_type=F32,
                    )
                    total = jnp.where(lane_group == group, part, total)
                rows32[half, pl.ds(first, tile), lanes] = total
        return carry

    lax.fori_loop(0, peers, one_tile, 0)

    for k, out_ref in zip(sending_order(peers), outs):
        firsts = [first_row(meta_ref, peers, me ^ k, block) for block in range(peers)]
        for half in range(2):
            pieces = [rows32[half, pl.ds(first, block_rows), :] for first in firsts]
            out_ref[half * tile : (half + 1) * tile, :] = jnp.concatenate(pieces, axis=0).astype(
                BF16
            )


def convolve(group_size, me_at, meta, received, masks, bases):
    peers = masks.shape[0]
    tile = LANES
    width = received[0].shape[-1]
    groups = bases.shape[1]
    out = (2 * tile, width)
    outs = pl.pallas_call(
        functools.partial(conv_kernel, group_size, me_at, peers),
        out_shape=[jax.ShapeDtypeStruct(out, BF16)] * peers,
        in_specs=[smem(), whole_block(*masks.shape), whole_block(*bases.shape)]
        + [whole_block(*r.shape) for r in received],
        out_specs=[whole_block(*out)] * peers,
        scratch_shapes=[
            pltpu.VMEM((2, peers * tile, width), F32),
            pltpu.VMEM((2, (peers + 1) * tile, width), BF16),
            pltpu.VMEM((2, groups, tile, 2 * tile), BF16),
        ],
        compiler_params=params(40),
        cost_estimate=pl.CostEstimate(
            flops=8 * groups * peers * tile**3,
            bytes_accessed=8 * peers * tile * width + 4 * peers * tile**2,
            transcendentals=0,
        ),
        grid=(1,),
        name="convolve",
    )(meta, masks, bases, *received)
    return list(outs)


def gradients_kernel(me_at, tp_at, peers, meta_ref, side_ref, *refs):
    result_ref, cross_ref = refs[-2:]
    rows = side_ref.shape[1]
    width = side_ref.shape[2] // peers
    part = cross_ref.shape[1]
    me = meta_ref[me_at]
    mine = meta_ref[tp_at]
    for out_ref, index in ((cross_ref, 1 - mine), (result_ref.at[0], mine)):
        first = pl.multiple_of(index * part, part)
        at = pl.ds(first, part)
        later = pl.ds(pl.multiple_of(first + rows, part), part)
        for k, back_ref in zip(sending_order(peers), refs):
            lanes = pl.ds(pl.multiple_of((me ^ k) * width, LANES), width)
            medium = back_ref[at, :].astype(F32)
            mixed_grad = back_ref[later, :].astype(F32)
            key_rows = side_ref[0, at, lanes].astype(F32)
            value = side_ref[1, at, lanes].astype(F32)
            grad_in = side_ref[2, at, lanes].astype(F32)
            out_ref[0, :, lanes] = (grad_in * medium).astype(BF16)
            out_ref[1, :, lanes] = (mixed_grad * value).astype(BF16)
            out_ref[2, :, lanes] = (mixed_grad * key_rows).astype(BF16)


def fixed(shape):
    return pl.BlockSpec(shape, lambda _, meta_ref: (0,) * len(shape))


def result_block(shape, chunk, chunks, tp_at, mine):
    def place(_, meta_ref):
        owner = meta_ref[tp_at] if mine else 1 - meta_ref[tp_at]
        return (0, 0, 0, owner * chunks + chunk)

    return pl.BlockSpec((1,) + shape, place)


def gradients(chunk, chunks, me_at, tp_at, tp_count, meta, backs, side, others):
    peers = len(backs)
    _, rows, channels = side.shape
    span = channels // chunks
    out = (3, rows // tp_count, span)
    whole = (1, 3, rows // tp_count, channels * tp_count)
    in_specs = [pl.BlockSpec((3, rows, span), lambda _, meta_ref: (0, 0, chunk))]
    in_specs += [fixed(backs[0].shape)] * peers
    args = [meta, side, *backs]
    aliases = {} if chunk == 0 else {len(args): 0}
    for other in others:
        args.append(other)
        in_specs.append(pl.BlockSpec(memory_space=pl.ANY))
    return pl.pallas_call(
        functools.partial(gradients_kernel, me_at, tp_at, peers),
        out_shape=[jax.ShapeDtypeStruct(whole, BF16), jax.ShapeDtypeStruct(out, BF16)],
        grid_spec=pltpu.PrefetchScalarGridSpec(
            num_scalar_prefetch=1,
            grid=(1,),
            in_specs=in_specs,
            out_specs=[result_block(out, chunk, chunks, tp_at, True), fixed(out)],
        ),
        input_output_aliases=aliases,
        compiler_params=params(24),
        cost_estimate=pl.CostEstimate(
            flops=3 * rows * span, bytes_accessed=16 * rows * span, transcendentals=0
        ),
        name="gradients",
    )(*args)


def place_kernel(meta_ref, cross_ref, held_ref, result_ref):
    result_ref[0] = cross_ref[...]


def place(chunk, chunks, tp_at, meta, cross, result):
    return pl.pallas_call(
        place_kernel,
        out_shape=jax.ShapeDtypeStruct(result.shape, BF16),
        grid_spec=pltpu.PrefetchScalarGridSpec(
            num_scalar_prefetch=1,
            grid=(1,),
            in_specs=[fixed(cross.shape), pl.BlockSpec(memory_space=pl.ANY)],
            out_specs=result_block(cross.shape, chunk, chunks, tp_at, False),
        ),
        input_output_aliases={2: 0},
        compiler_params=params(24),
        cost_estimate=pl.CostEstimate(
            flops=0, bytes_accessed=4 * math.prod(cross.shape), transcendentals=0
        ),
        name="place",
    )(meta, cross, result)


def swap(array, k):
    peers = lax.axis_size("ctx")
    return lax.ppermute(array, "ctx", [(i, i ^ k) for i in range(peers)]) if k else array


def swap_to_previous(array, k):
    peers = lax.axis_size("ctx")
    pipes = lax.axis_size("pipe")
    pairs = [
        (pipe * peers + i, (pipe - 1) % pipes * peers + (i ^ k))
        for pipe in range(pipes)
        for i in range(peers)
    ]
    return lax.ppermute(array, ("pipe", "ctx"), pairs)


def shards(qkv_proj, cotangent, block_dest, doc_start, mr_filter):
    peers = lax.axis_size("ctx")
    pipes = lax.axis_size("pipe")
    tp_count = lax.axis_size("tp")
    channels = cotangent.shape[2]
    group_count, taps = mr_filter.shape[1:]
    group_size = channels // group_count
    units = channels // (peers * LANES)
    chunks = math.gcd(units, CHUNKS)
    width = channels // (peers * chunks)
    chunk_groups = width // group_size

    dest = lax.dynamic_index_in_dim(block_dest, lax.axis_index("pipe"), 0, keepdims=False)
    me_at = dest.shape[0]
    tp_at = me_at + 1
    here = [lax.axis_index("ctx"), lax.axis_index("tp")]
    meta = jnp.concatenate([dest, jnp.stack(here).astype(jnp.int32)])

    filt = lax.dynamic_index_in_dim(
        mr_filter[0].astype(F32).reshape(chunks, peers, chunk_groups, taps),
        lax.axis_index("ctx"),
        1,
        keepdims=False,
    )
    causal = jnp.pad(filt[:, :, ::-1], ((0, 0), (0, 0), (1, taps - 1)))
    anti = jnp.pad(filt, ((0, 0), (0, 0), (0, taps)))
    bases = jnp.stack([causal, anti], axis=1)

    to_previous = [(pipe, (pipe - 1) % pipes) for pipe in range(pipes)]
    order = sending_order(peers)
    products, side = multiply(chunks, width, peers, qkv_proj, cotangent, doc_start)
    received = [swap(array, k) for array, k in zip(products[0], order)]
    side = lax.ppermute(side, "pipe", to_previous)

    first_out, first_back = OUT_FIRST * peers // 8, BACK_FIRST * peers // 8
    masks = document_masks(me_at, meta, received, MARK_ROWS)
    backs, late = [], []
    for chunk in range(chunks):
        coming = products[chunk + 1] if chunk + 1 < chunks else []
        convolved = convolve(group_size, me_at, meta, received, masks, bases[chunk])
        convolved, waited, late = lax.optimization_barrier((convolved, coming[first_out:], late))
        received = [swap(array, k) for array, k in zip(coming[:first_out] + waited, order)]
        if chunk:
            backs[-1] += [
                swap_to_previous(array, k) for array, k in zip(late, order[first_back:])
            ]
        if coming:
            late = convolved[first_back:]
        else:
            last, side = lax.optimization_barrier((convolved[first_back:], side))
            convolved = convolved[:first_back] + last
        now = first_back if coming else peers
        backs.append([swap_to_previous(array, k) for array, k in zip(convolved[:now], order)])

    result, held = None, []
    for chunk in range(chunks):
        others = [result] if chunk else [array for back in backs[1:] for array in back]
        result, cross = gradients(
            chunk, chunks, me_at, tp_at, tp_count, meta, backs[chunk], side, others
        )
        held.append(lax.ppermute(cross, "tp", [(0, 1), (1, 0)]))
    for chunk in range(chunks):
        result = place(chunk, chunks, tp_at, meta, held[chunk], result)
    return result


def solution(mesh):
    placed = (
        P("pipe", None, "ctx", "tp"),
        P("pipe", "ctx", "tp"),
        P(),
        P("pipe", "ctx"),
        P("pipe", "tp", None),
    )
    return jax.shard_map(
        shards,
        mesh=mesh,
        in_specs=placed,
        out_specs=P("pipe", None, ("ctx", "tp"), None),
        check_vma=False,
    )
```

```python
import functools
import math

import jax
import jax.numpy as jnp
from jax import lax
from jax.experimental import pallas as pl
from jax.experimental.pallas import tpu as pltpu
from jax.sharding import PartitionSpec as P

LANES = 128
CHUNKS = 1
MARK_ROWS = 16
OUT_FIRST = 5
BACK_FIRST = 5
F32 = jnp.float32
BF16 = jnp.bfloat16


def params(mebibytes):
    return pltpu.CompilerParams(vmem_limit_bytes=mebibytes * 1024 * 1024)


def whole_block(*shape):
    return pl.BlockSpec(shape, lambda _: (0,) * len(shape))


def smem():
    return pl.BlockSpec(memory_space=pltpu.SMEM)


def sending_order(peers):
    half = peers // 2
    return [k for i in range(half) for k in (i, half + i)]


def multiply_kernel(chunks, proj_ref, grad_ref, marks_ref, *refs):
    arrived, made, in_sems, out_sems, side_sems = refs[-5:]
    side_ref = refs[-6]
    outs = refs[:-6]
    peers = len(outs) // chunks
    rows = grad_ref.shape[1]
    width = outs[-1].shape[0] // (2 * rows) * LANES
    span = peers * width
    me = lax.axis_index("ctx")
    loads, stores = [], []
    for chunk in range(chunks):
        lanes = pl.ds(chunk * span, span)
        for array in range(4):
            source = grad_ref.at[0, :, lanes] if array == 3 else proj_ref.at[0, array, :, lanes]
            loads.append(
                pltpu.make_async_copy(
                    source, arrived.at[array, :, lanes], in_sems.at[chunk, array]
                )
            )
    for load in loads:
        load.start()
    marks = jnp.broadcast_to(marks_ref[...].astype(F32), (MARK_ROWS, LANES)).astype(BF16)
    for chunk in range(chunks):
        for load in loads[4 * chunk : 4 * chunk + 4]:
            load.wait()
        for j, k in enumerate(sending_order(peers)):
            at = chunk * peers + j
            first = pl.multiple_of(chunk * span + (me ^ k) * width, LANES)
            query, key_rows, value, grad_in = [
                arrived[array, :, pl.ds(first, width)].astype(F32) for array in range(4)
            ]
            for sub in range(width // LANES):
                lanes = slice(sub * LANES, (sub + 1) * LANES)
                top = 2 * rows * sub
                made[at, top : top + rows, :] = (key_rows * value)[:, lanes].astype(BF16)
                made[at, top + rows : top + 2 * rows, :] = (grad_in * query)[:, lanes].astype(BF16)
            if chunk == 0:
                made[at, made.shape[1] - MARK_ROWS :, :] = marks
            source = made.at[at] if chunk == 0 else made.at[at, : made.shape[1] - MARK_ROWS]
            stores.append(pltpu.make_async_copy(source, outs[at], out_sems.at[at]))
            stores[-1].start()
        lanes = pl.ds(chunk * span, span)
        for array in range(3):
            stores.append(
                pltpu.make_async_copy(
                    arrived.at[array + 1, :, lanes],
                    side_ref.at[array, :, lanes],
                    side_sems.at[chunk, array],
                )
            )
            stores[-1].start()
    for store in stores:
        store.wait()


def multiply(chunks, width, peers, qkv_proj, cotangent, marks):
    _, rows, channels = cotangent.shape
    anywhere = pl.BlockSpec(memory_space=pl.ANY)
    plain = 2 * rows * (width // LANES)
    tall = plain + MARK_ROWS
    shapes = [(tall if chunk == 0 else plain, LANES) for chunk in range(chunks)]
    shapes = [shape for shape in shapes for _ in range(peers)] + [(3, rows, channels)]
    made = pl.pallas_call(
        functools.partial(multiply_kernel, chunks),
        out_shape=[jax.ShapeDtypeStruct(shape, BF16) for shape in shapes],
        in_specs=[anywhere, anywhere, pl.BlockSpec(memory_space=pltpu.VMEM)],
        out_specs=[anywhere] * len(shapes),
        scratch_shapes=[
            pltpu.VMEM((4, rows, channels), BF16),
            pltpu.VMEM((chunks * peers, tall, LANES), BF16),
            pltpu.SemaphoreType.DMA((chunks, 4)),
            pltpu.SemaphoreType.DMA((chunks * peers,)),
            pltpu.SemaphoreType.DMA((chunks, 3)),
        ],
        compiler_params=params(60),
        cost_estimate=pl.CostEstimate(
            flops=2 * rows * channels, bytes_accessed=18 * rows * channels, transcendentals=0
        ),
        name="multiply",
    )(qkv_proj, cotangent, marks)
    return [list(made[c * peers : (c + 1) * peers]) for c in range(chunks)], made[-1]


def first_row(meta_ref, peers, source, block):
    block_rows = LANES // peers
    row = meta_ref[source * peers + block] * block_rows
    return pl.multiple_of(row, block_rows)


def masks_kernel(me_at, meta_ref, *refs):
    marks_refs, (out_ref, seq, across) = refs[:-3], refs[-3:]
    peers = len(marks_refs)
    tile = LANES
    block_rows = tile // peers
    me = meta_ref[me_at]
    row_ids = lax.broadcasted_iota(jnp.int32, (tile, tile), 0)
    lane_ids = lax.broadcasted_iota(jnp.int32, (tile, tile), 1)
    eye = (row_ids == lane_ids).astype(BF16)
    lower = (row_ids >= lane_ids).astype(BF16)
    for k, marks_ref in zip(sending_order(peers), marks_refs):
        spread = lax.dot_general(
            eye, marks_ref[...], (((1,), (1,)), ((), ())), preferred_element_type=F32
        )
        column = jnp.broadcast_to(spread[:, :1], (tile, tile))
        for block in range(peers):
            first = first_row(meta_ref, peers, me ^ k, block)
            seq[pl.ds(first, block_rows), :] = column[
                block * block_rows : (block + 1) * block_rows
            ]
    carry = jnp.zeros((1, tile), F32)
    for b in range(peers):
        rows = slice(b * tile, (b + 1) * tile)
        count = (
            jnp.dot(lower, seq[rows, :].astype(BF16), preferred_element_type=F32) + carry
        )
        carry = count[tile - 1 :, :]
        seq[rows, :] = count
        across[rows, :] = count.T
    for b in range(peers):
        here = seq[b * tile : (b + 1) * tile, :]

        def same(other):
            return (here == across[other * tile : (other + 1) * tile, :]).astype(F32).astype(BF16)

        out_ref[b, 0, :, :tile] = same(max(b - 1, 0))
        out_ref[b, 0, :, tile:] = same(b)
        out_ref[b, 1, :, :tile] = same(b)
        out_ref[b, 1, :, tile:] = same(min(b + 1, peers - 1))


def document_masks(me_at, meta, received, mark_rows):
    peers = len(received)
    tile = LANES
    last = received[0].shape[0] // mark_rows - 1
    out = (peers, 2, tile, 2 * tile)
    return pl.pallas_call(
        functools.partial(masks_kernel, me_at),
        out_shape=jax.ShapeDtypeStruct(out, BF16),
        in_specs=[smem()] + [pl.BlockSpec((mark_rows, tile), lambda _: (last, 0))] * peers,
        out_specs=whole_block(*out),
        scratch_shapes=[
            pltpu.VMEM((peers * tile, tile), F32),
            pltpu.VMEM((peers * tile, tile), F32),
        ],
        compiler_params=params(24),
        cost_estimate=pl.CostEstimate(
            flops=8 * peers * tile * tile, bytes_accessed=8 * peers * tile * tile, transcendentals=0
        ),
        grid=(1,),
        name="masks",
    )(meta, *received)


def toeplitz_kernel(base_ref, out_ref):
    _, groups, tile, span = out_ref.shape
    for group in range(groups):
        base = jnp.broadcast_to(base_ref[0, group : group + 1, :], (tile, span))
        out_ref[0, group] = pltpu.roll(base, 0, 1, stride=1, stride_axis=0).astype(BF16)


def toeplitz_of(bases):
    two, groups, span = bases.shape
    out = (two, groups, span // 2, span)
    return pl.pallas_call(
        toeplitz_kernel,
        out_shape=jax.ShapeDtypeStruct(out, BF16),
        in_specs=[pl.BlockSpec((1, groups, span), lambda i: (i, 0, 0))],
        out_specs=pl.BlockSpec((1,) + out[1:], lambda i: (i, 0, 0, 0)),
        compiler_params=params(24),
        cost_estimate=pl.CostEstimate(
            flops=two * groups * span * span, bytes_accessed=2 * math.prod(out), transcendentals=0
        ),
        grid=(two,),
        name="toeplitz",
    )(bases)


def conv_kernel(group_size, me_at, peers, meta_ref, mask_ref, toep_ref, *refs):
    rows32, rows16, toep, sem = refs[-4:]
    recv = refs[:peers]
    outs = refs[peers : 2 * peers]
    me = meta_ref[me_at]
    arrivals = [(me ^ k, recv_ref) for k, recv_ref in zip(sending_order(peers), recv)]
    tile = LANES
    width = outs[0].shape[1]
    block_rows = tile // peers
    rows16[0, :tile, :] = jnp.zeros((tile, width), BF16)
    rows16[1, peers * tile :, :] = jnp.zeros((tile, width), BF16)

    load = pltpu.make_async_copy(toep_ref, toep, sem)
    load.start()

    for source, recv_ref in arrivals:
        firsts = [first_row(meta_ref, peers, source, block) for block in range(peers)]
        for half in range(2):
            for sub in range(width // tile):
                top = (2 * sub + half) * tile
                lanes = slice(sub * tile, (sub + 1) * tile)
                arrived = recv_ref[top : top + tile, :].astype(F32)
                for block in range(peers):
                    rows32[half, pl.ds(firsts[block], block_rows), lanes] = arrived[
                        block * block_rows : (block + 1) * block_rows
                    ]
    rows16[0, tile:, :] = rows32[0].astype(BF16)
    rows16[1, : peers * tile, :] = rows32[1].astype(BF16)

    load.wait()
    tile_groups = tile // group_size
    lane_group = lax.broadcasted_iota(jnp.int32, (tile, tile), 1) // group_size

    def one_tile(b, carry):
        first = pl.multiple_of(b * tile, tile)
        for half in range(2):
            mask = mask_ref[b, half]
            for sub in range(width // tile):
                lanes = slice(sub * tile, (sub + 1) * tile)
                window = rows16[half, pl.ds(first, 2 * tile), lanes]
                total = jnp.zeros((tile, tile), F32)
                for group in range(tile_groups):
                    part = jnp.dot(
                        toep[half, sub * tile_groups + group] * mask,
                        window,
                        preferred_element_type=F32,
                    )
                    total = jnp.where(lane_group == group, part, total)
                rows32[half, pl.ds(first, tile), lanes] = total
        return carry

    lax.fori_loop(0, peers, one_tile, 0)

    for k, out_ref in zip(sending_order(peers), outs):
        firsts = [first_row(meta_ref, peers, me ^ k, block) for block in range(peers)]
        for half in range(2):
            pieces = [rows32[half, pl.ds(first, block_rows), :] for first in firsts]
            out_ref[half * tile : (half + 1) * tile, :] = jnp.concatenate(pieces, axis=0).astype(
                BF16
            )


def convolve(group_size, me_at, meta, received, masks, toeplitz):
    peers = masks.shape[0]
    tile = LANES
    groups = toeplitz.shape[1]
    width = groups * group_size
    out = (2 * tile, width)
    outs = pl.pallas_call(
        functools.partial(conv_kernel, group_size, me_at, peers),
        out_shape=[jax.ShapeDtypeStruct(out, BF16)] * peers,
        in_specs=[smem(), whole_block(*masks.shape), pl.BlockSpec(memory_space=pl.ANY)]
        + [whole_block(*r.shape) for r in received],
        out_specs=[whole_block(*out)] * peers,
        scratch_shapes=[
            pltpu.VMEM((2, peers * tile, width), F32),
            pltpu.VMEM((2, (peers + 1) * tile, width), BF16),
            pltpu.VMEM((2, groups, tile, 2 * tile), BF16),
            pltpu.SemaphoreType.DMA,
        ],
        compiler_params=params(40),
        cost_estimate=pl.CostEstimate(
            flops=8 * groups * peers * tile**3,
            bytes_accessed=8 * peers * tile * width + 4 * peers * tile**2,
            transcendentals=0,
        ),
        grid=(1,),
        name="convolve",
    )(meta, masks, toeplitz, *received)
    return list(outs)


def gradients_kernel(me_at, tp_at, peers, meta_ref, side_ref, *refs):
    result_ref, cross_ref = refs[-2:]
    rows = side_ref.shape[1]
    width = side_ref.shape[2] // peers
    part = cross_ref.shape[1]
    me = meta_ref[me_at]
    mine = meta_ref[tp_at]
    for out_ref, index in ((cross_ref, 1 - mine), (result_ref.at[0], mine)):
        first = pl.multiple_of(index * part, part)
        at = pl.ds(first, part)
        later = pl.ds(pl.multiple_of(first + rows, part), part)
        for k, back_ref in zip(sending_order(peers), refs):
            lanes = pl.ds(pl.multiple_of((me ^ k) * width, LANES), width)
            medium = back_ref[at, :].astype(F32)
            mixed_grad = back_ref[later, :].astype(F32)
            key_rows = side_ref[0, at, lanes].astype(F32)
            value = side_ref[1, at, lanes].astype(F32)
            grad_in = side_ref[2, at, lanes].astype(F32)
            out_ref[0, :, lanes] = (grad_in * medium).astype(BF16)
            out_ref[1, :, lanes] = (mixed_grad * value).astype(BF16)
            out_ref[2, :, lanes] = (mixed_grad * key_rows).astype(BF16)


def fixed(shape):
    return pl.BlockSpec(shape, lambda _, meta_ref: (0,) * len(shape))


def result_block(shape, chunk, chunks, tp_at, mine):
    def place(_, meta_ref):
        owner = meta_ref[tp_at] if mine else 1 - meta_ref[tp_at]
        return (0, 0, 0, owner * chunks + chunk)

    return pl.BlockSpec((1,) + shape, place)


def gradients(chunk, chunks, me_at, tp_at, tp_count, meta, backs, side, others):
    peers = len(backs)
    _, rows, channels = side.shape
    span = channels // chunks
    out = (3, rows // tp_count, span)
    whole = (1, 3, rows // tp_count, channels * tp_count)
    in_specs = [pl.BlockSpec((3, rows, span), lambda _, meta_ref: (0, 0, chunk))]
    in_specs += [fixed(backs[0].shape)] * peers
    args = [meta, side, *backs]
    aliases = {} if chunk == 0 else {len(args): 0}
    for other in others:
        args.append(other)
        in_specs.append(pl.BlockSpec(memory_space=pl.ANY))
    return pl.pallas_call(
        functools.partial(gradients_kernel, me_at, tp_at, peers),
        out_shape=[jax.ShapeDtypeStruct(whole, BF16), jax.ShapeDtypeStruct(out, BF16)],
        grid_spec=pltpu.PrefetchScalarGridSpec(
            num_scalar_prefetch=1,
            grid=(1,),
            in_specs=in_specs,
            out_specs=[result_block(out, chunk, chunks, tp_at, True), fixed(out)],
        ),
        input_output_aliases=aliases,
        compiler_params=params(24),
        cost_estimate=pl.CostEstimate(
            flops=3 * rows * span, bytes_accessed=16 * rows * span, transcendentals=0
        ),
        name="gradients",
    )(*args)


def place_kernel(meta_ref, cross_ref, held_ref, result_ref):
    result_ref[0] = cross_ref[...]


def place(chunk, chunks, tp_at, meta, cross, result):
    return pl.pallas_call(
        place_kernel,
        out_shape=jax.ShapeDtypeStruct(result.shape, BF16),
        grid_spec=pltpu.PrefetchScalarGridSpec(
            num_scalar_prefetch=1,
            grid=(1,),
            in_specs=[fixed(cross.shape), pl.BlockSpec(memory_space=pl.ANY)],
            out_specs=result_block(cross.shape, chunk, chunks, tp_at, False),
        ),
        input_output_aliases={2: 0},
        compiler_params=params(24),
        cost_estimate=pl.CostEstimate(
            flops=0, bytes_accessed=4 * math.prod(cross.shape), transcendentals=0
        ),
        name="place",
    )(meta, cross, result)


def swap(array, k):
    peers = lax.axis_size("ctx")
    return lax.ppermute(array, "ctx", [(i, i ^ k) for i in range(peers)]) if k else array


def swap_to_previous(array, k):
    peers = lax.axis_size("ctx")
    pipes = lax.axis_size("pipe")
    pairs = [
        (pipe * peers + i, (pipe - 1) % pipes * peers + (i ^ k))
        for pipe in range(pipes)
        for i in range(peers)
    ]
    return lax.ppermute(array, ("pipe", "ctx"), pairs)


def shards(qkv_proj, cotangent, block_dest, doc_start, mr_filter):
    peers = lax.axis_size("ctx")
    pipes = lax.axis_size("pipe")
    tp_count = lax.axis_size("tp")
    channels = cotangent.shape[2]
    group_count, taps = mr_filter.shape[1:]
    group_size = channels // group_count
    units = channels // (peers * LANES)
    chunks = math.gcd(units, CHUNKS)
    width = channels // (peers * chunks)
    chunk_groups = width // group_size

    dest = lax.dynamic_index_in_dim(block_dest, lax.axis_index("pipe"), 0, keepdims=False)
    me_at = dest.shape[0]
    tp_at = me_at + 1
    here = [lax.axis_index("ctx"), lax.axis_index("tp")]
    meta = jnp.concatenate([dest, jnp.stack(here).astype(jnp.int32)])

    filt = lax.dynamic_index_in_dim(
        mr_filter[0].astype(F32).reshape(chunks, peers, chunk_groups, taps),
        lax.axis_index("ctx"),
        1,
        keepdims=False,
    )
    causal = jnp.pad(filt[:, :, ::-1], ((0, 0), (0, 0), (1, taps - 1)))
    anti = jnp.pad(filt, ((0, 0), (0, 0), (0, taps)))
    bases = jnp.stack([causal, anti], axis=1)

    to_previous = [(pipe, (pipe - 1) % pipes) for pipe in range(pipes)]
    order = sending_order(peers)
    products, side = multiply(chunks, width, peers, qkv_proj, cotangent, doc_start)
    toeplitz = [toeplitz_of(bases[chunk]) for chunk in range(chunks)]
    received = [swap(array, k) for array, k in zip(products[0], order)]
    side = lax.ppermute(side, "pipe", to_previous)

    first_out, first_back = OUT_FIRST * peers // 8, BACK_FIRST * peers // 8
    masks = document_masks(me_at, meta, received, MARK_ROWS)
    backs, late = [], []
    for chunk in range(chunks):
        coming = products[chunk + 1] if chunk + 1 < chunks else []
        convolved = convolve(group_size, me_at, meta, received, masks, toeplitz[chunk])
        convolved, waited, late = lax.optimization_barrier((convolved, coming[first_out:], late))
        received = [swap(array, k) for array, k in zip(coming[:first_out] + waited, order)]
        if chunk:
            backs[-1] += [
                swap_to_previous(array, k) for array, k in zip(late, order[first_back:])
            ]
        if coming:
            late = convolved[first_back:]
        else:
            last, side = lax.optimization_barrier((convolved[first_back:], side))
            convolved = convolved[:first_back] + last
        now = first_back if coming else peers
        backs.append([swap_to_previous(array, k) for array, k in zip(convolved[:now], order)])

    result, held = None, []
    for chunk in range(chunks):
        others = [result] if chunk else [array for back in backs[1:] for array in back]
        result, cross = gradients(
            chunk, chunks, me_at, tp_at, tp_count, meta, backs[chunk], side, others
        )
        held.append(lax.ppermute(cross, "tp", [(0, 1), (1, 0)]))
    for chunk in range(chunks):
        result = place(chunk, chunks, tp_at, meta, held[chunk], result)
    return result


def solution(mesh):
    placed = (
        P("pipe", None, "ctx", "tp"),
        P("pipe", "ctx", "tp"),
        P(),
        P("pipe", "ctx"),
        P("pipe", "tp", None),
    )
    return jax.shard_map(
        shards,
        mesh=mesh,
        in_specs=placed,
        out_specs=P("pipe", None, ("ctx", "tp"), None),
        check_vma=False,
    )
```

```python
import functools
import math

import jax
import jax.numpy as jnp
from jax import lax
from jax.experimental import pallas as pl
from jax.experimental.pallas import tpu as pltpu
from jax.sharding import PartitionSpec as P

LANES = 128
CHUNKS = 1
MARK_ROWS = 16
OUT_FIRST = 5
BACK_FIRST = 5
F32 = jnp.float32
BF16 = jnp.bfloat16


def params(mebibytes):
    return pltpu.CompilerParams(vmem_limit_bytes=mebibytes * 1024 * 1024)


def whole_block(*shape):
    return pl.BlockSpec(shape, lambda _: (0,) * len(shape))


def smem():
    return pl.BlockSpec(memory_space=pltpu.SMEM)


def sending_order(peers):
    half = peers // 2
    return [k for i in range(half) for k in (i, half + i)]


def multiply_kernel(chunks, proj_ref, grad_ref, marks_ref, *refs):
    arrived, made, in_sems, out_sems = refs[-4:]
    outs = refs[:-4]
    peers = len(outs) // chunks
    rows = grad_ref.shape[1]
    width = outs[-1].shape[0] // (2 * rows) * LANES
    span = peers * width
    me = lax.axis_index("ctx")
    loads, stores = [], []
    for chunk in range(chunks):
        lanes = pl.ds(chunk * span, span)
        for array in range(4):
            source = grad_ref.at[0, :, lanes] if array == 3 else proj_ref.at[0, array, :, lanes]
            loads.append(
                pltpu.make_async_copy(
                    source, arrived.at[array, :, lanes], in_sems.at[chunk, array]
                )
            )
    for load in loads:
        load.start()
    marks = jnp.broadcast_to(marks_ref[...].astype(F32), (MARK_ROWS, LANES)).astype(BF16)
    for chunk in range(chunks):
        for load in loads[4 * chunk : 4 * chunk + 4]:
            load.wait()
        for j, k in enumerate(sending_order(peers)):
            at = chunk * peers + j
            first = pl.multiple_of(chunk * span + (me ^ k) * width, LANES)
            query, key_rows, value, grad_in = [
                arrived[array, :, pl.ds(first, width)].astype(F32) for array in range(4)
            ]
            for sub in range(width // LANES):
                lanes = slice(sub * LANES, (sub + 1) * LANES)
                top = 2 * rows * sub
                made[at, top : top + rows, :] = (key_rows * value)[:, lanes].astype(BF16)
                made[at, top + rows : top + 2 * rows, :] = (grad_in * query)[:, lanes].astype(BF16)
            if chunk == 0:
                made[at, made.shape[1] - MARK_ROWS :, :] = marks
            source = made.at[at] if chunk == 0 else made.at[at, : made.shape[1] - MARK_ROWS]
            stores.append(pltpu.make_async_copy(source, outs[at], out_sems.at[at]))
            stores[-1].start()
    for store in stores:
        store.wait()


def multiply(chunks, width, peers, qkv_proj, cotangent, marks):
    _, rows, channels = cotangent.shape
    anywhere = pl.BlockSpec(memory_space=pl.ANY)
    plain = 2 * rows * (width // LANES)
    tall = plain + MARK_ROWS
    shapes = [(tall if chunk == 0 else plain, LANES) for chunk in range(chunks)]
    shapes = [shape for shape in shapes for _ in range(peers)]
    made = pl.pallas_call(
        functools.partial(multiply_kernel, chunks),
        out_shape=[jax.ShapeDtypeStruct(shape, BF16) for shape in shapes],
        in_specs=[anywhere, anywhere, pl.BlockSpec(memory_space=pltpu.VMEM)],
        out_specs=[anywhere] * len(shapes),
        scratch_shapes=[
            pltpu.VMEM((4, rows, channels), BF16),
            pltpu.VMEM((chunks * peers, tall, LANES), BF16),
            pltpu.SemaphoreType.DMA((chunks, 4)),
            pltpu.SemaphoreType.DMA((chunks * peers,)),
        ],
        compiler_params=params(60),
        cost_estimate=pl.CostEstimate(
            flops=2 * rows * channels, bytes_accessed=12 * rows * channels, transcendentals=0
        ),
        name="multiply",
    )(qkv_proj, cotangent, marks)
    return [list(made[c * peers : (c + 1) * peers]) for c in range(chunks)]


def side_kernel(proj_ref, grad_ref, side_ref, arrived, in_sems, out_sems):
    sources = (proj_ref.at[0, 1], proj_ref.at[0, 2], grad_ref.at[0])
    rows = grad_ref.shape[1]
    parts = in_sems.shape[1]
    loads, stores = [], []
    for i, source in enumerate(sources):
        for part in range(parts):
            at = pl.ds(part * (rows // parts), rows // parts)
            loads.append(
                pltpu.make_async_copy(source.at[at], arrived.at[i, at], in_sems.at[i, part])
            )
            stores.append(
                pltpu.make_async_copy(arrived.at[i, at], side_ref.at[i, at], out_sems.at[i, part])
            )
    for load in loads:
        load.start()
    for load, store in zip(loads, stores):
        load.wait()
        store.start()
    for store in stores:
        store.wait()


def side_of(qkv_proj, cotangent):
    _, rows, channels = cotangent.shape
    anywhere = pl.BlockSpec(memory_space=pl.ANY)
    return pl.pallas_call(
        side_kernel,
        out_shape=jax.ShapeDtypeStruct((3, rows, channels), BF16),
        in_specs=[anywhere, anywhere],
        out_specs=anywhere,
        scratch_shapes=[
            pltpu.VMEM((3, rows, channels), BF16),
            pltpu.SemaphoreType.DMA((3, 2)),
            pltpu.SemaphoreType.DMA((3, 2)),
        ],
        compiler_params=params(60),
        cost_estimate=pl.CostEstimate(
            flops=0, bytes_accessed=12 * rows * channels, transcendentals=0
        ),
        name="side",
    )(qkv_proj, cotangent)


def first_row(meta_ref, peers, source, block):
    block_rows = LANES // peers
    row = meta_ref[source * peers + block] * block_rows
    return pl.multiple_of(row, block_rows)


def masks_kernel(me_at, meta_ref, *refs):
    marks_refs, (out_ref, seq, across) = refs[:-3], refs[-3:]
    peers = len(marks_refs)
    tile = LANES
    block_rows = tile // peers
    me = meta_ref[me_at]
    row_ids = lax.broadcasted_iota(jnp.int32, (tile, tile), 0)
    lane_ids = lax.broadcasted_iota(jnp.int32, (tile, tile), 1)
    eye = (row_ids == lane_ids).astype(BF16)
    lower = (row_ids >= lane_ids).astype(BF16)
    for k, marks_ref in zip(sending_order(peers), marks_refs):
        spread = lax.dot_general(
            eye, marks_ref[...], (((1,), (1,)), ((), ())), preferred_element_type=F32
        )
        column = jnp.broadcast_to(spread[:, :1], (tile, tile))
        for block in range(peers):
            first = first_row(meta_ref, peers, me ^ k, block)
            seq[pl.ds(first, block_rows), :] = column[
                block * block_rows : (block + 1) * block_rows
            ]
    carry = jnp.zeros((1, tile), F32)
    for b in range(peers):
        rows = slice(b * tile, (b + 1) * tile)
        count = (
            jnp.dot(lower, seq[rows, :].astype(BF16), preferred_element_type=F32) + carry
        )
        carry = count[tile - 1 :, :]
        seq[rows, :] = count
        across[rows, :] = count.T
    for b in range(peers):
        here = seq[b * tile : (b + 1) * tile, :]

        def same(other):
            return (here == across[other * tile : (other + 1) * tile, :]).astype(F32).astype(BF16)

        out_ref[b, 0, :, :tile] = same(max(b - 1, 0))
        out_ref[b, 0, :, tile:] = same(b)
        out_ref[b, 1, :, :tile] = same(b)
        out_ref[b, 1, :, tile:] = same(min(b + 1, peers - 1))


def document_masks(me_at, meta, received, mark_rows):
    peers = len(received)
    tile = LANES
    last = received[0].shape[0] // mark_rows - 1
    out = (peers, 2, tile, 2 * tile)
    return pl.pallas_call(
        functools.partial(masks_kernel, me_at),
        out_shape=jax.ShapeDtypeStruct(out, BF16),
        in_specs=[smem()] + [pl.BlockSpec((mark_rows, tile), lambda _: (last, 0))] * peers,
        out_specs=whole_block(*out),
        scratch_shapes=[
            pltpu.VMEM((peers * tile, tile), F32),
            pltpu.VMEM((peers * tile, tile), F32),
        ],
        compiler_params=params(24),
        cost_estimate=pl.CostEstimate(
            flops=8 * peers * tile * tile, bytes_accessed=8 * peers * tile * tile, transcendentals=0
        ),
        grid=(1,),
        name="masks",
    )(meta, *received)


def toeplitz_kernel(base_ref, out_ref):
    _, groups, tile, span = out_ref.shape
    for group in range(groups):
        base = jnp.broadcast_to(base_ref[0, group : group + 1, :], (tile, span))
        out_ref[0, group] = pltpu.roll(base, 0, 1, stride=1, stride_axis=0).astype(BF16)


def toeplitz_of(bases):
    two, groups, span = bases.shape
    out = (two, groups, span // 2, span)
    return pl.pallas_call(
        toeplitz_kernel,
        out_shape=jax.ShapeDtypeStruct(out, BF16),
        in_specs=[pl.BlockSpec((1, groups, span), lambda i: (i, 0, 0))],
        out_specs=pl.BlockSpec((1,) + out[1:], lambda i: (i, 0, 0, 0)),
        compiler_params=params(24),
        cost_estimate=pl.CostEstimate(
            flops=two * groups * span * span, bytes_accessed=2 * math.prod(out), transcendentals=0
        ),
        grid=(two,),
        name="toeplitz",
    )(bases)


def conv_kernel(group_size, me_at, peers, meta_ref, mask_ref, toep_ref, *refs):
    rows32, rows16, toep, sem = refs[-4:]
    recv = refs[:peers]
    outs = refs[peers : 2 * peers]
    me = meta_ref[me_at]
    arrivals = [(me ^ k, recv_ref) for k, recv_ref in zip(sending_order(peers), recv)]
    tile = LANES
    width = outs[0].shape[1]
    block_rows = tile // peers
    rows16[0, :tile, :] = jnp.zeros((tile, width), BF16)
    rows16[1, peers * tile :, :] = jnp.zeros((tile, width), BF16)

    load = pltpu.make_async_copy(toep_ref, toep, sem)
    load.start()

    for source, recv_ref in arrivals:
        firsts = [first_row(meta_ref, peers, source, block) for block in range(peers)]
        for half in range(2):
            for sub in range(width // tile):
                top = (2 * sub + half) * tile
                lanes = slice(sub * tile, (sub + 1) * tile)
                arrived = recv_ref[top : top + tile, :].astype(F32)
                for block in range(peers):
                    rows32[half, pl.ds(firsts[block], block_rows), lanes] = arrived[
                        block * block_rows : (block + 1) * block_rows
                    ]
    rows16[0, tile:, :] = rows32[0].astype(BF16)
    rows16[1, : peers * tile, :] = rows32[1].astype(BF16)

    load.wait()
    tile_groups = tile // group_size
    lane_group = lax.broadcasted_iota(jnp.int32, (tile, tile), 1) // group_size

    def one_tile(b, carry):
        first = pl.multiple_of(b * tile, tile)
        for half in range(2):
            mask = mask_ref[b, half]
            for sub in range(width // tile):
                lanes = slice(sub * tile, (sub + 1) * tile)
                window = rows16[half, pl.ds(first, 2 * tile), lanes]
                total = jnp.zeros((tile, tile), F32)
                for group in range(tile_groups):
                    part = jnp.dot(
                        toep[half, sub * tile_groups + group] * mask,
                        window,
                        preferred_element_type=F32,
                    )
                    total = jnp.where(lane_group == group, part, total)
                rows32[half, pl.ds(first, tile), lanes] = total
        return carry

    lax.fori_loop(0, peers, one_tile, 0)

    for k, out_ref in zip(sending_order(peers), outs):
        firsts = [first_row(meta_ref, peers, me ^ k, block) for block in range(peers)]
        for half in range(2):
            pieces = [rows32[half, pl.ds(first, block_rows), :] for first in firsts]
            out_ref[half * tile : (half + 1) * tile, :] = jnp.concatenate(pieces, axis=0).astype(
                BF16
            )


def convolve(group_size, me_at, meta, received, masks, toeplitz):
    peers = masks.shape[0]
    tile = LANES
    groups = toeplitz.shape[1]
    width = groups * group_size
    out = (2 * tile, width)
    outs = pl.pallas_call(
        functools.partial(conv_kernel, group_size, me_at, peers),
        out_shape=[jax.ShapeDtypeStruct(out, BF16)] * peers,
        in_specs=[smem(), whole_block(*masks.shape), pl.BlockSpec(memory_space=pl.ANY)]
        + [whole_block(*r.shape) for r in received],
        out_specs=[whole_block(*out)] * peers,
        scratch_shapes=[
            pltpu.VMEM((2, peers * tile, width), F32),
            pltpu.VMEM((2, (peers + 1) * tile, width), BF16),
            pltpu.VMEM((2, groups, tile, 2 * tile), BF16),
            pltpu.SemaphoreType.DMA,
        ],
        compiler_params=params(40),
        cost_estimate=pl.CostEstimate(
            flops=8 * groups * peers * tile**3,
            bytes_accessed=8 * peers * tile * width + 4 * peers * tile**2,
            transcendentals=0,
        ),
        grid=(1,),
        name="convolve",
    )(meta, masks, toeplitz, *received)
    return list(outs)


def gradients_kernel(me_at, tp_at, peers, meta_ref, side_ref, *refs):
    result_ref, cross_ref = refs[-2:]
    rows = side_ref.shape[1]
    width = side_ref.shape[2] // peers
    part = cross_ref.shape[1]
    me = meta_ref[me_at]
    mine = meta_ref[tp_at]
    for out_ref, index in ((cross_ref, 1 - mine), (result_ref.at[0], mine)):
        first = pl.multiple_of(index * part, part)
        at = pl.ds(first, part)
        later = pl.ds(pl.multiple_of(first + rows, part), part)
        for k, back_ref in zip(sending_order(peers), refs):
            lanes = pl.ds(pl.multiple_of((me ^ k) * width, LANES), width)
            medium = back_ref[at, :].astype(F32)
            mixed_grad = back_ref[later, :].astype(F32)
            key_rows = side_ref[0, at, lanes].astype(F32)
            value = side_ref[1, at, lanes].astype(F32)
            grad_in = side_ref[2, at, lanes].astype(F32)
            out_ref[0, :, lanes] = (grad_in * medium).astype(BF16)
            out_ref[1, :, lanes] = (mixed_grad * value).astype(BF16)
            out_ref[2, :, lanes] = (mixed_grad * key_rows).astype(BF16)


def fixed(shape):
    return pl.BlockSpec(shape, lambda _, meta_ref: (0,) * len(shape))


def result_block(shape, chunk, chunks, tp_at, mine):
    def place(_, meta_ref):
        owner = meta_ref[tp_at] if mine else 1 - meta_ref[tp_at]
        return (0, 0, 0, owner * chunks + chunk)

    return pl.BlockSpec((1,) + shape, place)


def gradients(chunk, chunks, me_at, tp_at, tp_count, meta, backs, side, others):
    peers = len(backs)
    _, rows, channels = side.shape
    span = channels // chunks
    out = (3, rows // tp_count, span)
    whole = (1, 3, rows // tp_count, channels * tp_count)
    in_specs = [pl.BlockSpec((3, rows, span), lambda _, meta_ref: (0, 0, chunk))]
    in_specs += [fixed(backs[0].shape)] * peers
    args = [meta, side, *backs]
    aliases = {} if chunk == 0 else {len(args): 0}
    for other in others:
        args.append(other)
        in_specs.append(pl.BlockSpec(memory_space=pl.ANY))
    return pl.pallas_call(
        functools.partial(gradients_kernel, me_at, tp_at, peers),
        out_shape=[jax.ShapeDtypeStruct(whole, BF16), jax.ShapeDtypeStruct(out, BF16)],
        grid_spec=pltpu.PrefetchScalarGridSpec(
            num_scalar_prefetch=1,
            grid=(1,),
            in_specs=in_specs,
            out_specs=[result_block(out, chunk, chunks, tp_at, True), fixed(out)],
        ),
        input_output_aliases=aliases,
        compiler_params=params(24),
        cost_estimate=pl.CostEstimate(
            flops=3 * rows * span, bytes_accessed=16 * rows * span, transcendentals=0
        ),
        name="gradients",
    )(*args)


def place_kernel(meta_ref, cross_ref, held_ref, result_ref):
    result_ref[0] = cross_ref[...]


def place(chunk, chunks, tp_at, meta, cross, result):
    return pl.pallas_call(
        place_kernel,
        out_shape=jax.ShapeDtypeStruct(result.shape, BF16),
        grid_spec=pltpu.PrefetchScalarGridSpec(
            num_scalar_prefetch=1,
            grid=(1,),
            in_specs=[fixed(cross.shape), pl.BlockSpec(memory_space=pl.ANY)],
            out_specs=result_block(cross.shape, chunk, chunks, tp_at, False),
        ),
        input_output_aliases={2: 0},
        compiler_params=params(24),
        cost_estimate=pl.CostEstimate(
            flops=0, bytes_accessed=4 * math.prod(cross.shape), transcendentals=0
        ),
        name="place",
    )(meta, cross, result)


def swap(array, k):
    peers = lax.axis_size("ctx")
    return lax.ppermute(array, "ctx", [(i, i ^ k) for i in range(peers)]) if k else array


def swap_to_previous(array, k):
    peers = lax.axis_size("ctx")
    pipes = lax.axis_size("pipe")
    pairs = [
        (pipe * peers + i, (pipe - 1) % pipes * peers + (i ^ k))
        for pipe in range(pipes)
        for i in range(peers)
    ]
    return lax.ppermute(array, ("pipe", "ctx"), pairs)


def shards(qkv_proj, cotangent, block_dest, doc_start, mr_filter):
    peers = lax.axis_size("ctx")
    pipes = lax.axis_size("pipe")
    tp_count = lax.axis_size("tp")
    channels = cotangent.shape[2]
    group_count, taps = mr_filter.shape[1:]
    group_size = channels // group_count
    units = channels // (peers * LANES)
    chunks = math.gcd(units, CHUNKS)
    width = channels // (peers * chunks)
    chunk_groups = width // group_size

    dest = lax.dynamic_index_in_dim(block_dest, lax.axis_index("pipe"), 0, keepdims=False)
    me_at = dest.shape[0]
    tp_at = me_at + 1
    here = [lax.axis_index("ctx"), lax.axis_index("tp")]
    meta = jnp.concatenate([dest, jnp.stack(here).astype(jnp.int32)])

    filt = lax.dynamic_index_in_dim(
        mr_filter[0].astype(F32).reshape(chunks, peers, chunk_groups, taps),
        lax.axis_index("ctx"),
        1,
        keepdims=False,
    )
    causal = jnp.pad(filt[:, :, ::-1], ((0, 0), (0, 0), (1, taps - 1)))
    anti = jnp.pad(filt, ((0, 0), (0, 0), (0, taps)))
    bases = jnp.stack([causal, anti], axis=1)

    to_previous = [(pipe, (pipe - 1) % pipes) for pipe in range(pipes)]
    order = sending_order(peers)
    products = multiply(chunks, width, peers, qkv_proj, cotangent, doc_start)
    toeplitz = [toeplitz_of(bases[chunk]) for chunk in range(chunks)]
    received = [swap(array, k) for array, k in zip(products[0], order)]
    side = lax.ppermute(side_of(qkv_proj, cotangent), "pipe", to_previous)

    first_out, first_back = OUT_FIRST * peers // 8, BACK_FIRST * peers // 8
    masks = document_masks(me_at, meta, received, MARK_ROWS)
    backs, late = [], []
    for chunk in range(chunks):
        coming = products[chunk + 1] if chunk + 1 < chunks else []
        convolved = convolve(group_size, me_at, meta, received, masks, toeplitz[chunk])
        convolved, waited, late = lax.optimization_barrier((convolved, coming[first_out:], late))
        received = [swap(array, k) for array, k in zip(coming[:first_out] + waited, order)]
        if chunk:
            backs[-1] += [
                swap_to_previous(array, k) for array, k in zip(late, order[first_back:])
            ]
        if coming:
            late = convolved[first_back:]
        else:
            last, side = lax.optimization_barrier((convolved[first_back:], side))
            convolved = convolved[:first_back] + last
        now = first_back if coming else peers
        backs.append([swap_to_previous(array, k) for array, k in zip(convolved[:now], order)])

    result, held = None, []
    for chunk in range(chunks):
        others = [result] if chunk else [array for back in backs[1:] for array in back]
        result, cross = gradients(
            chunk, chunks, me_at, tp_at, tp_count, meta, backs[chunk], side, others
        )
        held.append(lax.ppermute(cross, "tp", [(0, 1), (1, 0)]))
    for chunk in range(chunks):
        result = place(chunk, chunks, tp_at, meta, held[chunk], result)
    return result


def solution(mesh):
    placed = (
        P("pipe", None, "ctx", "tp"),
        P("pipe", "ctx", "tp"),
        P(),
        P("pipe", "ctx"),
        P("pipe", "tp", None),
    )
    return jax.shard_map(
        shards,
        mesh=mesh,
        in_specs=placed,
        out_specs=P("pipe", None, ("ctx", "tp"), None),
        check_vma=False,
    )
```

```python
import functools
import math

import jax
import jax.numpy as jnp
from jax import lax
from jax.experimental import pallas as pl
from jax.experimental.pallas import tpu as pltpu
from jax.sharding import PartitionSpec as P

LANES = 128
CHUNKS = 1
MARK_ROWS = 16
OUT_FIRST = 5
BACK_FIRST = 5
F32 = jnp.float32
BF16 = jnp.bfloat16


def params(mebibytes):
    return pltpu.CompilerParams(vmem_limit_bytes=mebibytes * 1024 * 1024)


def whole_block(*shape):
    return pl.BlockSpec(shape, lambda _: (0,) * len(shape))


def smem():
    return pl.BlockSpec(memory_space=pltpu.SMEM)


def sending_order(peers):
    half = peers // 2
    return [k for i in range(half) for k in (i, half + i)]


def multiply_kernel(chunks, proj_ref, grad_ref, marks_ref, *refs):
    arrived, made, in_sems, out_sems = refs[-4:]
    outs = refs[:-4]
    peers = len(outs) // chunks
    rows = grad_ref.shape[1]
    width = outs[-1].shape[0] // (2 * rows) * LANES
    span = peers * width
    me = lax.axis_index("ctx")
    loads, stores = [], []
    for chunk in range(chunks):
        lanes = pl.ds(chunk * span, span)
        for array in range(4):
            source = grad_ref.at[0, :, lanes] if array == 3 else proj_ref.at[0, array, :, lanes]
            loads.append(
                pltpu.make_async_copy(
                    source, arrived.at[array, :, lanes], in_sems.at[chunk, array]
                )
            )
    for load in loads:
        load.start()
    marks = jnp.broadcast_to(marks_ref[...].astype(F32), (MARK_ROWS, LANES)).astype(BF16)
    for chunk in range(chunks):
        for load in loads[4 * chunk : 4 * chunk + 4]:
            load.wait()
        for j, k in enumerate(sending_order(peers)):
            at = chunk * peers + j
            first = pl.multiple_of(chunk * span + (me ^ k) * width, LANES)
            query, key_rows, value, grad_in = [
                arrived[array, :, pl.ds(first, width)].astype(F32) for array in range(4)
            ]
            for sub in range(width // LANES):
                lanes = slice(sub * LANES, (sub + 1) * LANES)
                top = 2 * rows * sub
                made[at, top : top + rows, :] = (key_rows * value)[:, lanes].astype(BF16)
                made[at, top + rows : top + 2 * rows, :] = (grad_in * query)[:, lanes].astype(BF16)
            if chunk == 0:
                made[at, made.shape[1] - MARK_ROWS :, :] = marks
            source = made.at[at] if chunk == 0 else made.at[at, : made.shape[1] - MARK_ROWS]
            stores.append(pltpu.make_async_copy(source, outs[at], out_sems.at[at]))
            stores[-1].start()
    for store in stores:
        store.wait()


def multiply(chunks, width, peers, qkv_proj, cotangent, marks):
    _, rows, channels = cotangent.shape
    anywhere = pl.BlockSpec(memory_space=pl.ANY)
    plain = 2 * rows * (width // LANES)
    tall = plain + MARK_ROWS
    shapes = [(tall if chunk == 0 else plain, LANES) for chunk in range(chunks)]
    shapes = [shape for shape in shapes for _ in range(peers)]
    made = pl.pallas_call(
        functools.partial(multiply_kernel, chunks),
        out_shape=[jax.ShapeDtypeStruct(shape, BF16) for shape in shapes],
        in_specs=[anywhere, anywhere, pl.BlockSpec(memory_space=pltpu.VMEM)],
        out_specs=[anywhere] * len(shapes),
        scratch_shapes=[
            pltpu.VMEM((4, rows, channels), BF16),
            pltpu.VMEM((chunks * peers, tall, LANES), BF16),
            pltpu.SemaphoreType.DMA((chunks, 4)),
            pltpu.SemaphoreType.DMA((chunks * peers,)),
        ],
        compiler_params=params(60),
        cost_estimate=pl.CostEstimate(
            flops=2 * rows * channels, bytes_accessed=12 * rows * channels, transcendentals=0
        ),
        name="multiply",
    )(qkv_proj, cotangent, marks)
    return [list(made[c * peers : (c + 1) * peers]) for c in range(chunks)]


def side_kernel(proj_ref, grad_ref, side_ref, copy_ref, arrived, in_sems, out_sems):
    sources = (proj_ref.at[0, 1], proj_ref.at[0, 2], grad_ref.at[0])
    rows = grad_ref.shape[1]
    parts = in_sems.shape[1]
    loads, stores = [], []
    for i, source in enumerate(sources):
        for part in range(parts):
            at = pl.ds(part * (rows // parts), rows // parts)
            loads.append(
                pltpu.make_async_copy(source.at[at], arrived.at[i, at], in_sems.at[i, part])
            )
            target = copy_ref.at[0, at] if i == 2 else side_ref.at[i, at]
            stores.append(pltpu.make_async_copy(arrived.at[i, at], target, out_sems.at[i, part]))
    for load in loads:
        load.start()
    for load, store in zip(loads, stores):
        load.wait()
        store.start()
    for store in stores:
        store.wait()


def side_of(qkv_proj, cotangent):
    _, rows, channels = cotangent.shape
    anywhere = pl.BlockSpec(memory_space=pl.ANY)
    return pl.pallas_call(
        side_kernel,
        out_shape=[jax.ShapeDtypeStruct((n, rows, channels), BF16) for n in (2, 1)],
        in_specs=[anywhere, anywhere],
        out_specs=[anywhere] * 2,
        scratch_shapes=[
            pltpu.VMEM((3, rows, channels), BF16),
            pltpu.SemaphoreType.DMA((3, 2)),
            pltpu.SemaphoreType.DMA((3, 2)),
        ],
        compiler_params=params(60),
        cost_estimate=pl.CostEstimate(
            flops=0, bytes_accessed=12 * rows * channels, transcendentals=0
        ),
        name="side",
    )(qkv_proj, cotangent)


def first_row(meta_ref, peers, source, block):
    block_rows = LANES // peers
    row = meta_ref[source * peers + block] * block_rows
    return pl.multiple_of(row, block_rows)


def masks_kernel(me_at, meta_ref, *refs):
    marks_refs, (out_ref, seq, across) = refs[:-3], refs[-3:]
    peers = len(marks_refs)
    tile = LANES
    block_rows = tile // peers
    me = meta_ref[me_at]
    row_ids = lax.broadcasted_iota(jnp.int32, (tile, tile), 0)
    lane_ids = lax.broadcasted_iota(jnp.int32, (tile, tile), 1)
    eye = (row_ids == lane_ids).astype(BF16)
    lower = (row_ids >= lane_ids).astype(BF16)
    for k, marks_ref in zip(sending_order(peers), marks_refs):
        spread = lax.dot_general(
            eye, marks_ref[...], (((1,), (1,)), ((), ())), preferred_element_type=F32
        )
        column = jnp.broadcast_to(spread[:, :1], (tile, tile))
        for block in range(peers):
            first = first_row(meta_ref, peers, me ^ k, block)
            seq[pl.ds(first, block_rows), :] = column[
                block * block_rows : (block + 1) * block_rows
            ]
    carry = jnp.zeros((1, tile), F32)
    for b in range(peers):
        rows = slice(b * tile, (b + 1) * tile)
        count = (
            jnp.dot(lower, seq[rows, :].astype(BF16), preferred_element_type=F32) + carry
        )
        carry = count[tile - 1 :, :]
        seq[rows, :] = count
        across[rows, :] = count.T
    for b in range(peers):
        here = seq[b * tile : (b + 1) * tile, :]

        def same(other):
            return (here == across[other * tile : (other + 1) * tile, :]).astype(F32).astype(BF16)

        out_ref[b, 0, :, :tile] = same(max(b - 1, 0))
        out_ref[b, 0, :, tile:] = same(b)
        out_ref[b, 1, :, :tile] = same(b)
        out_ref[b, 1, :, tile:] = same(min(b + 1, peers - 1))


def document_masks(me_at, meta, received, mark_rows):
    peers = len(received)
    tile = LANES
    last = received[0].shape[0] // mark_rows - 1
    out = (peers, 2, tile, 2 * tile)
    return pl.pallas_call(
        functools.partial(masks_kernel, me_at),
        out_shape=jax.ShapeDtypeStruct(out, BF16),
        in_specs=[smem()] + [pl.BlockSpec((mark_rows, tile), lambda _: (last, 0))] * peers,
        out_specs=whole_block(*out),
        scratch_shapes=[
            pltpu.VMEM((peers * tile, tile), F32),
            pltpu.VMEM((peers * tile, tile), F32),
        ],
        compiler_params=params(24),
        cost_estimate=pl.CostEstimate(
            flops=8 * peers * tile * tile, bytes_accessed=8 * peers * tile * tile, transcendentals=0
        ),
        grid=(1,),
        name="masks",
    )(meta, *received)


def toeplitz_kernel(base_ref, out_ref):
    _, groups, tile, span = out_ref.shape
    for group in range(groups):
        base = jnp.broadcast_to(base_ref[0, group : group + 1, :], (tile, span))
        out_ref[0, group] = pltpu.roll(base, 0, 1, stride=1, stride_axis=0).astype(BF16)


def toeplitz_of(bases):
    two, groups, span = bases.shape
    out = (two, groups, span // 2, span)
    return pl.pallas_call(
        toeplitz_kernel,
        out_shape=jax.ShapeDtypeStruct(out, BF16),
        in_specs=[pl.BlockSpec((1, groups, span), lambda i: (i, 0, 0))],
        out_specs=pl.BlockSpec((1,) + out[1:], lambda i: (i, 0, 0, 0)),
        compiler_params=params(24),
        cost_estimate=pl.CostEstimate(
            flops=two * groups * span * span, bytes_accessed=2 * math.prod(out), transcendentals=0
        ),
        grid=(two,),
        name="toeplitz",
    )(bases)


def conv_kernel(group_size, me_at, peers, meta_ref, mask_ref, toep_ref, *refs):
    rows32, rows16, toep, sem = refs[-4:]
    recv = refs[:peers]
    outs = refs[peers : 2 * peers]
    me = meta_ref[me_at]
    arrivals = [(me ^ k, recv_ref) for k, recv_ref in zip(sending_order(peers), recv)]
    tile = LANES
    width = outs[0].shape[1]
    block_rows = tile // peers
    rows16[0, :tile, :] = jnp.zeros((tile, width), BF16)
    rows16[1, peers * tile :, :] = jnp.zeros((tile, width), BF16)

    load = pltpu.make_async_copy(toep_ref, toep, sem)
    load.start()

    for source, recv_ref in arrivals:
        firsts = [first_row(meta_ref, peers, source, block) for block in range(peers)]
        for half in range(2):
            for sub in range(width // tile):
                top = (2 * sub + half) * tile
                lanes = slice(sub * tile, (sub + 1) * tile)
                arrived = recv_ref[top : top + tile, :].astype(F32)
                for block in range(peers):
                    rows32[half, pl.ds(firsts[block], block_rows), lanes] = arrived[
                        block * block_rows : (block + 1) * block_rows
                    ]
    rows16[0, tile:, :] = rows32[0].astype(BF16)
    rows16[1, : peers * tile, :] = rows32[1].astype(BF16)

    load.wait()
    tile_groups = tile // group_size
    lane_group = lax.broadcasted_iota(jnp.int32, (tile, tile), 1) // group_size

    def one_tile(b, carry):
        first = pl.multiple_of(b * tile, tile)
        for half in range(2):
            mask = mask_ref[b, half]
            for sub in range(width // tile):
                lanes = slice(sub * tile, (sub + 1) * tile)
                window = rows16[half, pl.ds(first, 2 * tile), lanes]
                total = jnp.zeros((tile, tile), F32)
                for group in range(tile_groups):
                    part = jnp.dot(
                        toep[half, sub * tile_groups + group] * mask,
                        window,
                        preferred_element_type=F32,
                    )
                    total = jnp.where(lane_group == group, part, total)
                rows32[half, pl.ds(first, tile), lanes] = total
        return carry

    lax.fori_loop(0, peers, one_tile, 0)

    for k, out_ref in zip(sending_order(peers), outs):
        firsts = [first_row(meta_ref, peers, me ^ k, block) for block in range(peers)]
        for half in range(2):
            pieces = [rows32[half, pl.ds(first, block_rows), :] for first in firsts]
            out_ref[half * tile : (half + 1) * tile, :] = jnp.concatenate(pieces, axis=0).astype(
                BF16
            )


def convolve(group_size, me_at, meta, received, masks, toeplitz):
    peers = masks.shape[0]
    tile = LANES
    groups = toeplitz.shape[1]
    width = groups * group_size
    out = (2 * tile, width)
    outs = pl.pallas_call(
        functools.partial(conv_kernel, group_size, me_at, peers),
        out_shape=[jax.ShapeDtypeStruct(out, BF16)] * peers,
        in_specs=[smem(), whole_block(*masks.shape), pl.BlockSpec(memory_space=pl.ANY)]
        + [whole_block(*r.shape) for r in received],
        out_specs=[whole_block(*out)] * peers,
        scratch_shapes=[
            pltpu.VMEM((2, peers * tile, width), F32),
            pltpu.VMEM((2, (peers + 1) * tile, width), BF16),
            pltpu.VMEM((2, groups, tile, 2 * tile), BF16),
            pltpu.SemaphoreType.DMA,
        ],
        compiler_params=params(40),
        cost_estimate=pl.CostEstimate(
            flops=8 * groups * peers * tile**3,
            bytes_accessed=8 * peers * tile * width + 4 * peers * tile**2,
            transcendentals=0,
        ),
        grid=(1,),
        name="convolve",
    )(meta, masks, toeplitz, *received)
    return list(outs)


def gradients_kernel(me_at, tp_at, peers, meta_ref, side_ref, grad_ref, *refs):
    result_ref, cross_ref = refs[-2:]
    rows = side_ref.shape[1]
    width = side_ref.shape[2] // peers
    part = cross_ref.shape[1]
    me = meta_ref[me_at]
    mine = meta_ref[tp_at]
    for out_ref, index in ((cross_ref, 1 - mine), (result_ref.at[0], mine)):
        first = pl.multiple_of(index * part, part)
        at = pl.ds(first, part)
        later = pl.ds(pl.multiple_of(first + rows, part), part)
        for k, back_ref in zip(sending_order(peers), refs):
            lanes = pl.ds(pl.multiple_of((me ^ k) * width, LANES), width)
            medium = back_ref[at, :].astype(F32)
            mixed_grad = back_ref[later, :].astype(F32)
            key_rows = side_ref[0, at, lanes].astype(F32)
            value = side_ref[1, at, lanes].astype(F32)
            grad_in = grad_ref[0, at, lanes].astype(F32)
            out_ref[0, :, lanes] = (grad_in * medium).astype(BF16)
            out_ref[1, :, lanes] = (mixed_grad * value).astype(BF16)
            out_ref[2, :, lanes] = (mixed_grad * key_rows).astype(BF16)


def fixed(shape):
    return pl.BlockSpec(shape, lambda _, meta_ref: (0,) * len(shape))


def result_block(shape, chunk, chunks, tp_at, mine):
    def place(_, meta_ref):
        owner = meta_ref[tp_at] if mine else 1 - meta_ref[tp_at]
        return (0, 0, 0, owner * chunks + chunk)

    return pl.BlockSpec((1,) + shape, place)


def gradients(chunk, chunks, me_at, tp_at, tp_count, meta, backs, side, grad_in, others):
    peers = len(backs)
    _, rows, channels = side.shape
    span = channels // chunks
    out = (3, rows // tp_count, span)
    whole = (1, 3, rows // tp_count, channels * tp_count)
    in_specs = [
        pl.BlockSpec((2, rows, span), lambda _, meta_ref: (0, 0, chunk)),
        pl.BlockSpec((1, rows, span), lambda _, meta_ref: (0, 0, chunk)),
    ]
    in_specs += [fixed(backs[0].shape)] * peers
    args = [meta, side, grad_in, *backs]
    aliases = {} if chunk == 0 else {len(args): 0}
    for other in others:
        args.append(other)
        in_specs.append(pl.BlockSpec(memory_space=pl.ANY))
    return pl.pallas_call(
        functools.partial(gradients_kernel, me_at, tp_at, peers),
        out_shape=[jax.ShapeDtypeStruct(whole, BF16), jax.ShapeDtypeStruct(out, BF16)],
        grid_spec=pltpu.PrefetchScalarGridSpec(
            num_scalar_prefetch=1,
            grid=(1,),
            in_specs=in_specs,
            out_specs=[result_block(out, chunk, chunks, tp_at, True), fixed(out)],
        ),
        input_output_aliases=aliases,
        compiler_params=params(24),
        cost_estimate=pl.CostEstimate(
            flops=3 * rows * span, bytes_accessed=16 * rows * span, transcendentals=0
        ),
        name="gradients",
    )(*args)


def place_kernel(meta_ref, cross_ref, held_ref, result_ref):
    result_ref[0] = cross_ref[...]


def place(chunk, chunks, tp_at, meta, cross, result):
    return pl.pallas_call(
        place_kernel,
        out_shape=jax.ShapeDtypeStruct(result.shape, BF16),
        grid_spec=pltpu.PrefetchScalarGridSpec(
            num_scalar_prefetch=1,
            grid=(1,),
            in_specs=[fixed(cross.shape), pl.BlockSpec(memory_space=pl.ANY)],
            out_specs=result_block(cross.shape, chunk, chunks, tp_at, False),
        ),
        input_output_aliases={2: 0},
        compiler_params=params(24),
        cost_estimate=pl.CostEstimate(
            flops=0, bytes_accessed=4 * math.prod(cross.shape), transcendentals=0
        ),
        name="place",
    )(meta, cross, result)


def swap(array, k):
    peers = lax.axis_size("ctx")
    return lax.ppermute(array, "ctx", [(i, i ^ k) for i in range(peers)]) if k else array


def swap_to_previous(array, k):
    peers = lax.axis_size("ctx")
    pipes = lax.axis_size("pipe")
    pairs = [
        (pipe * peers + i, (pipe - 1) % pipes * peers + (i ^ k))
        for pipe in range(pipes)
        for i in range(peers)
    ]
    return lax.ppermute(array, ("pipe", "ctx"), pairs)


def shards(qkv_proj, cotangent, block_dest, doc_start, mr_filter):
    peers = lax.axis_size("ctx")
    pipes = lax.axis_size("pipe")
    tp_count = lax.axis_size("tp")
    channels = cotangent.shape[2]
    group_count, taps = mr_filter.shape[1:]
    group_size = channels // group_count
    units = channels // (peers * LANES)
    chunks = math.gcd(units, CHUNKS)
    width = channels // (peers * chunks)
    chunk_groups = width // group_size

    dest = lax.dynamic_index_in_dim(block_dest, lax.axis_index("pipe"), 0, keepdims=False)
    me_at = dest.shape[0]
    tp_at = me_at + 1
    here = [lax.axis_index("ctx"), lax.axis_index("tp")]
    meta = jnp.concatenate([dest, jnp.stack(here).astype(jnp.int32)])

    filt = lax.dynamic_index_in_dim(
        mr_filter[0].astype(F32).reshape(chunks, peers, chunk_groups, taps),
        lax.axis_index("ctx"),
        1,
        keepdims=False,
    )
    causal = jnp.pad(filt[:, :, ::-1], ((0, 0), (0, 0), (1, taps - 1)))
    anti = jnp.pad(filt, ((0, 0), (0, 0), (0, taps)))
    bases = jnp.stack([causal, anti], axis=1)

    to_previous = [(pipe, (pipe - 1) % pipes) for pipe in range(pipes)]
    order = sending_order(peers)
    products = multiply(chunks, width, peers, qkv_proj, cotangent, doc_start)
    toeplitz = [toeplitz_of(bases[chunk]) for chunk in range(chunks)]
    received = [swap(array, k) for array, k in zip(products[0], order)]
    side, grad_in = [
        lax.ppermute(array, "pipe", to_previous) for array in side_of(qkv_proj, cotangent)
    ]

    first_out, first_back = OUT_FIRST * peers // 8, BACK_FIRST * peers // 8
    masks = document_masks(me_at, meta, received, MARK_ROWS)
    backs, late = [], []
    for chunk in range(chunks):
        coming = products[chunk + 1] if chunk + 1 < chunks else []
        convolved = convolve(group_size, me_at, meta, received, masks, toeplitz[chunk])
        convolved, waited, late = lax.optimization_barrier((convolved, coming[first_out:], late))
        received = [swap(array, k) for array, k in zip(coming[:first_out] + waited, order)]
        if chunk:
            backs[-1] += [
                swap_to_previous(array, k) for array, k in zip(late, order[first_back:])
            ]
        if coming:
            late = convolved[first_back:]
        else:
            last, side, grad_in = lax.optimization_barrier((convolved[first_back:], side, grad_in))
            convolved = convolved[:first_back] + last
        now = first_back if coming else peers
        backs.append([swap_to_previous(array, k) for array, k in zip(convolved[:now], order)])

    result, held = None, []
    for chunk in range(chunks):
        others = [result] if chunk else [array for back in backs[1:] for array in back]
        result, cross = gradients(
            chunk, chunks, me_at, tp_at, tp_count, meta, backs[chunk], side, grad_in, others
        )
        held.append(lax.ppermute(cross, "tp", [(0, 1), (1, 0)]))
    for chunk in range(chunks):
        result = place(chunk, chunks, tp_at, meta, held[chunk], result)
    return result


def solution(mesh):
    placed = (
        P("pipe", None, "ctx", "tp"),
        P("pipe", "ctx", "tp"),
        P(),
        P("pipe", "ctx"),
        P("pipe", "tp", None),
    )
    return jax.shard_map(
        shards,
        mesh=mesh,
        in_specs=placed,
        out_specs=P("pipe", None, ("ctx", "tp"), None),
        check_vma=False,
    )
```

```python
import functools
import math

import jax
import jax.numpy as jnp
from jax import lax
from jax.experimental import pallas as pl
from jax.experimental.pallas import tpu as pltpu
from jax.sharding import PartitionSpec as P

LANES = 128
CHUNKS = 1
MARK_ROWS = 16
OUT_FIRST = 5
BACK_FIRST = 5
F32 = jnp.float32
BF16 = jnp.bfloat16


def params(mebibytes):
    return pltpu.CompilerParams(vmem_limit_bytes=mebibytes * 1024 * 1024)


def whole_block(*shape):
    return pl.BlockSpec(shape, lambda _: (0,) * len(shape))


def smem():
    return pl.BlockSpec(memory_space=pltpu.SMEM)


def sending_order(peers):
    half = peers // 2
    return [k for i in range(half) for k in (i, half + i)]


def multiply_kernel(chunks, proj_ref, grad_ref, marks_ref, *refs):
    arrived, made, in_sems, out_sems = refs[-4:]
    outs = refs[:-4]
    peers = len(outs) // chunks
    rows = grad_ref.shape[1]
    width = outs[-1].shape[0] // (2 * rows) * LANES
    span = peers * width
    me = lax.axis_index("ctx")
    loads, stores = [], []
    for chunk in range(chunks):
        lanes = pl.ds(chunk * span, span)
        for array in range(4):
            source = grad_ref.at[0, :, lanes] if array == 3 else proj_ref.at[0, array, :, lanes]
            loads.append(
                pltpu.make_async_copy(
                    source, arrived.at[array, :, lanes], in_sems.at[chunk, array]
                )
            )
    for load in loads:
        load.start()
    marks = jnp.broadcast_to(marks_ref[...].astype(F32), (MARK_ROWS, LANES)).astype(BF16)
    for chunk in range(chunks):
        for load in loads[4 * chunk : 4 * chunk + 4]:
            load.wait()
        for j, k in enumerate(sending_order(peers)):
            at = chunk * peers + j
            first = pl.multiple_of(chunk * span + (me ^ k) * width, LANES)
            query, key_rows, value, grad_in = [
                arrived[array, :, pl.ds(first, width)].astype(F32) for array in range(4)
            ]
            for sub in range(width // LANES):
                lanes = slice(sub * LANES, (sub + 1) * LANES)
                top = 2 * rows * sub
                made[at, top : top + rows, :] = (key_rows * value)[:, lanes].astype(BF16)
                made[at, top + rows : top + 2 * rows, :] = (grad_in * query)[:, lanes].astype(BF16)
            if chunk == 0:
                made[at, made.shape[1] - MARK_ROWS :, :] = marks
            source = made.at[at] if chunk == 0 else made.at[at, : made.shape[1] - MARK_ROWS]
            stores.append(pltpu.make_async_copy(source, outs[at], out_sems.at[at]))
            stores[-1].start()
    for store in stores:
        store.wait()


def multiply(chunks, width, peers, qkv_proj, cotangent, marks):
    _, rows, channels = cotangent.shape
    anywhere = pl.BlockSpec(memory_space=pl.ANY)
    plain = 2 * rows * (width // LANES)
    tall = plain + MARK_ROWS
    shapes = [(tall if chunk == 0 else plain, LANES) for chunk in range(chunks)]
    shapes = [shape for shape in shapes for _ in range(peers)]
    made = pl.pallas_call(
        functools.partial(multiply_kernel, chunks),
        out_shape=[jax.ShapeDtypeStruct(shape, BF16) for shape in shapes],
        in_specs=[anywhere, anywhere, pl.BlockSpec(memory_space=pltpu.VMEM)],
        out_specs=[anywhere] * len(shapes),
        scratch_shapes=[
            pltpu.VMEM((4, rows, channels), BF16),
            pltpu.VMEM((chunks * peers, tall, LANES), BF16),
            pltpu.SemaphoreType.DMA((chunks, 4)),
            pltpu.SemaphoreType.DMA((chunks * peers,)),
        ],
        compiler_params=params(60),
        cost_estimate=pl.CostEstimate(
            flops=2 * rows * channels, bytes_accessed=12 * rows * channels, transcendentals=0
        ),
        name="multiply",
    )(qkv_proj, cotangent, marks)
    return [list(made[c * peers : (c + 1) * peers]) for c in range(chunks)]


def side_kernel(proj_ref, grad_ref, side_ref, arrived, in_sems, out_sems):
    sources = (proj_ref.at[0, 1], proj_ref.at[0, 2], grad_ref.at[0])
    rows = grad_ref.shape[1]
    parts = in_sems.shape[1]
    loads, stores = [], []
    for i, source in enumerate(sources):
        for part in range(parts):
            at = pl.ds(part * (rows // parts), rows // parts)
            loads.append(
                pltpu.make_async_copy(source.at[at], arrived.at[i, at], in_sems.at[i, part])
            )
            stores.append(
                pltpu.make_async_copy(arrived.at[i, at], side_ref.at[i, at], out_sems.at[i, part])
            )
    for load in loads:
        load.start()
    for load, store in zip(loads, stores):
        load.wait()
        store.start()
    for store in stores:
        store.wait()


def side_of(qkv_proj, cotangent):
    _, rows, channels = cotangent.shape
    anywhere = pl.BlockSpec(memory_space=pl.ANY)
    return pl.pallas_call(
        side_kernel,
        out_shape=jax.ShapeDtypeStruct((3, rows, channels), BF16),
        in_specs=[anywhere, anywhere],
        out_specs=anywhere,
        scratch_shapes=[
            pltpu.VMEM((3, rows, channels), BF16),
            pltpu.SemaphoreType.DMA((3, 4)),
            pltpu.SemaphoreType.DMA((3, 4)),
        ],
        compiler_params=params(60),
        cost_estimate=pl.CostEstimate(
            flops=0, bytes_accessed=12 * rows * channels, transcendentals=0
        ),
        name="side",
    )(qkv_proj, cotangent)


def first_row(meta_ref, peers, source, block):
    block_rows = LANES // peers
    row = meta_ref[source * peers + block] * block_rows
    return pl.multiple_of(row, block_rows)


def masks_kernel(me_at, meta_ref, *refs):
    marks_refs, (out_ref, seq, across) = refs[:-3], refs[-3:]
    peers = len(marks_refs)
    tile = LANES
    block_rows = tile // peers
    me = meta_ref[me_at]
    row_ids = lax.broadcasted_iota(jnp.int32, (tile, tile), 0)
    lane_ids = lax.broadcasted_iota(jnp.int32, (tile, tile), 1)
    eye = (row_ids == lane_ids).astype(BF16)
    lower = (row_ids >= lane_ids).astype(BF16)
    for k, marks_ref in zip(sending_order(peers), marks_refs):
        spread = lax.dot_general(
            eye, marks_ref[...], (((1,), (1,)), ((), ())), preferred_element_type=F32
        )
        column = jnp.broadcast_to(spread[:, :1], (tile, tile))
        for block in range(peers):
            first = first_row(meta_ref, peers, me ^ k, block)
            seq[pl.ds(first, block_rows), :] = column[
                block * block_rows : (block + 1) * block_rows
            ]
    carry = jnp.zeros((1, tile), F32)
    for b in range(peers):
        rows = slice(b * tile, (b + 1) * tile)
        count = (
            jnp.dot(lower, seq[rows, :].astype(BF16), preferred_element_type=F32) + carry
        )
        carry = count[tile - 1 :, :]
        seq[rows, :] = count
        across[rows, :] = count.T
    for b in range(peers):
        here = seq[b * tile : (b + 1) * tile, :]

        def same(other):
            return (here == across[other * tile : (other + 1) * tile, :]).astype(F32).astype(BF16)

        out_ref[b, 0, :, :tile] = same(max(b - 1, 0))
        out_ref[b, 0, :, tile:] = same(b)
        out_ref[b, 1, :, :tile] = same(b)
        out_ref[b, 1, :, tile:] = same(min(b + 1, peers - 1))


def document_masks(me_at, meta, received, mark_rows):
    peers = len(received)
    tile = LANES
    last = received[0].shape[0] // mark_rows - 1
    out = (peers, 2, tile, 2 * tile)
    return pl.pallas_call(
        functools.partial(masks_kernel, me_at),
        out_shape=jax.ShapeDtypeStruct(out, BF16),
        in_specs=[smem()] + [pl.BlockSpec((mark_rows, tile), lambda _: (last, 0))] * peers,
        out_specs=whole_block(*out),
        scratch_shapes=[
            pltpu.VMEM((peers * tile, tile), F32),
            pltpu.VMEM((peers * tile, tile), F32),
        ],
        compiler_params=params(24),
        cost_estimate=pl.CostEstimate(
            flops=8 * peers * tile * tile, bytes_accessed=8 * peers * tile * tile, transcendentals=0
        ),
        grid=(1,),
        name="masks",
    )(meta, *received)


def toeplitz_kernel(base_ref, out_ref):
    _, groups, tile, span = out_ref.shape
    for group in range(groups):
        base = jnp.broadcast_to(base_ref[0, group : group + 1, :], (tile, span))
        out_ref[0, group] = pltpu.roll(base, 0, 1, stride=1, stride_axis=0).astype(BF16)


def toeplitz_of(bases):
    two, groups, span = bases.shape
    out = (two, groups, span // 2, span)
    return pl.pallas_call(
        toeplitz_kernel,
        out_shape=jax.ShapeDtypeStruct(out, BF16),
        in_specs=[pl.BlockSpec((1, groups, span), lambda i: (i, 0, 0))],
        out_specs=pl.BlockSpec((1,) + out[1:], lambda i: (i, 0, 0, 0)),
        compiler_params=params(24),
        cost_estimate=pl.CostEstimate(
            flops=two * groups * span * span, bytes_accessed=2 * math.prod(out), transcendentals=0
        ),
        grid=(two,),
        name="toeplitz",
    )(bases)


def conv_kernel(group_size, me_at, peers, meta_ref, mask_ref, toep_ref, *refs):
    rows32, rows16, toep, sem = refs[-4:]
    recv = refs[:peers]
    outs = refs[peers : 2 * peers]
    me = meta_ref[me_at]
    arrivals = [(me ^ k, recv_ref) for k, recv_ref in zip(sending_order(peers), recv)]
    tile = LANES
    width = outs[0].shape[1]
    block_rows = tile // peers
    rows16[0, :tile, :] = jnp.zeros((tile, width), BF16)
    rows16[1, peers * tile :, :] = jnp.zeros((tile, width), BF16)

    load = pltpu.make_async_copy(toep_ref, toep, sem)
    load.start()

    for source, recv_ref in arrivals:
        firsts = [first_row(meta_ref, peers, source, block) for block in range(peers)]
        for half in range(2):
            for sub in range(width // tile):
                top = (2 * sub + half) * tile
                lanes = slice(sub * tile, (sub + 1) * tile)
                arrived = recv_ref[top : top + tile, :].astype(F32)
                for block in range(peers):
                    rows32[half, pl.ds(firsts[block], block_rows), lanes] = arrived[
                        block * block_rows : (block + 1) * block_rows
                    ]
    rows16[0, tile:, :] = rows32[0].astype(BF16)
    rows16[1, : peers * tile, :] = rows32[1].astype(BF16)

    load.wait()
    tile_groups = tile // group_size
    lane_group = lax.broadcasted_iota(jnp.int32, (tile, tile), 1) // group_size

    def one_tile(b, carry):
        first = pl.multiple_of(b * tile, tile)
        for half in range(2):
            mask = mask_ref[b, half]
            for sub in range(width // tile):
                lanes = slice(sub * tile, (sub + 1) * tile)
                window = rows16[half, pl.ds(first, 2 * tile), lanes]
                total = jnp.zeros((tile, tile), F32)
                for group in range(tile_groups):
                    part = jnp.dot(
                        toep[half, sub * tile_groups + group] * mask,
                        window,
                        preferred_element_type=F32,
                    )
                    total = jnp.where(lane_group == group, part, total)
                rows32[half, pl.ds(first, tile), lanes] = total
        return carry

    lax.fori_loop(0, peers, one_tile, 0)

    for k, out_ref in zip(sending_order(peers), outs):
        firsts = [first_row(meta_ref, peers, me ^ k, block) for block in range(peers)]
        for half in range(2):
            pieces = [rows32[half, pl.ds(first, block_rows), :] for first in firsts]
            out_ref[half * tile : (half + 1) * tile, :] = jnp.concatenate(pieces, axis=0).astype(
                BF16
            )


def convolve(group_size, me_at, meta, received, masks, toeplitz):
    peers = masks.shape[0]
    tile = LANES
    groups = toeplitz.shape[1]
    width = groups * group_size
    out = (2 * tile, width)
    outs = pl.pallas_call(
        functools.partial(conv_kernel, group_size, me_at, peers),
        out_shape=[jax.ShapeDtypeStruct(out, BF16)] * peers,
        in_specs=[smem(), whole_block(*masks.shape), pl.BlockSpec(memory_space=pl.ANY)]
        + [whole_block(*r.shape) for r in received],
        out_specs=[whole_block(*out)] * peers,
        scratch_shapes=[
            pltpu.VMEM((2, peers * tile, width), F32),
            pltpu.VMEM((2, (peers + 1) * tile, width), BF16),
            pltpu.VMEM((2, groups, tile, 2 * tile), BF16),
            pltpu.SemaphoreType.DMA,
        ],
        compiler_params=params(40),
        cost_estimate=pl.CostEstimate(
            flops=8 * groups * peers * tile**3,
            bytes_accessed=8 * peers * tile * width + 4 * peers * tile**2,
            transcendentals=0,
        ),
        grid=(1,),
        name="convolve",
    )(meta, masks, toeplitz, *received)
    return list(outs)


def gradients_kernel(me_at, tp_at, peers, meta_ref, side_ref, *refs):
    result_ref, cross_ref = refs[-2:]
    rows = side_ref.shape[1]
    width = side_ref.shape[2] // peers
    part = cross_ref.shape[1]
    me = meta_ref[me_at]
    mine = meta_ref[tp_at]
    for out_ref, index in ((cross_ref, 1 - mine), (result_ref.at[0], mine)):
        first = pl.multiple_of(index * part, part)
        at = pl.ds(first, part)
        later = pl.ds(pl.multiple_of(first + rows, part), part)
        for k, back_ref in zip(sending_order(peers), refs):
            lanes = pl.ds(pl.multiple_of((me ^ k) * width, LANES), width)
            medium = back_ref[at, :].astype(F32)
            mixed_grad = back_ref[later, :].astype(F32)
            key_rows = side_ref[0, at, lanes].astype(F32)
            value = side_ref[1, at, lanes].astype(F32)
            grad_in = side_ref[2, at, lanes].astype(F32)
            out_ref[0, :, lanes] = (grad_in * medium).astype(BF16)
            out_ref[1, :, lanes] = (mixed_grad * value).astype(BF16)
            out_ref[2, :, lanes] = (mixed_grad * key_rows).astype(BF16)


def fixed(shape):
    return pl.BlockSpec(shape, lambda _, meta_ref: (0,) * len(shape))


def result_block(shape, chunk, chunks, tp_at, mine):
    def place(_, meta_ref):
        owner = meta_ref[tp_at] if mine else 1 - meta_ref[tp_at]
        return (0, 0, 0, owner * chunks + chunk)

    return pl.BlockSpec((1,) + shape, place)


def gradients(chunk, chunks, me_at, tp_at, tp_count, meta, backs, side, others):
    peers = len(backs)
    _, rows, channels = side.shape
    span = channels // chunks
    out = (3, rows // tp_count, span)
    whole = (1, 3, rows // tp_count, channels * tp_count)
    in_specs = [pl.BlockSpec((3, rows, span), lambda _, meta_ref: (0, 0, chunk))]
    in_specs += [fixed(backs[0].shape)] * peers
    args = [meta, side, *backs]
    aliases = {} if chunk == 0 else {len(args): 0}
    for other in others:
        args.append(other)
        in_specs.append(pl.BlockSpec(memory_space=pl.ANY))
    return pl.pallas_call(
        functools.partial(gradients_kernel, me_at, tp_at, peers),
        out_shape=[jax.ShapeDtypeStruct(whole, BF16), jax.ShapeDtypeStruct(out, BF16)],
        grid_spec=pltpu.PrefetchScalarGridSpec(
            num_scalar_prefetch=1,
            grid=(1,),
            in_specs=in_specs,
            out_specs=[result_block(out, chunk, chunks, tp_at, True), fixed(out)],
        ),
        input_output_aliases=aliases,
        compiler_params=params(24),
        cost_estimate=pl.CostEstimate(
            flops=3 * rows * span, bytes_accessed=16 * rows * span, transcendentals=0
        ),
        name="gradients",
    )(*args)


def place_kernel(meta_ref, cross_ref, held_ref, result_ref):
    result_ref[0] = cross_ref[...]


def place(chunk, chunks, tp_at, meta, cross, result):
    three, part, span = cross.shape

    def other(i, meta_ref):
        return (0, i, 0, (1 - meta_ref[tp_at]) * chunks + chunk)

    return pl.pallas_call(
        place_kernel,
        out_shape=jax.ShapeDtypeStruct(result.shape, BF16),
        grid_spec=pltpu.PrefetchScalarGridSpec(
            num_scalar_prefetch=1,
            grid=(three,),
            in_specs=[
                pl.BlockSpec((1, part, span), lambda i, _: (i, 0, 0)),
                pl.BlockSpec(memory_space=pl.ANY),
            ],
            out_specs=pl.BlockSpec((1, 1, part, span), other),
        ),
        input_output_aliases={2: 0},
        compiler_params=params(24),
        cost_estimate=pl.CostEstimate(
            flops=0, bytes_accessed=4 * math.prod(cross.shape), transcendentals=0
        ),
        name="place",
    )(meta, cross, result)


def gradients(chunk, chunks, me_at, tp_at, tp_count, meta, backs, side, others):
    peers = len(backs)
    _, rows, channels = side.shape
    span = channels // chunks
    out = (3, rows // tp_count, span)
    whole = (1, 3, rows // tp_count, channels * tp_count)
    in_specs = [pl.BlockSpec((3, rows, span), lambda _, meta_ref: (0, 0, chunk))]
    in_specs += [fixed(backs[0].shape)] * peers
    args = [meta, side, *backs]
    aliases = {} if chunk == 0 else {len(args): 0}
    for other in others:
        args.append(other)
        in_specs.append(pl.BlockSpec(memory_space=pl.ANY))
    return pl.pallas_call(
        functools.partial(gradients_kernel, me_at, tp_at, peers),
        out_shape=[jax.ShapeDtypeStruct(whole, BF16), jax.ShapeDtypeStruct(out, BF16)],
        grid_spec=pltpu.PrefetchScalarGridSpec(
            num_scalar_prefetch=1,
            grid=(1,),
            in_specs=in_specs,
            out_specs=[result_block(out, chunk, chunks, tp_at, True), fixed(out)],
        ),
        input_output_aliases=aliases,
        compiler_params=params(24),
        cost_estimate=pl.CostEstimate(
            flops=3 * rows * span, bytes_accessed=16 * rows * span, transcendentals=0
        ),
        name="gradients",
    )(*args)


def place_kernel(meta_ref, cross_ref, held_ref, result_ref):
    result_ref[0] = cross_ref[...]


def place(chunk, chunks, tp_at, meta, cross, result):
    return pl.pallas_call(
        place_kernel,
        out_shape=jax.ShapeDtypeStruct(result.shape, BF16),
        grid_spec=pltpu.PrefetchScalarGridSpec(
            num_scalar_prefetch=1,
            grid=(1,),
            in_specs=[fixed(cross.shape), pl.BlockSpec(memory_space=pl.ANY)],
            out_specs=result_block(cross.shape, chunk, chunks, tp_at, False),
        ),
        input_output_aliases={2: 0},
        compiler_params=params(24),
        cost_estimate=pl.CostEstimate(
            flops=0, bytes_accessed=4 * math.prod(cross.shape), transcendentals=0
        ),
        name="place",
    )(meta, cross, result)


def swap(array, k):
    peers = lax.axis_size("ctx")
    return lax.ppermute(array, "ctx", [(i, i ^ k) for i in range(peers)]) if k else array


def swap_to_previous(array, k):
    peers = lax.axis_size("ctx")
    pipes = lax.axis_size("pipe")
    pairs = [
        (pipe * peers + i, (pipe - 1) % pipes * peers + (i ^ k))
        for pipe in range(pipes)
        for i in range(peers)
    ]
    return lax.ppermute(array, ("pipe", "ctx"), pairs)


def shards(qkv_proj, cotangent, block_dest, doc_start, mr_filter):
    peers = lax.axis_size("ctx")
    pipes = lax.axis_size("pipe")
    tp_count = lax.axis_size("tp")
    channels = cotangent.shape[2]
    group_count, taps = mr_filter.shape[1:]
    group_size = channels // group_count
    units = channels // (peers * LANES)
    chunks = math.gcd(units, CHUNKS)
    width = channels // (peers * chunks)
    chunk_groups = width // group_size

    dest = lax.dynamic_index_in_dim(block_dest, lax.axis_index("pipe"), 0, keepdims=False)
    me_at = dest.shape[0]
    tp_at = me_at + 1
    here = [lax.axis_index("ctx"), lax.axis_index("tp")]
    meta = jnp.concatenate([dest, jnp.stack(here).astype(jnp.int32)])

    filt = lax.dynamic_index_in_dim(
        mr_filter[0].astype(F32).reshape(chunks, peers, chunk_groups, taps),
        lax.axis_index("ctx"),
        1,
        keepdims=False,
    )
    causal = jnp.pad(filt[:, :, ::-1], ((0, 0), (0, 0), (1, taps - 1)))
    anti = jnp.pad(filt, ((0, 0), (0, 0), (0, taps)))
    bases = jnp.stack([causal, anti], axis=1)

    to_previous = [(pipe, (pipe - 1) % pipes) for pipe in range(pipes)]
    order = sending_order(peers)
    products = multiply(chunks, width, peers, qkv_proj, cotangent, doc_start)
    toeplitz = [toeplitz_of(bases[chunk]) for chunk in range(chunks)]
    received = [swap(array, k) for array, k in zip(products[0], order)]
    side = lax.ppermute(side_of(qkv_proj, cotangent), "pipe", to_previous)

    first_out, first_back = OUT_FIRST * peers // 8, BACK_FIRST * peers // 8
    masks = document_masks(me_at, meta, received, MARK_ROWS)
    backs, late = [], []
    for chunk in range(chunks):
        coming = products[chunk + 1] if chunk + 1 < chunks else []
        convolved = convolve(group_size, me_at, meta, received, masks, toeplitz[chunk])
        convolved, waited, late = lax.optimization_barrier((convolved, coming[first_out:], late))
        received = [swap(array, k) for array, k in zip(coming[:first_out] + waited, order)]
        if chunk:
            backs[-1] += [
                swap_to_previous(array, k) for array, k in zip(late, order[first_back:])
            ]
        if coming:
            late = convolved[first_back:]
        else:
            last, side = lax.optimization_barrier((convolved[first_back:], side))
            convolved = convolved[:first_back] + last
        now = first_back if coming else peers
        backs.append([swap_to_previous(array, k) for array, k in zip(convolved[:now], order)])

    result, held = None, []
    for chunk in range(chunks):
        others = [result] if chunk else [array for back in backs[1:] for array in back]
        result, cross = gradients(
            chunk, chunks, me_at, tp_at, tp_count, meta, backs[chunk], side, others
        )
        held.append(lax.ppermute(cross, "tp", [(0, 1), (1, 0)]))
    for chunk in range(chunks):
        result = place(chunk, chunks, tp_at, meta, held[chunk], result)
    return result


def solution(mesh):
    placed = (
        P("pipe", None, "ctx", "tp"),
        P("pipe", "ctx", "tp"),
        P(),
        P("pipe", "ctx"),
        P("pipe", "tp", None),
    )
    return jax.shard_map(
        shards,
        mesh=mesh,
        in_specs=placed,
        out_specs=P("pipe", None, ("ctx", "tp"), None),
        check_vma=False,
    )
```
